128 devices in a mesh: dp: 8 (over z_lo, y), row: 8 (over x, z_hi), col: 2 (over core).
Axes of the slice: x: 4, y: 4, z: 4 (z_hi: 2, z_lo: 2; z = z_hi * 2 + z_lo), core: 2. Of those that a mesh axis runs over, the one named last changes fastest.
Arguments:
- block_in: bfloat16 [16, 1024, 1088], P('dp', 'row', 'col'), may hold values from -6 to 6
- query_key_value_weight: bfloat16 [3, 1088, 1088], P(None, 'row', 'col'), may hold values from -0.1875 to 0.1875
- bias_qv: float32 [2, 1088], P(None, 'row'), may hold values from -3 to 3
- output_weight: bfloat16 [1088, 1088], P('row', 'col'), may hold values from -1.5 to 1.5
- bias_out: float32 [1088], P('col'), may hold values from -3 to 3
- gain_one: float32 [1088], P('col'), may hold values from 0.5 to 1.5
- shift_one: float32 [1088], P('col'), may hold values from -2 to 2
- gain_two: float32 [1088], P('col'), may hold values from 0.5 to 1.5
- shift_two: float32 [1088], P('col'), may hold values from -2 to 2
- up_weight: bfloat16 [4352, 1088], P('row', 'col'), may hold values from -0.1875 to 0.1875
- bias_up: float32 [4352], P('row'), may hold values from -3 to 3
- down_weight: bfloat16 [4352, 1088], P('row', 'col'), may hold values from -0.09375 to 0.09375
- bias_down: float32 [1088], P('col'), may hold values from -3 to 3
- out_grad: bfloat16 [16, 1024, 1088], P('dp', 'row', 'col'), may hold values from -6 to 6
Outputs:
- block_out: bfloat16 [16, 1024, 1088], P('dp', 'row', 'col')
- in_grad: float32 [16, 1024, 1088], P('dp', 'row', 'col')
- grad_qkv: float32 [3, 1088, 1088], P(None, 'row', 'col')
- grad_bias_qv: float32 [2, 1088], P(None, 'row')
- grad_out: float32 [1088, 1088], P('row', 'col')
- grad_bias_out: float32 [1088], P('col')
- grad_gain_one: float32 [1088], P('col')
- grad_shift_one: float32 [1088], P('col')
- grad_gain_two: float32 [1088], P('col')
- grad_shift_two: float32 [1088], P('col')
- up_weight_gradient: float32 [4352, 1088], P('row', 'col')
- grad_bias_up: float32 [4352], P('row')
- down_weight_gradient: float32 [4352, 1088], P('row', 'col')
- grad_bias_down: float32 [1088], P('col')
The draws below stay inside these ranges and needn't reach their ends.
All inputs are finite; a program needn't handle non-finite values.
Results may differ from the reference program's by a relative error of at most 0.012.
Values may be sent and summed in bfloat16 or wider, within the bound.
A program may use at most 192 MiB of HBM per device.

```python
import jax
import jax.numpy as jnp
from jax import lax

D = 1088
HDIM = 64
FF = 4352
LEN = 1024
SEQS = 16


def block_levels(rng, shape, split, low, high):
    def one(dim, shards_of):
        steps = jax.random.uniform(jax.random.fold_in(jax.random.fold_in(rng, 6), dim), (shards_of,), jnp.float32, low / len(split), high / len(split))
        return jnp.repeat(jnp.exp(steps), shape[dim] // shards_of).reshape((-1,) + (1,) * (len(shape) - dim - 1))

    factor_of = one(*split[0])
    for cut in split[1:]:
        factor_of = factor_of * one(*cut)
    return factor_of


def scatter_about(key, shape, spread, limit, shards=(), dtype=jnp.bfloat16):
    values = spread * jax.random.normal(key, shape, jnp.float32)
    if shards:
        values = values * block_levels(key, shape, shards, -0.22, 0.18)
    return jnp.clip(values, -limit, limit).astype(dtype)


def setup_inputs(seed: int = 0) -> dict:
    seeds = jax.random.split(jax.random.key(seed), 15)
    block_in = scatter_about(seeds[0], (SEQS, LEN, D), 1.0, 6.0, ((0, 8), (1, 8), (2, 2)))
    query_key_value_weight = scatter_about(seeds[1], (3, D, D), D ** -0.5, 0.1875, ((1, 8), (2, 2)))
    bias_qv = scatter_about(seeds[2], (2, D), 0.5, 3.0, ((1, 8),), jnp.float32)
    output_weight = scatter_about(seeds[3], (D, D), (max(D // 64, 4)) ** -0.5, 1.5, ((0, 8), (1, 2)))
    bias_out = scatter_about(seeds[4], (D,), 0.5, 3.0, ((0, 2),), jnp.float32)
    gain_one = jnp.clip(1.0 + 0.1 * jax.random.normal(seeds[5], (D,), jnp.float32), 0.5, 1.5)
    shift_one = scatter_about(seeds[6], (D,), 0.3, 2.0, ((0, 2),), jnp.float32)
    gain_two = jnp.clip(1.0 + 0.1 * jax.random.normal(seeds[7], (D,), jnp.float32), 0.5, 1.5)
    shift_two = scatter_about(seeds[8], (D,), 0.3, 2.0, ((0, 2),), jnp.float32)
    up_weight = scatter_about(seeds[9], (FF, D), D ** -0.5, 0.1875, ((0, 8), (1, 2)))
    bias_up = scatter_about(seeds[10], (FF,), 0.5, 3.0, ((0, 8),), jnp.float32)
    down_weight = scatter_about(seeds[11], (FF, D), FF ** -0.5, 0.09375, ((0, 8), (1, 2)))
    bias_down = scatter_about(seeds[12], (D,), 0.5, 3.0, ((0, 2),), jnp.float32)
    out_grad = scatter_about(seeds[13], (SEQS, LEN, D), 1.0, 6.0, ((0, 8), (1, 8), (2, 2)))
    return dict(block_in=block_in, query_key_value_weight=query_key_value_weight, bias_qv=bias_qv, output_weight=output_weight, bias_out=bias_out, gain_one=gain_one, shift_one=shift_one, gain_two=gain_two, shift_two=shift_two, up_weight=up_weight, bias_up=bias_up, down_weight=down_weight, bias_down=bias_down, out_grad=out_grad)


@jax.custom_vjp
def low(v):
    return lax.optimization_barrier(v.astype(jnp.bfloat16)).astype(jnp.float32)

@jax.custom_vjp
def low_back(v):
    return v

def low_keep(v):
    return (low(v), None)

def low_pass(kept, grad):
    return (grad,)

def back_keep(v):
    return (v, None)

def back_low(kept, grad):
    return (low(grad),)
low.defvjp(low_keep, low_pass)
low_back.defvjp(back_keep, back_low)
EPSILON = 1e-05
HIGHEST = lax.Precision.HIGHEST
MASKED = -1e+30

def layer_norm(values, gain, shift):
    centre = lax.optimization_barrier(jnp.mean(values, axis=-1, keepdims=True))
    second = lax.optimization_barrier(jnp.mean(values * values, axis=-1, keepdims=True))
    inverse = lax.rsqrt(second - centre * centre + EPSILON)
    return (values - centre) * inverse * gain + shift

def forward(inputs, query_key_value_weight, bias_qv, output_weight, bias_out, gain_one, shift_one, gain_two, shift_two, up_weight, bias_up, down_weight, bias_down):
    length = inputs.shape[0]
    count_heads = D // HDIM
    normed_one = low(layer_norm(inputs, gain_one, shift_one))
    projected = jnp.einsum('td,kod->tko', normed_one, query_key_value_weight, precision=HIGHEST)
    bias_full = jnp.stack([bias_qv[0], jnp.zeros_like(bias_qv[0]), bias_qv[1]])
    projected = low(low_back(projected + bias_full))
    query = projected[:, 0].reshape(length, count_heads, HDIM) * HDIM ** (-0.5)
    keys_all = projected[:, 1].reshape(length, count_heads, HDIM)
    values_all = projected[:, 2].reshape(length, count_heads, HDIM)
    scores = jnp.einsum('qhd,khd->hqk', query, keys_all, precision=HIGHEST)
    causal = jnp.arange(length)[:, None] >= jnp.arange(length)[None, :]
    scores = low_back(jnp.where(causal[None], scores, MASKED))
    highest = lax.optimization_barrier(jnp.max(scores, axis=-1, keepdims=True))
    exponent = jnp.exp(scores - highest)
    weights = low(exponent / lax.optimization_barrier(jnp.sum(exponent, axis=-1, keepdims=True)))
    mixed = jnp.einsum('hqk,khd->qhd', weights, values_all, precision=HIGHEST).reshape(length, D)
    mixed = low(low_back(mixed))
    attended = jnp.dot(mixed, output_weight, precision=HIGHEST) + bias_out
    residual = inputs + low_back(attended)
    normed_two = low(layer_norm(residual, gain_two, shift_two))
    hidden = low_back(jnp.einsum('td,fd->tf', normed_two, up_weight, precision=HIGHEST) + bias_up)
    active = low(jax.nn.gelu(hidden, approximate=False))
    return residual + low_back(jnp.dot(active, down_weight, precision=HIGHEST) + bias_down)

def reference(block_in, query_key_value_weight, bias_qv, output_weight, bias_out, gain_one, shift_one, gain_two, shift_two, up_weight, bias_up, down_weight, bias_down, out_grad):
    params = tuple((operand.astype(jnp.float32) for operand in (query_key_value_weight, bias_qv, output_weight, bias_out, gain_one, shift_one, gain_two, shift_two, up_weight, bias_up, down_weight, bias_down)))
    inputs = block_in.astype(jnp.float32)
    cotangent = out_grad.astype(jnp.float32)

    def one_sequence(running, sequence_pair):
        sequence, tangent = sequence_pair
        result, pullback = jax.vjp(forward, sequence, *params)
        gradients = pullback(tangent)
        running = tuple((earlier + gradient for earlier, gradient in zip(running, gradients[1:])))
        return (running, (result.astype(jnp.bfloat16), gradients[0]))
    initial = tuple((jnp.zeros(operand.shape, jnp.float32) for operand in params))
    totals, (outputs, input_grads) = lax.scan(one_sequence, initial, (inputs, cotangent))
    return (outputs, input_grads, totals[0], totals[1], totals[2], totals[3], totals[4], totals[5], totals[6], totals[7], totals[8], totals[9], totals[10], totals[11])
```

```python
import functools

import jax
import jax.numpy as jnp
from jax import lax
from jax.experimental import pallas as pl
from jax.experimental.pallas import tpu as pltpu
from jax.sharding import Mesh
from jax.sharding import PartitionSpec as P


HDIM = 64
D = 1088
HALF = D // 2
TOK = 128
LEN = 1024
SLOT = 192
EPSILON = 1e-05
MASKED = -1e30
DP = ("zl", "y")
ROW = ("x", "zh")
ALL = ("zl", "y", "x", "zh", "c")
MESH = pl.DeviceIdType.MESH
BF = jnp.bfloat16
F32 = jnp.float32


def greet(targets):
    barrier = pltpu.get_barrier_semaphore()
    for target in targets:
        pl.semaphore_signal(barrier, inc=1, device_id=target, device_id_type=MESH)
    pl.semaphore_wait(barrier, len(targets))


def remote(src, dst, send, recv, target):
    return pltpu.make_async_remote_copy(
        src_ref=src, dst_ref=dst, send_sem=send, recv_sem=recv, device_id=target, device_id_type=MESH
    )


def gather_kernel(a_ref, o_ref, own_sem, x_send, x_recv, c_send, c_recv):
    x, c = lax.axis_index("x"), lax.axis_index("c")
    sibling = {"c": 1 - c}
    greet([{"x": lax.rem(x + k, 4)} for k in (1, 2, 3)] + [sibling])
    own = 2 * x + c
    kept = pltpu.make_async_copy(a_ref, o_ref.at[own], own_sem)
    kept.start()
    far = {}
    for k in (1, 3, 2):
        far[k] = remote(a_ref, o_ref.at[own], x_send.at[k], x_recv.at[k], {"x": lax.rem(x + k, 4)})
        far[k].start()
    near = [remote(a_ref, o_ref.at[own], c_send.at[0], c_recv.at[0], sibling)]
    near[0].start()
    for k in (1, 3, 2):
        far[k].wait_recv()
        slot = 2 * lax.rem(x + 4 - k, 4) + c
        copy = remote(o_ref.at[slot], o_ref.at[slot], c_send.at[k], c_recv.at[k], sibling)
        copy.start()
        near.append(copy)
    kept.wait()
    for copy in near:
        copy.wait()
    for k in (1, 3, 2):
        far[k].wait_send()


def line_gather(a, cid):
    return pl.pallas_call(
        gather_kernel,
        out_shape=jax.ShapeDtypeStruct((8, *a.shape), a.dtype),
        in_specs=[pl.BlockSpec(memory_space=pltpu.VMEM)],
        out_specs=pl.BlockSpec(memory_space=pltpu.VMEM),
        scratch_shapes=[pltpu.SemaphoreType.DMA] + [pltpu.SemaphoreType.DMA((4,))] * 4,
        compiler_params=pltpu.CompilerParams(
            collective_id=cid, has_side_effects=True, vmem_limit_bytes=32 << 20
        ),
        name="line_gather",
    )(a)


def scatter_kernel(p_ref, o_ref, near, out, arrived, c_send, c_recv, x_send, x_recv):
    x, c = lax.axis_index("x"), lax.axis_index("c")
    sibling = {"c": 1 - c}
    greet([{"x": lax.rem(x + k, 4)} for k in (1, 2, 3)] + [sibling])
    order = (2, 1, 3, 0)
    swaps, sends = {}, {}
    for k in order:
        to = lax.rem(x + k, 4)
        swaps[k] = remote(p_ref.at[2 * to + 1 - c], near.at[k], c_send.at[k], c_recv.at[k], sibling)
        swaps[k].start()
    for k in order:
        to = lax.rem(x + k, 4)
        swaps[k].wait_recv()
        both = p_ref[2 * to + c].astype(F32) + near[k].astype(F32)
        if k == 0:
            o_ref[...] = both
        else:
            out[k] = both.astype(BF)
            sends[k] = remote(out.at[k], arrived.at[k], x_send.at[k], x_recv.at[k], {"x": to})
            sends[k].start()
    for k in (1, 3, 2):
        sends[k].wait_recv()
        o_ref[...] += arrived[k].astype(F32)
    for k in (1, 3, 2):
        sends[k].wait_send()
    for k in order:
        swaps[k].wait_send()


def line_scatter(p, cid):
    return pl.pallas_call(
        scatter_kernel,
        out_shape=jax.ShapeDtypeStruct(p.shape[1:], F32),
        in_specs=[pl.BlockSpec(memory_space=pltpu.VMEM)],
        out_specs=pl.BlockSpec(memory_space=pltpu.VMEM),
        scratch_shapes=[pltpu.VMEM((4, *p.shape[1:]), BF)] * 3 + [pltpu.SemaphoreType.DMA((4,))] * 4,
        compiler_params=pltpu.CompilerParams(
            collective_id=cid, has_side_effects=True, vmem_limit_bytes=32 << 20
        ),
        name="line_scatter",
    )(p)


def others(x, c):
    return [(k, j, lax.rem(x + k, 4), lax.rem(c + j, 2)) for k, j in ((2, 0), (2, 1), (1, 0), (1, 1), (3, 0), (3, 1), (0, 1))]


def to_tokens_kernel(m_ref, o_ref, own_sem, send, recv):
    x, c = lax.axis_index("x"), lax.axis_index("c")
    peers = others(x, c)
    greet([{"x": xx, "c": cc} for _, _, xx, cc in peers])
    own = 2 * x + c
    columns = pl.ds(pl.multiple_of(own * TOK, TOK), TOK)
    kept = pltpu.make_async_copy(m_ref.at[:, columns], o_ref.at[own], own_sem)
    kept.start()
    copies = []
    for k, j, xx, cc in peers:
        columns = pl.ds(pl.multiple_of((2 * xx + cc) * TOK, TOK), TOK)
        n = 2 * k + j
        copy = remote(m_ref.at[:, columns], o_ref.at[own], send.at[n], recv.at[n], {"x": xx, "c": cc})
        copy.start()
        copies.append(copy)
    kept.wait()
    for copy in copies:
        copy.wait()


def to_tokens(m, cid):
    return pl.pallas_call(
        to_tokens_kernel,
        out_shape=jax.ShapeDtypeStruct((8, SLOT, TOK), BF),
        in_specs=[pl.BlockSpec(memory_space=pltpu.VMEM)],
        out_specs=pl.BlockSpec(memory_space=pltpu.VMEM),
        scratch_shapes=[pltpu.SemaphoreType.DMA] + [pltpu.SemaphoreType.DMA((8,))] * 2,
        compiler_params=pltpu.CompilerParams(
            collective_id=cid, has_side_effects=True, vmem_limit_bytes=32 << 20
        ),
        name="to_tokens",
    )(m)


def to_heads_kernel(m_ref, o_ref, own_sem, send, recv):
    x, c = lax.axis_index("x"), lax.axis_index("c")
    peers = others(x, c)
    greet([{"x": xx, "c": cc} for _, _, xx, cc in peers])
    own = 2 * x + c
    columns = pl.ds(pl.multiple_of(own * TOK, TOK), TOK)

    def rows(rank):
        return pl.ds(pl.multiple_of(rank * 2 * HDIM, 2 * HDIM), SLOT)

    kept = pltpu.make_async_copy(m_ref.at[rows(own)], o_ref.at[:, columns], own_sem)
    kept.start()
    copies = []
    for k, j, xx, cc in peers:
        n = 2 * k + j
        copy = remote(
            m_ref.at[rows(2 * xx + cc)], o_ref.at[:, columns], send.at[n], recv.at[n], {"x": xx, "c": cc}
        )
        copy.start()
        copies.append(copy)
    kept.wait()
    for copy in copies:
        copy.wait()


def to_heads(m, cid):
    return pl.pallas_call(
        to_heads_kernel,
        out_shape=jax.ShapeDtypeStruct((SLOT, LEN), BF),
        in_specs=[pl.BlockSpec(memory_space=pltpu.VMEM)],
        out_specs=pl.BlockSpec(memory_space=pltpu.VMEM),
        scratch_shapes=[pltpu.SemaphoreType.DMA] + [pltpu.SemaphoreType.DMA((8,))] * 2,
        compiler_params=pltpu.CompilerParams(
            collective_id=cid, has_side_effects=True, vmem_limit_bytes=32 << 20
        ),
        name="to_heads",
    )(m)


BLOCK = 256


def dot(a, b, dims):
    return lax.dot_general(a, b, (dims, ((), ())), preferred_element_type=F32)


def attend_kernel(q_ref, k_ref, v_ref, o_ref, p_ref):
    keys = lax.broadcasted_iota(jnp.int32, (BLOCK, BLOCK), 0)
    queries = lax.broadcasted_iota(jnp.int32, (BLOCK, BLOCK), 1)
    for i in range(LEN // BLOCK):
        low, high = i * BLOCK, (i + 1) * BLOCK
        q = q_ref[:, low:high] * BF(HDIM**-0.5)
        parts = [dot(k_ref[:, low:high], q, ((0,), (0,)))]
        parts[0] = jnp.where(keys <= queries, parts[0], MASKED)
        if i:
            parts.insert(0, dot(k_ref[:, :low], q, ((0,), (0,))))
        highest = functools.reduce(jnp.maximum, [jnp.max(s, axis=0, keepdims=True) for s in parts])
        parts = [jnp.exp(s - highest) for s in parts]
        share = 1.0 / sum(jnp.sum(s, axis=0, keepdims=True) for s in parts)
        parts = [(s * share).astype(BF) for s in parts]
        p_ref[0, low:high, low:high] = parts[-1]
        mixed = dot(v_ref[:, low:high], parts[-1], ((1,), (0,)))
        if i:
            p_ref[0, :low, low:high] = parts[0]
            mixed += dot(v_ref[:, :low], parts[0], ((1,), (0,)))
        o_ref[:, low:high] = mixed.astype(BF)


def attend(qkv):
    head = lambda k: pl.BlockSpec((pl.squeezed, HDIM, LEN), lambda h: (k, h, 0))
    return pl.pallas_call(
        attend_kernel,
        grid=(SLOT // HDIM,),
        out_shape=(
            jax.ShapeDtypeStruct((SLOT, LEN), BF),
            jax.ShapeDtypeStruct((SLOT // HDIM, LEN, LEN), BF),
        ),
        in_specs=[head(0), head(1), head(2)],
        out_specs=(
            pl.BlockSpec((HDIM, LEN), lambda h: (h, 0)),
            pl.BlockSpec((1, LEN, LEN), lambda h: (h, 0, 0)),
        ),
        compiler_params=pltpu.CompilerParams(vmem_limit_bytes=40 << 20),
        cost_estimate=pl.CostEstimate(flops=2 * 3 * 2 * 64 * 10 * 65536, bytes_accessed=8 << 20, transcendentals=3 * 655360),
        name="attend",
    )(qkv, qkv, qkv)


def attend_back_kernel(q_ref, k_ref, v_ref, u_ref, p_ref, dq_ref, dk_ref, dv_ref, dk_sum, dv_sum):
    dk_sum[...] = jnp.zeros_like(dk_sum)
    dv_sum[...] = jnp.zeros_like(dv_sum)
    for i in range(LEN // BLOCK):
        low, high = i * BLOCK, (i + 1) * BLOCK
        q = q_ref[:, low:high] * BF(HDIM**-0.5)
        u = u_ref[:, low:high]
        p = p_ref[0, :high, low:high]
        wide = p.astype(F32)
        dp = dot(v_ref[:, :high], u, ((0,), (0,)))
        centre = jnp.sum(wide * dp, axis=0, keepdims=True)
        ds = (wide * (dp - centre)).astype(BF)
        dq_ref[:, low:high] = (dot(k_ref[:, :high], ds, ((1,), (0,))) * HDIM**-0.5).astype(BF)
        dk_sum[:, :high] += dot(q, ds, ((1,), (1,)))
        dv_sum[:, :high] += dot(u, p, ((1,), (1,)))
    dk_ref[...] = dk_sum[...].astype(BF)
    dv_ref[...] = dv_sum[...].astype(BF)


def attend_back(qkv, upstream, probs):
    head = lambda k: pl.BlockSpec((pl.squeezed, HDIM, LEN), lambda h: (k, h, 0))
    flat = pl.BlockSpec((HDIM, LEN), lambda h: (h, 0))
    return pl.pallas_call(
        attend_back_kernel,
        grid=(SLOT // HDIM,),
        out_shape=(jax.ShapeDtypeStruct((SLOT, LEN), BF),) * 3,
        in_specs=[head(0), head(1), head(2), flat, pl.BlockSpec((1, LEN, LEN), lambda h: (h, 0, 0))],
        out_specs=(flat,) * 3,
        scratch_shapes=[pltpu.VMEM((HDIM, LEN), F32)] * 2,
        compiler_params=pltpu.CompilerParams(vmem_limit_bytes=40 << 20),
        cost_estimate=pl.CostEstimate(flops=4 * 3 * 2 * 64 * 10 * 65536, bytes_accessed=8 << 20, transcendentals=0),
        name="attend_back",
    )(qkv, qkv, qkv, upstream, probs)


def swap(a, axis):
    return lax.ppermute(a, axis, [(0, 1), (1, 0)])


def shifted(a, axis, k):
    return lax.ppermute(a, axis, [(i, (i + k) % 4) for i in range(4)])


def pick(flag, a, b):
    return jnp.where(flag, a, b), jnp.where(flag, b, a)


def at(a, i):
    return lax.dynamic_index_in_dim(a, i, 0, keepdims=False)


def halves(c, mine, theirs):
    first, second = pick(c == 0, mine, theirs)
    return jnp.concatenate([first, second], axis=-1)


def tokens_in(a, zh, c):
    mine, other = at(a, zh), at(a, 1 - zh)
    got = swap(other, "zh")
    keep, send = pick(zh == c, mine, got)
    return halves(c, keep, swap(send, "c"))


def tokens_out(a, zh, c):
    keep, send = pick(c == 0, a[:, :HALF], a[:, HALF:])
    part, other = pick(c == zh, keep, swap(send, "c"))
    got = swap(other, "zh")
    first, second = pick(zh == 0, part, got)
    return jnp.stack([first, second])


def weight_in(w, zh, c):
    keep, send = pick(zh == c, w, swap(w, "zh"))
    return halves(c, keep, swap(send, "c"))


def over_replicas(pieces):
    y = lax.axis_index("y")
    pieces = pieces.astype(BF)
    total = at(pieces, y).astype(F32)
    for k in (2, 1, 3):
        total += shifted(at(pieces, lax.rem(y + k, 4)), "y", k).astype(F32)
    total = total.astype(BF)
    total = (total.astype(F32) + swap(total, "zl").astype(F32)).astype(BF)
    found = jnp.stack([total] + [shifted(total, "y", 4 - k) for k in (1, 2, 3)])
    return jnp.concatenate([at(found, lax.rem(k - y + 4, 4))[None] for k in range(4)])


def block_grad(grad, zh, c):
    rows = grad.shape[0]
    keep, send = pick(c == 0, grad[:, :HALF], grad[:, HALF:])
    block, other = pick(c == zh, keep, swap(send, "c"))
    total = block.astype(F32) + swap(other, "zh").astype(F32)
    return over_replicas(total.reshape(4, rows // 4, HALF)).reshape(rows, HALF).astype(F32)


def normed(values, gain, shift):
    centre = jnp.mean(values, axis=1, keepdims=True)
    second = jnp.mean(values * values, axis=1, keepdims=True)
    inverse = lax.rsqrt(second - centre * centre + EPSILON)
    centred = (values - centre) * inverse
    return (centred * gain + shift).astype(BF), centred, inverse


def normed_back(upstream, centred, inverse, gain):
    scaled = upstream * gain
    result = inverse * (
        scaled
        - jnp.mean(scaled, axis=1, keepdims=True)
        - centred * jnp.mean(scaled * centred, axis=1, keepdims=True)
    )
    return result, jnp.sum(upstream * centred, axis=0), jnp.sum(upstream, axis=0)


def per_device(
    block_in,
    query_key_value_weight,
    bias_qv,
    output_weight,
    bias_out,
    gain_one,
    shift_one,
    gain_two,
    shift_two,
    up_weight,
    bias_up,
    down_weight,
    bias_down,
    out_grad,
):
    x, y, zh, c = (lax.axis_index(a) for a in ("x", "y", "zh", "c"))
    rank = 2 * x + c
    last = rank == 7

    inputs = tokens_in(block_in, zh, c).astype(F32)
    columns = jnp.stack([bias_out, gain_one, shift_one, gain_two, shift_two, bias_down])
    bias_out, gain_one, shift_one, gain_two, shift_two, bias_down = halves(c, columns, swap(columns, "c"))

    w = query_key_value_weight
    even, odd = pick(zh == 0, w, swap(w, "zh"))
    w = jnp.concatenate([even, odd], axis=1)
    w = jnp.concatenate([shifted(w[:, 224:], "x", 1), w, jnp.zeros((3, 48, HALF), BF)], axis=1)
    mine = lax.dynamic_slice_in_dim(w, 48 - 16 * x + 128 * c, SLOT, 1)
    theirs = lax.dynamic_slice_in_dim(w, 48 - 16 * x + 128 * (1 - c), SLOT, 1)
    weight_qkv = halves(c, mine, swap(theirs, "c"))
    real = jnp.logical_or(jnp.arange(SLOT) < 128, last)
    weight_qkv = jnp.where(real[None, :, None], weight_qkv, BF(0))

    rows = jnp.concatenate([bias_qv.reshape(-1), bias_up])
    even, odd = pick(zh == 0, rows, swap(rows, "zh"))
    bias_up = jnp.where(c == 0, even[272:], odd[272:])
    qv = jnp.concatenate([even[:272].reshape(2, 136), odd[:272].reshape(2, 136)], axis=1)
    qv = jnp.concatenate([shifted(qv[:, 224:], "x", 1), qv, jnp.zeros((2, 48), F32)], axis=1)
    qv = lax.dynamic_slice_in_dim(qv, 48 - 16 * x + 128 * c, SLOT, 1)
    qv = jnp.where(real[None], qv, 0.0)
    bias_qkv = jnp.stack([qv[0], jnp.zeros_like(qv[0]), qv[1]])

    normed_one, centred_one, inverse_one = normed(inputs, gain_one, shift_one)
    first_rows = line_gather(normed_one, 1).reshape(LEN, D)
    qkv = jnp.einsum("koi,ti->kot", weight_qkv, first_rows, preferred_element_type=F32)
    qkv = (qkv + bias_qkv[..., None]).astype(BF)
    mixed, probs = attend(qkv)
    found = to_tokens(mixed, 2)
    mixed_here = jnp.concatenate([found[:7, :128].reshape(896, TOK), found[7]])

    even, odd = pick(zh == 0, output_weight, swap(output_weight, "zh"))
    wo = jnp.concatenate([even, odd]).reshape(4, 68, HALF)
    part = at(wo, y)
    parts = jnp.stack([part] + [shifted(part, "x", 4 - k) for k in (1, 2, 3)])
    parts = jnp.concatenate([at(parts, lax.rem(k - x + 4, 4))[None] for k in range(4)])
    parts = jnp.stack([parts] + [shifted(parts, "y", 4 - k) for k in (1, 2, 3)])
    parts = jnp.concatenate([at(parts, lax.rem(k - y + 4, 4))[None] for k in range(4)])
    wo = jnp.transpose(parts, (1, 0, 2, 3)).reshape(D, HALF)
    wo = halves(c, wo, swap(wo, "c"))

    attended = jnp.einsum("ft,fo->to", mixed_here, wo, preferred_element_type=F32) + bias_out
    residual = inputs + attended

    weight_up = weight_in(up_weight, zh, c)
    weight_down = weight_in(down_weight, zh, c)
    normed_two, centred_two, inverse_two = normed(residual, gain_two, shift_two)
    second_rows = line_gather(normed_two, 3).reshape(LEN, D)
    hidden = jnp.einsum("td,fd->tf", second_rows, weight_up, preferred_element_type=F32) + bias_up
    cumulative = 0.5 * (1.0 + lax.erf(hidden * 0.7071067811865476))
    density = jnp.exp(-0.5 * hidden * hidden) * 0.3989422804014327
    active = (hidden * cumulative).astype(BF)
    slope = cumulative + hidden * density
    lowered = jnp.einsum("tf,fo->to", active, weight_down, preferred_element_type=F32).astype(BF)
    lowered = line_scatter(lowered.reshape(8, TOK, D), 4)
    block_out = tokens_out((residual + (lowered + bias_down)).astype(BF), zh, c)

    tangent = tokens_in(out_grad, zh, c)
    tangent_rows = line_gather(tangent, 5).reshape(LEN, D)
    down_grad = jnp.einsum("tf,to->fo", active, tangent_rows, preferred_element_type=F32).astype(BF)
    down_weight_gradient = block_grad(down_grad, zh, c)
    d_active = jnp.einsum("to,fo->tf", tangent_rows, weight_down, preferred_element_type=F32)
    d_hidden = (d_active * slope).astype(BF)
    grad_bias_up = jnp.sum(d_hidden, axis=0, dtype=F32)
    up_grad = jnp.einsum("tf,to->fo", d_hidden, second_rows, preferred_element_type=F32).astype(BF)
    up_weight_gradient = block_grad(up_grad, zh, c)
    d_normed_two = jnp.einsum("tf,fd->td", d_hidden, weight_up, preferred_element_type=F32).astype(BF)
    d_normed_two = line_scatter(d_normed_two.reshape(8, TOK, D), 6)
    tangent = tangent.astype(F32)
    grad_bias_down = jnp.sum(tangent, axis=0)
    part, grad_gain_two, grad_shift_two = normed_back(d_normed_two, centred_two, inverse_two, gain_two)
    d_residual = tangent + part
    d_attended = d_residual.astype(BF)
    grad_bias_out = jnp.sum(d_attended, axis=0, dtype=F32)

    d_mixed = jnp.einsum("fo,to->ft", wo, d_attended, preferred_element_type=F32).astype(BF)
    upstream = to_heads(d_mixed, 7)
    grad_out = jnp.einsum("ft,to->fo", mixed_here, d_attended, preferred_element_type=F32).astype(BF)
    keep, send = pick(c == 0, grad_out[:, :HALF], grad_out[:, HALF:])
    grad_out = (keep.astype(F32) + swap(send, "c").astype(F32)).astype(BF).reshape(4, 272, HALF)
    total = at(grad_out, x).astype(F32)
    for k in (2, 1, 3):
        total += shifted(at(grad_out, lax.rem(x + k, 4)), "x", k).astype(F32)
    keep, send = pick(zh == 0, total[:136], total[136:])
    grad_out = keep + swap(send.astype(BF), "zh").astype(F32)
    grad_out = over_replicas(grad_out.reshape(4, 34, HALF)).reshape(136, HALF).astype(F32)

    d_query, d_key, d_value = attend_back(qkv, upstream, probs)
    d_qkv = jnp.stack([d_query, d_key, d_value])
    d_normed_one = jnp.einsum("kot,koi->ti", d_qkv, weight_qkv, preferred_element_type=F32).astype(BF)
    d_normed_one = line_scatter(d_normed_one.reshape(8, TOK, D), 8)
    grad_qkv = jnp.einsum("kot,ti->koi", d_qkv, first_rows, preferred_element_type=F32).astype(BF)
    keep, send = pick(c == 0, grad_qkv[..., :HALF], grad_qkv[..., HALF:])
    first, second = pick(c == 0, keep, swap(send, "c"))
    tail = jnp.pad(shifted(first[:, :48], "x", 3), ((0, 0), (0, 16), (0, 0)))
    chip = jnp.concatenate([first[:, :128], second[:, :128], jnp.where(x == 3, second[:, 128:], tail)], axis=1)
    chip = lax.dynamic_slice_in_dim(chip, 16 * x, 272, 1)
    keep, send = pick(zh == 0, chip[:, :136], chip[:, 136:])
    total = keep.astype(F32) + swap(send, "zh").astype(F32)
    grad_qkv = over_replicas(total.reshape(4, 102, HALF)).reshape(3, 136, HALF).astype(F32)

    part, grad_gain_one, grad_shift_one = normed_back(d_normed_one, centred_one, inverse_one, gain_one)
    in_grad = tokens_out((d_residual + part).astype(BF), zh, c).astype(F32)

    bias_sums = jnp.sum(d_qkv, axis=2, dtype=F32)
    bias_sums = jnp.where(real[None], jnp.stack([bias_sums[0], bias_sums[2]]), 0.0)
    wide = lax.dynamic_update_slice(jnp.zeros((2, D), F32), bias_sums, (0, 128 * rank))
    hidden_sums = lax.dynamic_update_slice(jnp.zeros((8, 544), F32), grad_bias_up[None], (rank, 0))
    vector = jnp.concatenate(
        [grad_bias_out, grad_gain_one, grad_shift_one, grad_gain_two, grad_shift_two, grad_bias_down]
        + [wide.reshape(-1), hidden_sums.reshape(-1)]
    )
    vector = lax.psum(vector, ALL)
    six = vector[: 6 * D].reshape(6, 2, HALF)
    grad_bias_out, grad_gain_one, grad_shift_one, grad_gain_two, grad_shift_two, grad_bias_down = (
        lax.dynamic_index_in_dim(six, c, 1, keepdims=False)
    )
    row = 2 * x + zh
    grad_bias_qv = lax.dynamic_slice(vector[6 * D : 8 * D].reshape(2, D), (0, 136 * row), (2, 136))
    grad_bias_up = lax.dynamic_slice_in_dim(vector[8 * D :], 544 * row, 544, 0)

    return (
        block_out,
        in_grad,
        grad_qkv,
        grad_bias_qv,
        grad_out,
        grad_bias_out,
        grad_gain_one,
        grad_shift_one,
        grad_gain_two,
        grad_shift_two,
        up_weight_gradient,
        grad_bias_up,
        down_weight_gradient,
        grad_bias_down,
    )


def solution(mesh):
    finer = Mesh(mesh.devices.reshape(2, 4, 4, 2, 2), ALL)
    return jax.shard_map(
        per_device,
        mesh=finer,
        in_specs=(
            P(DP, ROW, "c"),
            P(None, ROW, "c"),
            P(None, ROW),
            P(ROW, "c"),
            P("c"),
            P("c"),
            P("c"),
            P("c"),
            P("c"),
            P(ROW, "c"),
            P(ROW),
            P(ROW, "c"),
            P("c"),
            P(DP, ROW, "c"),
        ),
        out_specs=(
            P(DP, ROW, "c"),
            P(DP, ROW, "c"),
            P(None, ROW, "c"),
            P(None, ROW),
            P(ROW, "c"),
            P("c"),
            P("c"),
            P("c"),
            P("c"),
            P("c"),
            P(ROW, "c"),
            P(ROW),
            P(ROW, "c"),
            P("c"),
        ),
        check_vma=False,
    )
```

```python
import functools

import jax
import jax.numpy as jnp
from jax import lax
from jax.experimental import pallas as pl
from jax.experimental.pallas import tpu as pltpu
from jax.sharding import Mesh
from jax.sharding import PartitionSpec as P


HDIM = 64
D = 1088
HALF = D // 2
TOK = 128
LEN = 1024
SLOT = 192
EPSILON = 1e-05
MASKED = -1e30
DP = ("zl", "y")
ROW = ("x", "zh")
ALL = ("zl", "y", "x", "zh", "c")
MESH = pl.DeviceIdType.MESH
PART = 68
BF = jnp.bfloat16
F32 = jnp.float32


class Links:
    def __init__(self, send, recv, local):
        self.send, self.recv, self.local = send, recv, local
        self.pushed, self.kept = [], []
        self.x, self.c, self.y = lax.axis_index("x"), lax.axis_index("c"), lax.axis_index("y")
        self.zh, self.zl = lax.axis_index("zh"), lax.axis_index("zl")
        self.rank = 2 * self.x + self.c
        self.sibling = {"c": 1 - self.c}
        self.partner = {"zh": 1 - self.zh}

    def along_x(self, k):
        return {"x": lax.rem(self.x + k, 4)}

    def along_y(self, k):
        return {"y": lax.rem(self.y + k, 4)}

    def line(self):
        found = []
        for k, j in ((2, 0), (2, 1), (1, 0), (1, 1), (3, 0), (3, 1), (0, 1)):
            found.append((lax.rem(self.x + k, 4), lax.rem(self.c + j, 2)))
        return [({"x": x, "c": c}, 2 * x + c) for x, c in found]

    def plane(self, both=True):
        found = []
        for h in (1, 0) if both else (0,):
            for l in (1, 0):
                for k in (2, 1, 3, 0):
                    if h or l or k:
                        y, zl = lax.rem(self.y + k, 4), lax.rem(self.zl + l, 2)
                        zh = lax.rem(self.zh + h, 2)
                        found.append(({"y": y, "zl": zl, "zh": zh}, zh, 2 * y + zl))
        return found

    def greet(self, targets):
        barrier = pltpu.get_barrier_semaphore()
        for target in targets:
            pl.semaphore_signal(barrier, inc=1, device_id=target, device_id_type=MESH)
        pl.semaphore_wait(barrier, len(targets))

    def push(self, src, dst, target):
        n = len(self.pushed)
        copy = pltpu.make_async_remote_copy(
            src_ref=src,
            dst_ref=dst,
            send_sem=self.send.at[n],
            recv_sem=self.recv.at[n],
            device_id=target,
            device_id_type=MESH,
        )
        copy.start()
        self.pushed.append([copy, False])
        return n

    def arrived(self, n):
        if not self.pushed[n][1]:
            self.pushed[n][0].wait_recv()
            self.pushed[n][1] = True

    def keep(self, src, dst):
        n = len(self.kept)
        copy = pltpu.make_async_copy(src, dst, self.local.at[n])
        copy.start()
        self.kept.append([copy, False])
        return n

    def stored(self, n):
        if not self.kept[n][1]:
            self.kept[n][0].wait()
            self.kept[n][1] = True

    def finish(self):
        for n in range(len(self.kept)):
            self.stored(n)
        for n in range(len(self.pushed)):
            self.arrived(n)
        for copy, _ in self.pushed:
            copy.wait_send()


SEMS = [pltpu.SemaphoreType.DMA((64,)), pltpu.SemaphoreType.DMA((64,)), pltpu.SemaphoreType.DMA((32,))]
SPACES = {"v": pltpu.VMEM, "h": pl.ANY}


def call(kernel, name, cid, args, spaces, outs, scratch=()):
    return pl.pallas_call(
        kernel,
        out_shape=tuple(jax.ShapeDtypeStruct(shape, dtype) for _, shape, dtype in outs),
        in_specs=[pl.BlockSpec(memory_space=SPACES[s]) for s in spaces],
        out_specs=tuple(pl.BlockSpec(memory_space=SPACES[s]) for s, _, _ in outs),
        scratch_shapes=[*scratch, *SEMS],
        compiler_params=pltpu.CompilerParams(
            collective_id=cid, has_side_effects=True, vmem_limit_bytes=44 << 20
        ),
        name=name,
    )(*args)


class Gather:
    def __init__(self, links, a_ref, o_ref):
        self.links, self.o = links, o_ref
        links.keep(a_ref, o_ref.at[links.rank])
        self.far = {k: links.push(a_ref, o_ref.at[links.rank], links.along_x(k)) for k in (2, 1, 3)}
        links.push(a_ref, o_ref.at[links.rank], links.sibling)

    def forward(self, k):
        links = self.links
        links.arrived(self.far[k])
        slot = 2 * lax.rem(links.x + 4 - k, 4) + links.c
        links.push(self.o.at[slot], self.o.at[slot], links.sibling)


class Scatter:
    def __init__(self, links, p_ref, near, out, came):
        self.links, self.p, self.near, self.out, self.came = links, p_ref, near, out, came
        self.swaps = {}
        for k in (2, 1, 3, 0):
            to = lax.rem(links.x + k, 4)
            self.swaps[k] = links.push(p_ref.at[2 * to + 1 - links.c], near.at[k], links.sibling)
        self.sends = {}

    def both(self, k):
        links = self.links
        links.arrived(self.swaps[k])
        to = lax.rem(links.x + k, 4)
        return self.p[2 * to + links.c].astype(F32) + self.near[k].astype(F32)

    def forward(self):
        for k in (2, 1, 3):
            self.out[k] = self.both(k).astype(BF)
            self.sends[k] = self.links.push(self.out.at[k], self.came.at[k], self.links.along_x(k))

    def total(self):
        total = self.both(0)
        for k in (1, 3, 2):
            self.links.arrived(self.sends[k])
            total += self.came[k].astype(F32)
        return total


SCATTER_ROOM = [pltpu.VMEM((4, TOK, D), BF)] * 3
PIECES = (8, PART, HALF)
GRADS_ROOM = [pltpu.VMEM((2, *PIECES), BF), pltpu.VMEM((16, PART, HALF), BF)]


class GradScatter:
    def __init__(self, links, parts, came):
        self.links, self.parts, self.came = links, parts, came

    @staticmethod
    def between_cores(links, own, parts):
        kept = links.keep(own.at[links.c], parts.at[links.c])
        swap = links.push(own.at[1 - links.c], parts.at[links.c], links.sibling)
        return kept, swap

    def start(self):
        self.sends = [
            self.links.push(self.parts.at[zh, piece], self.came.at[n + 1], target)
            for n, (target, zh, piece) in enumerate(self.links.plane())
        ]

    def total(self):
        links = self.links
        total = self.parts[links.zh, 2 * links.y + links.zl].astype(F32)
        for n, send in enumerate(self.sends):
            links.arrived(send)
            total += self.came[n + 1].astype(F32)
        return total.astype(BF)


def spread_grads(links, piece_ref, o_ref):
    slot = o_ref.at[2 * links.y + links.zl]
    links.keep(piece_ref, slot)
    for target, _, _ in links.plane(both=False):
        links.push(piece_ref, slot, target)


def targets(links, *groups):
    found = []
    for group in groups:
        if group == "x":
            found += [links.along_x(k) for k in (1, 2, 3)]
        if group == "y":
            found += [links.along_y(k) for k in (1, 2, 3)]
        if group == "c":
            found.append(links.sibling)
        if group == "z":
            found.append(links.partner)
        if group == "line":
            found += [target for target, _ in links.line()]
        if group == "plane":
            found += [target for target, _, _ in links.plane()]
    return found


def enter_kernel(a_ref, wo_ref, cols_ref, tok_ref, wo4_ref, colso_ref, pair, *sems):
    links = Links(*sems)
    x, zh, c = links.x, links.zh, links.c
    links.greet(targets(links, "x", "c", "z"))
    other = links.push(a_ref.at[1 - zh], pair.at[zh], links.partner)
    mine = links.keep(a_ref.at[zh], pair.at[zh])
    for k in (2, 1, 3):
        links.push(wo_ref, wo4_ref.at[x], links.along_x(k))
    links.keep(wo_ref, wo4_ref.at[x])
    links.push(cols_ref, colso_ref.at[c], links.sibling)
    links.keep(cols_ref, colso_ref.at[c])
    links.stored(mine)
    links.arrived(other)
    links.push(pair.at[1 - c], tok_ref.at[c], links.sibling)
    links.keep(pair.at[c], tok_ref.at[c])
    links.finish()


def enter(block_in, output_weight, columns):
    return call(
        enter_kernel,
        "enter",
        1,
        (block_in, output_weight, columns),
        "hhv",
        [("v", (2, TOK, HALF), BF), ("h", (4, 136, HALF), BF), ("v", (2, 8, HALF), F32)],
        [pltpu.VMEM((2, TOK, HALF), BF)],
    )


def first_kernel(n_ref, t_ref, w_ref, tail_ref, rows_ref, wo4_ref, o_ref, to_ref, wq_ref, tails_ref, rowso_ref, woo_ref, pair, mid, *sems):
    links = Links(*sems)
    x, y, zh, c = links.x, links.y, links.zh, links.c
    right, left = lax.rem(x + 1, 4), lax.rem(x + 3, 4)
    diagonal = [{"x": right, "zh": 1 - zh}, {"x": left, "zh": 1 - zh}]
    links.greet(targets(links, "x", "y", "c", "z") + diagonal)
    gather = Gather(links, n_ref, o_ref)
    t_other = links.push(t_ref.at[1 - zh], pair.at[zh], links.partner)
    t_mine = links.keep(t_ref.at[zh], pair.at[zh])
    wo_own = links.push(wo4_ref.at[y], mid, links.partner)
    rows_other = links.push(rows_ref, rowso_ref.at[zh], links.partner)
    links.keep(rows_ref, rowso_ref.at[zh])
    w_other = links.push(w_ref, wq_ref.at[c, zh], links.partner)
    links.keep(w_ref, wq_ref.at[c, zh])
    links.push(w_ref, wq_ref.at[c, zh], links.sibling)
    n = len(links.pushed)
    shifts = []
    for i, target in enumerate(({"x": right}, diagonal[0])):
        for j, (src, dst) in enumerate(((tail_ref, tails_ref.at[c]), (rows_ref, rowso_ref.at[2]))):
            shifts.append(
                pltpu.make_async_remote_copy(
                    src_ref=src,
                    dst_ref=dst,
                    send_sem=links.send.at[50 + 2 * i + j],
                    recv_sem=links.recv.at[50 + j],
                    device_id=target,
                    device_id_type=MESH,
                )
            )

    @pl.when(zh == 1)
    def _():
        for copy in shifts:
            copy.start()

    links.keep(wo4_ref, woo_ref.at[c, zh])
    links.push(wo4_ref, woo_ref.at[c, zh], links.sibling)
    gather.forward(1)
    gather.forward(3)
    links.stored(t_mine)
    links.arrived(t_other)
    links.push(pair.at[1 - c], to_ref.at[c], links.sibling)
    links.keep(pair.at[c], to_ref.at[c])
    links.arrived(wo_own)
    slot = woo_ref.at[c, 1 - zh, y]
    links.keep(mid, slot)
    round_y = [links.push(mid, slot, links.along_y(k)) for k in (2, 1, 3)]
    links.push(mid, slot, links.sibling)
    shifts[0].wait_recv()
    shifts[1].wait_recv()
    links.push(tails_ref.at[c], tails_ref.at[c], links.sibling)
    for k, copy in zip((2, 1, 3), round_y):
        links.arrived(copy)
        slot = woo_ref.at[c, 1 - zh, lax.rem(y + 4 - k, 4)]
        links.push(slot, slot, links.sibling)
    links.arrived(w_other)
    slot = wq_ref.at[c, 1 - zh]
    links.push(slot, slot, links.sibling)
    gather.forward(2)
    links.finish()

    @pl.when(zh == 1)
    def _():
        for copy in shifts:
            copy.wait_send()


def first(normed, out_grad, w, tail, rows, wo4):
    return call(
        first_kernel,
        "first",
        2,
        (normed, out_grad, w, tail, rows, wo4),
        "vhhhvh",
        [
            ("v", (8, TOK, D), BF),
            ("v", (2, TOK, HALF), BF),
            ("h", (2, 2, 3, 136, HALF), BF),
            ("h", (2, 3, 48, HALF), BF),
            ("v", (3, 8, 128), F32),
            ("h", (2, 2, 4, 136, HALF), BF),
        ],
        [pltpu.VMEM((2, TOK, HALF), BF), pltpu.VMEM((136, HALF), BF)],
    )


BLOCK = 256


def dot(a, b, dims):
    return lax.dot_general(a, b, (dims, ((), ())), preferred_element_type=F32)


def attend_head(qkv_ref, h, m_ref, p_ref):
    keys = lax.broadcasted_iota(jnp.int32, (BLOCK, BLOCK), 0)
    queries = lax.broadcasted_iota(jnp.int32, (BLOCK, BLOCK), 1)
    head = pl.ds(h * HDIM, HDIM)
    for i in range(LEN // BLOCK):
        low, high = i * BLOCK, (i + 1) * BLOCK
        q = qkv_ref[0, head, low:high] * BF(HDIM**-0.5)
        parts = [dot(qkv_ref[1, head, low:high], q, ((0,), (0,)))]
        parts[0] = jnp.where(keys <= queries, parts[0], MASKED)
        if i:
            parts.insert(0, dot(qkv_ref[1, head, :low], q, ((0,), (0,))))
        highest = functools.reduce(jnp.maximum, [jnp.max(s, axis=0, keepdims=True) for s in parts])
        parts = [jnp.exp(s - highest) for s in parts]
        share = 1.0 / sum(jnp.sum(s, axis=0, keepdims=True) for s in parts)
        parts = [(s * share).astype(BF) for s in parts]
        p_ref[h, low:high, low:high] = parts[-1]
        mixed = dot(qkv_ref[2, head, low:high], parts[-1], ((1,), (0,)))
        if i:
            p_ref[h, :low, low:high] = parts[0]
            mixed += dot(qkv_ref[2, head, :low], parts[0], ((1,), (0,)))
        m_ref[head, low:high] = mixed.astype(BF)


def attend_kernel(qkv_ref, t_ref, m_ref, p_ref, f_ref, o_ref, *sems):
    links = Links(*sems)
    links.greet(targets(links, "line"))
    gather = Gather(links, t_ref, o_ref)
    for h in range(SLOT // HDIM):
        attend_head(qkv_ref, h, m_ref, p_ref)
    own = links.rank
    columns = pl.ds(pl.multiple_of(own * TOK, TOK), TOK)
    links.keep(m_ref.at[:, columns], f_ref.at[own])
    for target, rank in links.line():
        columns = pl.ds(pl.multiple_of(rank * TOK, TOK), TOK)
        links.push(m_ref.at[:, columns], f_ref.at[own], target)
    for k in (1, 3, 2):
        gather.forward(k)
    links.finish()


def attend(qkv, tangent):
    return call(
        attend_kernel,
        "attend",
        3,
        (qkv, tangent),
        "vv",
        [
            ("v", (SLOT, LEN), BF),
            ("v", (SLOT // HDIM, LEN, LEN), BF),
            ("v", (8, SLOT, TOK), BF),
            ("v", (8, TOK, D), BF),
        ],
    )


def second_kernel(n_ref, up_ref, down_ref, o_ref, upo_ref, downo_ref, up_pair, down_pair, *sems):
    links = Links(*sems)
    y, zh, c = links.y, links.zh, links.c
    links.greet(targets(links, "x", "y", "c", "z"))
    gather = Gather(links, n_ref, o_ref)
    crossed = []
    for w_ref, pair in ((up_ref, up_pair), (down_ref, down_pair)):
        crossed.append((links.push(w_ref.at[y], pair.at[zh, y], links.partner), links.keep(w_ref, pair.at[zh])))
    turned = []
    for (other, _), pair in zip(crossed, (up_pair, down_pair)):
        links.arrived(other)
        slot = pair.at[1 - zh, y]
        turned.append([links.push(slot, slot, links.along_y(k)) for k in (2, 1, 3)])
    gather.forward(1)
    gather.forward(3)
    for (_, kept), copies, pair, out in zip(crossed, turned, (up_pair, down_pair), (upo_ref, downo_ref)):
        links.stored(kept)
        for copy in copies:
            links.arrived(copy)
        links.push(pair.at[1 - c], out.at[c], links.sibling)
        links.keep(pair.at[c], out.at[c])
    gather.forward(2)
    links.finish()


def second(normed, up, down):
    return call(
        second_kernel,
        "second",
        4,
        (normed, up, down),
        "vhh",
        [("v", (8, TOK, D), BF), ("v", (2, 4, 136, HALF), BF), ("v", (2, 4, 136, HALF), BF)],
        [pltpu.VMEM((2, 4, 136, HALF), BF)] * 2,
    )


def hidden_kernel(n_ref, t_ref, up_ref, down_ref, b_ref, low_ref, dn_ref, gup_ref, gdown_ref, gb_ref, up, down, up_sum, down_sum):
    step = pl.program_id(0)

    @pl.when(step == 0)
    def _():
        for h in range(2):
            up[:, h * HALF : (h + 1) * HALF] = up_ref[h]
            down[:, h * HALF : (h + 1) * HALF] = down_ref[h]
        up_sum[...] = jnp.zeros_like(up_sum)
        down_sum[...] = jnp.zeros_like(down_sum)
        gb_ref[...] = jnp.zeros_like(gb_ref)

    n = n_ref[...].reshape(BLOCK, D)
    t = t_ref[...].reshape(BLOCK, D)
    pre = dot(n, up[...], ((1,), (1,))) + b_ref[...]
    cumulative = 0.5 * (1.0 + lax.erf(pre * 0.7071067811865476))
    density = jnp.exp(-0.5 * pre * pre) * 0.3989422804014327
    active = (pre * cumulative).astype(BF)
    slope = cumulative + pre * density
    low_ref[...] = dot(active, down[...], ((1,), (0,))).astype(BF).reshape(low_ref.shape)
    d_pre = (dot(t, down[...], ((1,), (1,))) * slope).astype(BF)
    dn_ref[...] = dot(d_pre, up[...], ((1,), (0,))).astype(BF).reshape(dn_ref.shape)
    down_sum[...] += dot(active, t, ((0,), (0,)))
    up_sum[...] += dot(d_pre, n, ((0,), (0,)))
    gb_ref[...] += jnp.sum(d_pre.astype(F32), axis=0, keepdims=True)

    @pl.when(step == pl.num_programs(0) - 1)
    def _():
        for h in range(2):
            for out, total in ((gup_ref, up_sum), (gdown_ref, down_sum)):
                for j in range(8):
                    out[h, j] = total[j * PART : (j + 1) * PART, h * HALF : (h + 1) * HALF].astype(BF)


def hidden_part(second_rows, tangent_rows, up, down, bias):
    rows = pl.BlockSpec((BLOCK // TOK, TOK, D), lambda i: (i, 0, 0))
    weight = pl.BlockSpec((2, HALF, HALF), lambda i: (0, 0, 0))
    grad = pl.BlockSpec((2, *PIECES), lambda i: (0, 0, 0, 0))
    one = pl.BlockSpec((1, HALF), lambda i: (0, 0))
    return pl.pallas_call(
        hidden_kernel,
        grid=(LEN // BLOCK,),
        in_specs=[rows, rows, weight, weight, one],
        out_specs=(rows, rows, grad, grad, one),
        out_shape=(
            jax.ShapeDtypeStruct((8, TOK, D), BF),
            jax.ShapeDtypeStruct((8, TOK, D), BF),
            jax.ShapeDtypeStruct((2, *PIECES), BF),
            jax.ShapeDtypeStruct((2, *PIECES), BF),
            jax.ShapeDtypeStruct((1, HALF), F32),
        ),
        scratch_shapes=[pltpu.VMEM((HALF, D), BF)] * 2 + [pltpu.VMEM((HALF, D), F32)] * 2,
        compiler_params=pltpu.CompilerParams(vmem_limit_bytes=44 << 20),
        name="hidden_part",
    )(second_rows, tangent_rows, up, down, bias)


def third_kernel(p_ref, g_ref, o_ref, piece_ref, near, out, came, parts, found, *sems):
    links = Links(*sems)
    links.greet(targets(links, "x", "c", "plane"))
    scatter = Scatter(links, p_ref, near, out, came)
    grads = GradScatter(links, parts, found)
    kept, swap = grads.between_cores(links, g_ref, parts)
    scatter.forward()
    links.stored(kept)
    links.arrived(swap)
    grads.start()
    o_ref[...] = scatter.total()
    piece_ref[...] = grads.total()
    links.finish()


def third(d_normed, grad):
    return call(
        third_kernel,
        "third",
        5,
        (d_normed, grad),
        "vv",
        [("v", (TOK, D), F32), ("v", (PART, HALF), BF)],
        SCATTER_ROOM + GRADS_ROOM,
    )


def attend_back_head(qkv_ref, h, u_ref, p_ref, d_ref, dk_sum, dv_sum):
    head = pl.ds(h * HDIM, HDIM)
    for i in range(LEN // BLOCK):
        low, high = i * BLOCK, (i + 1) * BLOCK
        q = qkv_ref[0, head, low:high] * BF(HDIM**-0.5)
        u = u_ref[head, low:high]
        p = p_ref[h, :high, low:high]
        wide = p.astype(F32)
        dp = dot(qkv_ref[2, head, :high], u, ((0,), (0,)))
        centre = jnp.sum(wide * dp, axis=0, keepdims=True)
        ds = (wide * (dp - centre)).astype(BF)
        d_ref[0, head, low:high] = (dot(qkv_ref[1, head, :high], ds, ((1,), (0,))) * HDIM**-0.5).astype(BF)
        dk = dot(q, ds, ((1,), (1,)))
        dv = dot(u, p, ((1,), (1,)))
        if i:
            dk_sum[:, :low] += dk[:, :low]
            dv_sum[:, :low] += dv[:, :low]
        dk_sum[:, low:high] = dk[:, low:]
        dv_sum[:, low:high] = dv[:, low:]
    d_ref[1, head] = dk_sum[...].astype(BF)
    d_ref[2, head] = dv_sum[...].astype(BF)


def back_kernel(m_ref, a_ref, qkv_ref, p_ref, g_ref, d_ref, o_ref, piece_ref, u, dk_sum, dv_sum, parts, found, *sems):
    links = Links(*sems)
    links.greet(targets(links, "line", "plane"))
    own = links.rank
    columns = pl.ds(pl.multiple_of(own * TOK, TOK), TOK)

    def rows(rank):
        return pl.ds(pl.multiple_of(rank * 2 * HDIM, 2 * HDIM), SLOT)

    mine = links.keep(m_ref.at[rows(own)], u.at[:, columns])
    others = [links.push(m_ref.at[rows(rank)], u.at[:, columns], target) for target, rank in links.line()]
    gather = Gather(links, a_ref, o_ref)
    grads = GradScatter(links, parts, found)
    kept, swap = grads.between_cores(links, g_ref, parts)
    links.stored(kept)
    links.arrived(swap)
    grads.start()
    links.stored(mine)
    for copy in others:
        links.arrived(copy)
    for h in range(SLOT // HDIM):
        attend_back_head(qkv_ref, h, u, p_ref, d_ref, dk_sum, dv_sum)
    for k in (1, 3, 2):
        gather.forward(k)
    piece_ref[...] = grads.total()
    links.finish()


def back(d_mixed, d_attended, qkv, probs, grad):
    return call(
        back_kernel,
        "back",
        6,
        (d_mixed, d_attended, qkv, probs, grad),
        "vvvvv",
        [("v", (3, SLOT, LEN), BF), ("v", (8, TOK, D), BF), ("v", (PART, HALF), BF)],
        [pltpu.VMEM((SLOT, LEN), BF)] + [pltpu.VMEM((HDIM, LEN), F32)] * 2 + GRADS_ROOM,
    )


def fourth_kernel(p_ref, up_ref, down_ref, s_ref, o_ref, gup_ref, gdown_ref, chip_ref, tail_ref, near, out, came, *sems):
    links = Links(*sems)
    c = links.c
    links.greet(targets(links, "x", "c", "plane"))
    scatter = Scatter(links, p_ref, near, out, came)
    kept = links.keep(s_ref.at[c], chip_ref.at[c])
    swap = links.push(s_ref.at[1 - c], chip_ref.at[c], links.sibling)
    spread_grads(links, up_ref, gup_ref)
    spread_grads(links, down_ref, gdown_ref)
    scatter.forward()
    links.stored(kept)
    links.arrived(swap)
    links.push(chip_ref.at[0, :, pl.ds(0, 48)], tail_ref, links.along_x(3))
    o_ref[...] = scatter.total()
    links.finish()


def fourth(d_normed, up_piece, down_piece, slots):
    return call(
        fourth_kernel,
        "fourth",
        7,
        (d_normed, up_piece, down_piece, slots),
        "vvvv",
        [
            ("v", (TOK, D), F32),
            ("h", PIECES, BF),
            ("h", PIECES, BF),
            ("v", (2, 4, SLOT, HALF), BF),
            ("v", (4, 48, HALF), BF),
        ],
        SCATTER_ROOM,
    )


def leave_kernel(p_ref, r_ref, i_ref, g_ref, v_ref, b_ref, oo_ref, io_ref, go_ref, vo_ref, near, out, came, found, piece, halves_o, pair_o, pair_i, v_line, v_own, v_plane, v_sum, *sems):
    links = Links(*sems)
    y, zh, zl, c = links.y, links.zh, links.zl, links.c
    links.greet(targets(links, "line", "plane"))
    scatter = Scatter(links, p_ref, near, out, came)
    grads = GradScatter(links, g_ref, found)
    line = [links.push(v_ref.at[rank], v_line.at[n], target) for n, (target, rank) in enumerate(links.line())]

    def between_cores(src, pair):
        return links.keep(src.at[c], pair.at[c]), links.push(src.at[1 - c], pair.at[c], links.sibling)

    def to_partner(src, pair, dst, copies):
        links.stored(copies[0])
        links.arrived(copies[1])
        links.push(pair.at[1 - zh], dst.at[zh], links.partner)
        links.keep(pair.at[zh], dst.at[zh])

    copies = between_cores(i_ref, pair_i)
    scatter.forward()
    grads.start()
    to_partner(i_ref, pair_i, io_ref, copies)
    total = v_ref[links.rank]
    for n, copy in enumerate(line):
        links.arrived(copy)
        total += v_line[n]
    v_own[pl.ds(0, 16)] = total
    v_own[pl.ds(16, 8)] = b_ref[...]
    place = (2 * zh + zl) * 4 + y
    kept = links.keep(v_own, v_plane.at[place])
    plane = [links.push(v_own, v_plane.at[place], target) for target, _, _ in links.plane()]
    links.stored(kept)
    for copy in plane:
        links.arrived(copy)
    total = v_plane[0]
    for n in range(1, 16):
        total += v_plane[n]
    v_sum[...] = total
    links.keep(v_sum, vo_ref.at[links.rank])
    for target, _ in links.line():
        links.push(v_sum, vo_ref.at[links.rank], target)
    result = (scatter.total() + r_ref[...]).astype(BF)
    halves_o[0] = result[:, :HALF]
    halves_o[1] = result[:, HALF:]
    copies = between_cores(halves_o, pair_o)
    piece[...] = grads.total()
    spread_grads(links, piece, go_ref)
    to_partner(halves_o, pair_o, oo_ref, copies)
    links.finish()


def leave(lowered, residual, in_grad, grads, vectors, bias_up):
    pair = pltpu.VMEM((2, TOK, HALF), BF)
    return call(
        leave_kernel,
        "leave",
        8,
        (lowered, residual, in_grad, grads, vectors, bias_up),
        "vvvvvv",
        [
            ("v", (2, TOK, HALF), BF),
            ("v", (2, TOK, HALF), BF),
            ("v", PIECES, BF),
            ("v", (8, 24, 128), F32),
        ],
        SCATTER_ROOM
        + [GRADS_ROOM[1], pltpu.VMEM((PART, HALF), BF), pair, pair, pair]
        + [pltpu.VMEM((7, 16, 128), F32), pltpu.VMEM((24, 128), F32)]
        + [pltpu.VMEM((16, 24, 128), F32), pltpu.VMEM((24, 128), F32)],
    )


def normed(values, gain, shift):
    centre = jnp.mean(values, axis=1, keepdims=True)
    second_moment = jnp.mean(values * values, axis=1, keepdims=True)
    inverse = lax.rsqrt(second_moment - centre * centre + EPSILON)
    centred = (values - centre) * inverse
    return (centred * gain + shift).astype(BF), centred, inverse


def normed_back(upstream, centred, inverse, gain):
    scaled = upstream * gain
    result = inverse * (
        scaled
        - jnp.mean(scaled, axis=1, keepdims=True)
        - centred * jnp.mean(scaled * centred, axis=1, keepdims=True)
    )
    return result, jnp.sum(upstream * centred, axis=0), jnp.sum(upstream, axis=0)


def joined(halves):
    return jnp.concatenate([halves[0], halves[1]], axis=-1)


def parted(whole):
    return jnp.stack([whole[..., :HALF], whole[..., HALF:]])


def per_device(
    block_in,
    query_key_value_weight,
    bias_qv,
    output_weight,
    bias_out,
    gain_one,
    shift_one,
    gain_two,
    shift_two,
    up_weight,
    bias_up,
    down_weight,
    bias_down,
    out_grad,
):
    x, zh, c = (lax.axis_index(a) for a in ("x", "zh", "c"))
    rank = 2 * x + c
    last = rank == 7
    real = jnp.logical_or(jnp.arange(SLOT) < 128, last)

    columns = jnp.stack([bias_out, gain_one, shift_one, gain_two, shift_two, bias_down, bias_down, bias_down])
    tokens, wo4, columns = enter(block_in, output_weight, columns)
    inputs = joined(tokens).astype(F32)
    bias_out, gain_one, shift_one, gain_two, shift_two, bias_down = joined(columns)[:6]
    normed_one, centred_one, inverse_one = normed(inputs, gain_one, shift_one)
    rows = jnp.concatenate([bias_qv.reshape(-1), bias_up, jnp.zeros((208,), F32)]).reshape(8, 128)
    first_rows, tangent, wq, tails, rows, wo = first(
        normed_one, out_grad, query_key_value_weight, query_key_value_weight[:, 88:], rows, wo4
    )
    tangent = joined(tangent)

    def slots(before, chip):
        width = chip.ndim - 2
        spare = jnp.zeros((*chip.shape[:-2], 48, chip.shape[-1]), chip.dtype)
        chip = jnp.concatenate([before, chip, spare], axis=width)
        return lax.dynamic_slice_in_dim(chip, 48 - 16 * x + 128 * c, SLOT, width)

    w = [
        slots(tails[h], jnp.concatenate([wq[h, 0], wq[h, 1]], axis=1)) for h in range(2)
    ]
    weight_qkv = jnp.where(real[None, :, None], joined(w), BF(0))
    rows = rows.reshape(3, 1024)
    bias_up = lax.dynamic_slice(rows, (c, 272), (1, HALF))
    qv = rows[:, :272].reshape(3, 2, 136)
    qv = slots(qv[2, :, 88:, None], jnp.concatenate([qv[0], qv[1]], axis=1)[..., None])[..., 0]
    qv = jnp.where(real[None], qv, 0.0)
    bias_qkv = jnp.stack([qv[0], jnp.zeros_like(qv[0]), qv[1]])

    flat_rows = first_rows.reshape(LEN, D)
    qkv = jnp.einsum("koi,ti->kot", weight_qkv, flat_rows, preferred_element_type=F32)
    qkv = (qkv + bias_qkv[..., None]).astype(BF)
    mixed, probs, found, tangent_rows = attend(qkv, tangent)
    mixed_here = jnp.concatenate([found[:7, :128].reshape(896, TOK), found[7]])
    wo = jnp.transpose(wo, (0, 2, 1, 3, 4)).reshape(2, D, HALF)
    attended = [jnp.einsum("ft,fo->to", mixed_here, wo[h], preferred_element_type=F32) for h in range(2)]
    residual = inputs + (joined(attended) + bias_out)

    normed_two, centred_two, inverse_two = normed(residual, gain_two, shift_two)
    quarters = (4, 136, HALF)
    second_rows, up, down = second(normed_two, up_weight.reshape(quarters), down_weight.reshape(quarters))
    lowered, d_normed_two, up_grad, down_grad, grad_bias_up = hidden_part(
        second_rows,
        tangent_rows,
        up.reshape(2, HALF, HALF),
        down.reshape(2, HALF, HALF),
        bias_up,
    )
    d_normed_two, down_piece = third(d_normed_two, down_grad)
    tangent = tangent.astype(F32)
    grad_bias_down = jnp.sum(tangent, axis=0)
    part, grad_gain_two, grad_shift_two = normed_back(d_normed_two, centred_two, inverse_two, gain_two)
    d_residual = tangent + part
    d_attended = d_residual.astype(BF)
    grad_bias_out = jnp.sum(d_attended, axis=0, dtype=F32)

    d_mixed = sum(
        jnp.einsum("fo,to->ft", wo[h], d_attended[:, h * HALF : (h + 1) * HALF], preferred_element_type=F32)
        for h in range(2)
    ).astype(BF)
    d_qkv, attended_rows, up_piece = back(d_mixed, d_attended, qkv, probs, up_grad)
    attended_rows = attended_rows.reshape(LEN, D)
    d_normed_one = jnp.einsum("kot,koi->ti", d_qkv, weight_qkv, preferred_element_type=F32).astype(BF)
    grad_qkv = jnp.einsum("kot,ti->koi", d_qkv, flat_rows, preferred_element_type=F32).astype(BF)
    grad_out = jnp.einsum("ft,to->fo", mixed, attended_rows, preferred_element_type=F32).astype(BF)
    grads = parted(jnp.concatenate([grad_qkv, grad_out[None]]))
    d_normed_one, up_grad, down_grad, chip, tail = fourth(
        d_normed_one.reshape(8, TOK, D), up_piece, down_piece, grads
    )
    tail = jnp.pad(tail, ((0, 0), (0, 16), (0, 0)))
    chip = jnp.concatenate([chip[0, :, :128], chip[1, :, :128], jnp.where(x == 3, chip[1, :, 128:], tail)], axis=1)
    chip = lax.dynamic_slice_in_dim(chip, 16 * x, 272, 1)
    chip = jnp.transpose(chip.reshape(4, 2, 2, PART, HALF), (1, 0, 2, 3, 4)).reshape(2, *PIECES)

    part, grad_gain_one, grad_shift_one = normed_back(d_normed_one, centred_one, inverse_one, gain_one)
    in_grad = parted((d_residual + part).astype(BF))

    bias_sums = jnp.sum(d_qkv, axis=2, dtype=F32)
    bias_sums = jnp.where(real[None], jnp.stack([bias_sums[0], bias_sums[2]]), 0.0)
    wide = lax.dynamic_update_slice(jnp.zeros((2, D), F32), bias_sums, (0, 128 * rank))
    vectors = jnp.stack(
        [grad_bias_out, grad_gain_one, grad_shift_one, grad_gain_two, grad_shift_two, grad_bias_down, wide[0], wide[1]]
    )
    vectors = jnp.pad(vectors, ((0, 0), (0, 2048 - D))).reshape(8, 16, 128)
    grad_bias_up = jnp.pad(grad_bias_up.reshape(-1), (0, 480)).reshape(8, 128)
    block_out, in_grad, grads, vectors = leave(lowered, residual + bias_down, in_grad, chip, vectors, grad_bias_up)
    grads = grads.reshape(4, 136, HALF).astype(F32)
    row = 2 * x + zh
    grad_bias_up = lax.dynamic_index_in_dim(vectors, row, 0, keepdims=False)[16:].reshape(-1)[:HALF]
    vectors = vectors[:, :16].reshape(8, 2048)[:, :D]
    six = lax.dynamic_slice_in_dim(vectors[:6], HALF * c, HALF, 1)
    grad_bias_out, grad_gain_one, grad_shift_one, grad_gain_two, grad_shift_two, grad_bias_down = six
    grad_bias_qv = lax.dynamic_slice_in_dim(vectors[6:], 136 * row, 136, 1)

    return (
        block_out,
        in_grad.astype(F32),
        grads[:3],
        grad_bias_qv,
        grads[3],
        grad_bias_out,
        grad_gain_one,
        grad_shift_one,
        grad_gain_two,
        grad_shift_two,
        up_grad.reshape(HALF, HALF).astype(F32),
        grad_bias_up,
        down_grad.reshape(HALF, HALF).astype(F32),
        grad_bias_down,
    )


def solution(mesh):
    finer = Mesh(mesh.devices.reshape(2, 4, 4, 2, 2), ALL)
    return jax.shard_map(
        per_device,
        mesh=finer,
        in_specs=(
            P(DP, ROW, "c"),
            P(None, ROW, "c"),
            P(None, ROW),
            P(ROW, "c"),
            P("c"),
            P("c"),
            P("c"),
            P("c"),
            P("c"),
            P(ROW, "c"),
            P(ROW),
            P(ROW, "c"),
            P("c"),
            P(DP, ROW, "c"),
        ),
        out_specs=(
            P(DP, ROW, "c"),
            P(DP, ROW, "c"),
            P(None, ROW, "c"),
            P(None, ROW),
            P(ROW, "c"),
            P("c"),
            P("c"),
            P("c"),
            P("c"),
            P("c"),
            P(ROW, "c"),
            P(ROW),
            P(ROW, "c"),
            P("c"),
        ),
        check_vma=False,
    )
```

```python
import functools

import jax
import jax.numpy as jnp
from jax import lax
from jax.experimental import pallas as pl
from jax.experimental.pallas import tpu as pltpu
from jax.sharding import Mesh
from jax.sharding import PartitionSpec as P


HDIM = 64
D = 1088
HALF = D // 2
TOK = 128
LEN = 1024
SLOT = 192
EPSILON = 1e-05
MASKED = -1e30
DP = ("zl", "y")
ROW = ("x", "zh")
ALL = ("zl", "y", "x", "zh", "c")
MESH = pl.DeviceIdType.MESH
PART = 68
BF = jnp.bfloat16
F32 = jnp.float32


class Links:
    def __init__(self, send, recv, local):
        self.send, self.recv, self.local = send, recv, local
        self.pushed, self.kept = [], []
        self.x, self.c, self.y = lax.axis_index("x"), lax.axis_index("c"), lax.axis_index("y")
        self.zh, self.zl = lax.axis_index("zh"), lax.axis_index("zl")
        self.rank = 2 * self.x + self.c
        self.sibling = {"c": 1 - self.c}
        self.partner = {"zh": 1 - self.zh}

    def along_x(self, k):
        return {"x": lax.rem(self.x + k, 4)}

    def along_y(self, k):
        return {"y": lax.rem(self.y + k, 4)}

    def line(self):
        found = []
        for k, j in ((2, 0), (2, 1), (1, 0), (1, 1), (3, 0), (3, 1), (0, 1)):
            found.append((lax.rem(self.x + k, 4), lax.rem(self.c + j, 2)))
        return [({"x": x, "c": c}, 2 * x + c) for x, c in found]

    def plane(self, both=True):
        found = []
        for h in (1, 0) if both else (0,):
            for l in (1, 0):
                for k in (2, 1, 3, 0):
                    if h or l or k:
                        y, zl = lax.rem(self.y + k, 4), lax.rem(self.zl + l, 2)
                        zh = lax.rem(self.zh + h, 2)
                        found.append(({"y": y, "zl": zl, "zh": zh}, zh, 2 * y + zl))
        return found

    def greet(self, targets):
        barrier = pltpu.get_barrier_semaphore()
        for target in targets:
            pl.semaphore_signal(barrier, inc=1, device_id=target, device_id_type=MESH)
        pl.semaphore_wait(barrier, len(targets))

    def push(self, src, dst, target):
        n = len(self.pushed)
        copy = pltpu.make_async_remote_copy(
            src_ref=src,
            dst_ref=dst,
            send_sem=self.send.at[n],
            recv_sem=self.recv.at[n],
            device_id=target,
            device_id_type=MESH,
        )
        copy.start()
        self.pushed.append([copy, False])
        return n

    def arrived(self, n):
        if not self.pushed[n][1]:
            self.pushed[n][0].wait_recv()
            self.pushed[n][1] = True

    def keep(self, src, dst):
        n = len(self.kept)
        copy = pltpu.make_async_copy(src, dst, self.local.at[n])
        copy.start()
        self.kept.append([copy, False])
        return n

    def stored(self, n):
        if not self.kept[n][1]:
            self.kept[n][0].wait()
            self.kept[n][1] = True

    def finish(self):
        for n in range(len(self.kept)):
            self.stored(n)
        for n in range(len(self.pushed)):
            self.arrived(n)
        for copy, _ in self.pushed:
            copy.wait_send()


SEMS = [pltpu.SemaphoreType.DMA((64,)), pltpu.SemaphoreType.DMA((64,)), pltpu.SemaphoreType.DMA((32,))]
SPACES = {"v": pltpu.VMEM, "h": pl.ANY}


def call(kernel, name, cid, args, spaces, outs, scratch=(), mib=12):
    return pl.pallas_call(
        kernel,
        out_shape=tuple(jax.ShapeDtypeStruct(shape, dtype) for _, shape, dtype in outs),
        in_specs=[pl.BlockSpec(memory_space=SPACES[s]) for s in spaces],
        out_specs=tuple(pl.BlockSpec(memory_space=SPACES[s]) for s, _, _ in outs),
        scratch_shapes=[*scratch, *SEMS],
        compiler_params=pltpu.CompilerParams(
            collective_id=cid, has_side_effects=True, vmem_limit_bytes=mib << 20
        ),
        name=name,
    )(*args)


def top(ref):
    return ref.at[pl.ds(0, TOK // 2)]


def bottom(ref):
    return ref.at[pl.ds(TOK // 2, TOK // 2)]


class Gather:
    def __init__(self, links, a_ref, o_ref):
        self.links, self.o = links, o_ref
        own = o_ref.at[links.rank]
        self.kept = links.keep(a_ref, own)
        right, left = links.along_x(1), links.along_x(3)
        self.ahead = [links.push(top(a_ref), top(own), right)]
        self.back = [links.push(bottom(a_ref), bottom(own), left)]
        self.ahead.append(links.push(bottom(a_ref), bottom(own), right))
        self.back.append(links.push(top(a_ref), top(own), left))
        self.near = [links.push(a_ref, own, links.sibling)]

    def slot(self, k):
        return self.o.at[2 * lax.rem(self.links.x + 4 - k, 4) + self.links.c]

    def share(self, piece):
        self.near.append(self.links.push(piece, piece, self.links.sibling))

    def relay(self):
        links = self.links
        links.arrived(self.ahead[0])
        self.far = [links.push(top(self.slot(1)), top(self.slot(1)), links.along_x(1))]
        links.arrived(self.back[0])
        self.far.append(links.push(bottom(self.slot(3)), bottom(self.slot(3)), links.along_x(3)))
        self.share(top(self.slot(1)))
        self.share(bottom(self.slot(3)))

    def middle(self):
        links = self.links
        links.arrived(self.ahead[1])
        self.share(bottom(self.slot(1)))
        links.arrived(self.back[1])
        self.share(top(self.slot(3)))

    def last(self):
        links = self.links
        links.arrived(self.far[0])
        self.share(top(self.slot(2)))
        links.arrived(self.far[1])
        self.share(bottom(self.slot(2)))

    def complete(self):
        self.links.stored(self.kept)
        for copy in self.near:
            self.links.arrived(copy)


class Scatter:
    def __init__(self, links, p_ref, near, out, came):
        self.links, self.p, self.near, self.out, self.came = links, p_ref, near, out, came
        self.swaps = {}
        for k in (2, 1, 3, 0):
            to = lax.rem(links.x + k, 4)
            self.swaps[k] = links.push(p_ref.at[2 * to + 1 - links.c], near.at[k], links.sibling)

    def both(self, k):
        links = self.links
        links.arrived(self.swaps[k])
        to = lax.rem(links.x + k, 4)
        return self.p[2 * to + links.c].astype(F32) + self.near[k].astype(F32)

    def forward(self):
        links, out, came = self.links, self.out, self.came
        right, left = links.along_x(1), links.along_x(3)
        out[2] = self.both(2).astype(BF)
        ahead = links.push(top(out.at[2]), top(came.at[2]), right)
        back = links.push(bottom(out.at[2]), bottom(came.at[2]), left)
        half = TOK // 2
        one = self.both(1)
        out[1, half:] = one[half:].astype(BF)
        self.sends = [links.push(bottom(out.at[1]), bottom(came.at[1]), right)]
        three = self.both(3)
        out[3, :half] = three[:half].astype(BF)
        self.sends.append(links.push(top(out.at[3]), top(came.at[3]), left))
        links.arrived(ahead)
        out[1, :half] = (one[:half] + came[2, :half].astype(F32)).astype(BF)
        self.sends.append(links.push(top(out.at[1]), top(came.at[1]), right))
        links.arrived(back)
        out[3, half:] = (three[half:] + came[2, half:].astype(F32)).astype(BF)
        self.sends.append(links.push(bottom(out.at[3]), bottom(came.at[3]), left))

    def total(self):
        total = self.both(0)
        for copy in self.sends:
            self.links.arrived(copy)
        return total + self.came[1].astype(F32) + self.came[3].astype(F32)


SCATTER_ROOM = [pltpu.VMEM((4, TOK, D), BF)] * 3
PACKED = PART * HALF // 128
PIECES = (8, PACKED, 128)
GRADS_ROOM = [pltpu.VMEM((2, *PIECES), BF), pltpu.VMEM((16, PACKED, 128), BF)]


def pack(rows):
    tiles = [rows[:, 128 * t : 128 * (t + 1)] for t in range(4)]
    rest = jnp.concatenate([rows[17 * q : 17 * (q + 1), 512:] for q in range(4)], axis=1)
    return jnp.concatenate([*tiles, rest], axis=0)


def unpack(packed, o_ref):
    for j in range(8):
        piece = packed[j].astype(F32)
        rows = slice(PART * j, PART * (j + 1))
        for t in range(4):
            o_ref[rows, 128 * t : 128 * (t + 1)] = piece[PART * t : PART * (t + 1)]
        rest = [piece[4 * PART :, 32 * q : 32 * (q + 1)] for q in range(4)]
        o_ref[rows, 512:] = jnp.concatenate(rest, axis=0)


class GradScatter:
    def __init__(self, links, parts, came):
        self.links, self.parts, self.came = links, parts, came

    @staticmethod
    def between_cores(links, own, parts):
        kept = links.keep(own.at[links.c], parts.at[links.c])
        swap = links.push(own.at[1 - links.c], parts.at[links.c], links.sibling)
        return kept, swap

    def start(self):
        self.sends = [
            self.links.push(self.parts.at[zh, piece], self.came.at[n + 1], target)
            for n, (target, zh, piece) in enumerate(self.links.plane())
        ]

    def total(self):
        links = self.links
        total = self.parts[links.zh, 2 * links.y + links.zl].astype(F32)
        for n, send in enumerate(self.sends):
            links.arrived(send)
            total += self.came[n + 1].astype(F32)
        return total.astype(BF)


def spread_grads(links, piece_ref, o_ref):
    slot = o_ref.at[2 * links.y + links.zl]
    kept = links.keep(piece_ref, slot)
    return kept, [links.push(piece_ref, slot, target) for target, _, _ in links.plane(both=False)]


def spread_done(links, copies):
    links.stored(copies[0])
    for copy in copies[1]:
        links.arrived(copy)


def targets(links, *groups):
    found = []
    for group in groups:
        if group == "x":
            found += [links.along_x(k) for k in (1, 2, 3)]
        if group == "y":
            found += [links.along_y(k) for k in (1, 2, 3)]
        if group == "c":
            found.append(links.sibling)
        if group == "z":
            found.append(links.partner)
        if group == "line":
            found += [target for target, _ in links.line()]
        if group == "plane":
            found += [target for target, _, _ in links.plane()]
    return found


def normed(values, gain, shift):
    centre = jnp.mean(values, axis=1, keepdims=True)
    second_moment = jnp.mean(values * values, axis=1, keepdims=True)
    inverse = lax.rsqrt(second_moment - centre * centre + EPSILON)
    centred = (values - centre) * inverse
    return (centred * gain + shift).astype(BF), centred, inverse


def enter_kernel(a_ref, wo_ref, tail_ref, b0, b1, b2, b3, b4, b5, wo4_ref, colso_ref, tailo_ref, i_ref, n_ref, cent_ref, inv_ref, pair, tok, cols, *sems):
    links = Links(*sems)
    x, y, zh, c = links.x, links.y, links.zh, links.c
    right, left = lax.rem(x + 1, 4), lax.rem(x + 3, 4)
    diagonal = [{"x": right, "zh": 1 - zh}, {"x": left, "zh": 1 - zh}]
    links.greet(targets(links, "x", "c", "z") + diagonal)
    other = links.push(a_ref.at[1 - zh], pair.at[zh], links.partner)
    mine = links.keep(a_ref.at[zh], pair.at[zh])
    for k in (2, 1, 3):
        links.push(wo_ref, wo4_ref.at[x], links.along_x(k))
    links.keep(wo_ref, wo4_ref.at[x])
    shifts = [
        pltpu.make_async_remote_copy(
            src_ref=tail_ref.at[y],
            dst_ref=tailo_ref,
            send_sem=links.send.at[50 + i],
            recv_sem=links.recv.at[50],
            device_id=target,
            device_id_type=MESH,
        )
        for i, target in enumerate(({"x": right}, diagonal[0]))
    ]

    @pl.when(zh == 1)
    def _():
        for copy in shifts:
            copy.start()

    cols[...] = jnp.concatenate([b0[...], b1[...], b2[...], b3[...], b4[...], b5[...], b5[...], b5[...]], axis=0)
    swap = links.push(cols, colso_ref.at[c], links.sibling)
    own = links.keep(cols, colso_ref.at[c])
    links.stored(mine)
    links.arrived(other)
    got = links.push(pair.at[1 - c], tok.at[c], links.sibling)
    kept = links.keep(pair.at[c], tok.at[c])
    links.arrived(swap)
    links.stored(own)
    links.stored(kept)
    links.arrived(got)
    values = jnp.concatenate([tok[0], tok[1]], axis=1).astype(F32)
    i_ref[...] = values
    gains = jnp.concatenate([colso_ref[0], colso_ref[1]], axis=1)
    n_ref[...], cent_ref[...], inv_ref[...] = normed(values, gains[1:2], gains[2:3])
    links.finish()
    shifts[0].wait_recv()

    @pl.when(zh == 1)
    def _():
        for copy in shifts:
            copy.wait_send()


def enter(block_in, output_weight, tail, columns):
    return call(
        enter_kernel,
        "enter",
        1,
        (block_in, output_weight, tail, *columns),
        "hhhvvvvvv",
        [
            ("v", (4, 136, HALF), BF),
            ("v", (2, 8, HALF), F32),
            ("v", (48, HALF), BF),
            ("v", (TOK, D), F32),
            ("v", (TOK, D), BF),
            ("v", (TOK, D), F32),
            ("v", (TOK, 1), F32),
        ],
        [pltpu.VMEM((2, TOK, HALF), BF), pltpu.VMEM((2, TOK, HALF), BF), pltpu.VMEM((8, HALF), F32)],
    )


def first_kernel(n_ref, t_ref, w_ref, tail_ref, rows_ref, wo4_ref, o_ref, to_ref, wq_ref, tails_ref, rowso_ref, woo_ref, pair, mid, *sems):
    links = Links(*sems)
    x, y, zh, c = links.x, links.y, links.zh, links.c
    right, left = lax.rem(x + 1, 4), lax.rem(x + 3, 4)
    diagonal = [{"x": right, "zh": 1 - zh}, {"x": left, "zh": 1 - zh}]
    links.greet(targets(links, "x", "y", "c", "z") + diagonal)
    gather = Gather(links, n_ref, o_ref)
    t_other = links.push(t_ref.at[1 - zh], pair.at[zh], links.partner)
    t_mine = links.keep(t_ref.at[zh], pair.at[zh])
    wo_own = links.push(wo4_ref.at[y], mid, links.partner)
    w_other = links.push(w_ref, wq_ref.at[c, zh], links.partner)
    links.keep(w_ref, wq_ref.at[c, zh])
    links.push(w_ref, wq_ref.at[c, zh], links.sibling)
    links.push(rows_ref, rowso_ref.at[zh], links.partner)
    links.keep(rows_ref, rowso_ref.at[zh])
    slot = tails_ref.at[c, y]
    links.keep(tail_ref, slot)
    links.push(tail_ref, slot, links.sibling)
    tails = [links.push(tail_ref, slot, links.along_y(k)) for k in (2, 1, 3)]
    shifts = [
        pltpu.make_async_remote_copy(
            src_ref=rows_ref,
            dst_ref=rowso_ref.at[2],
            send_sem=links.send.at[50 + i],
            recv_sem=links.recv.at[50],
            device_id=target,
            device_id_type=MESH,
        )
        for i, target in enumerate(({"x": right}, diagonal[0]))
    ]

    @pl.when(zh == 1)
    def _():
        for copy in shifts:
            copy.start()

    links.keep(wo4_ref, woo_ref.at[c, :, zh])
    links.push(wo4_ref, woo_ref.at[c, :, zh], links.sibling)
    for k, copy in zip((2, 1, 3), tails):
        links.arrived(copy)
        slot = tails_ref.at[c, lax.rem(y + 4 - k, 4)]
        links.push(slot, slot, links.sibling)
    gather.relay()
    links.stored(t_mine)
    links.arrived(t_other)
    links.push(pair.at[1 - c], to_ref.at[c], links.sibling)
    links.keep(pair.at[c], to_ref.at[c])
    links.arrived(wo_own)
    slot = woo_ref.at[c, y, 1 - zh]
    links.keep(mid, slot)
    round_y = [links.push(mid, slot, links.along_y(k)) for k in (2, 1, 3)]
    links.push(mid, slot, links.sibling)
    gather.middle()
    for k, copy in zip((2, 1, 3), round_y):
        links.arrived(copy)
        slot = woo_ref.at[c, lax.rem(y + 4 - k, 4), 1 - zh]
        links.push(slot, slot, links.sibling)
    links.arrived(w_other)
    slot = wq_ref.at[c, 1 - zh]
    links.push(slot, slot, links.sibling)
    gather.last()
    links.finish()
    shifts[0].wait_recv()

    @pl.when(zh == 1)
    def _():
        for copy in shifts:
            copy.wait_send()


def first(normed, out_grad, w, tail, rows, wo4):
    return call(
        first_kernel,
        "first",
        2,
        (normed, out_grad, w, tail, rows, wo4),
        "vhhvvv",
        [
            ("v", (8, TOK, D), BF),
            ("v", (2, TOK, HALF), BF),
            ("v", (2, 2, 3, 136, HALF), BF),
            ("v", (2, 4, 48, HALF), BF),
            ("v", (3, 8, 128), F32),
            ("v", (2, 4, 2, 136, HALF), BF),
        ],
        [pltpu.VMEM((2, TOK, HALF), BF), pltpu.VMEM((136, HALF), BF)],
    )


class WeightBlock:
    def __init__(self, links, w_ref, pair, o_ref):
        self.links, self.pair, self.o = links, pair, o_ref
        self.other = links.push(w_ref.at[links.y], pair.at[links.zh, links.y], links.partner)
        self.kept = links.keep(w_ref, pair.at[links.zh])

    def turn(self):
        links = self.links
        links.arrived(self.other)
        slot = self.pair.at[1 - links.zh, links.y]
        self.round = [links.push(slot, slot, links.along_y(k)) for k in (2, 1, 3)]

    def between_cores(self):
        links = self.links
        links.stored(self.kept)
        for copy in self.round:
            links.arrived(copy)
        links.push(self.pair.at[1 - links.c], self.o.at[links.c], links.sibling)
        links.keep(self.pair.at[links.c], self.o.at[links.c])


QUARTERS = (4, 136, HALF)

BLOCK = 256


def dot(a, b, dims):
    return lax.dot_general(a, b, (dims, ((), ())), preferred_element_type=F32)


def attend_head(qkv_ref, h, m_ref, p_ref):
    keys = lax.broadcasted_iota(jnp.int32, (BLOCK, BLOCK), 0)
    queries = lax.broadcasted_iota(jnp.int32, (BLOCK, BLOCK), 1)
    head = pl.ds(h * HDIM, HDIM)
    for i in range(LEN // BLOCK):
        low, high = i * BLOCK, (i + 1) * BLOCK
        q = qkv_ref[0, head, low:high] * BF(HDIM**-0.5)
        parts = [dot(qkv_ref[1, head, low:high], q, ((0,), (0,)))]
        parts[0] = jnp.where(keys <= queries, parts[0], MASKED)
        if i:
            parts.insert(0, dot(qkv_ref[1, head, :low], q, ((0,), (0,))))
        highest = functools.reduce(jnp.maximum, [jnp.max(s, axis=0, keepdims=True) for s in parts])
        parts = [jnp.exp(s - highest) for s in parts]
        share = 1.0 / sum(jnp.sum(s, axis=0, keepdims=True) for s in parts)
        parts = [(s * share).astype(BF) for s in parts]
        p_ref[h, low:high, low:high] = parts[-1]
        mixed = dot(qkv_ref[2, head, low:high], parts[-1], ((1,), (0,)))
        if i:
            p_ref[h, :low, low:high] = parts[0]
            mixed += dot(qkv_ref[2, head, :low], parts[0], ((1,), (0,)))
        m_ref[head, low:high] = mixed.astype(BF)


def attend_kernel(t_ref, n_ref, wq_ref, tails_ref, bias_ref, up_ref, qkv_ref, w_ref, m_ref, p_ref, f_ref, o_ref, upo_ref, a, room, pair, *sems):
    links = Links(*sems)
    x, c = links.x, links.c
    links.greet(targets(links, "line", "y", "z"))
    for h in range(2):
        a[:, h * HALF : (h + 1) * HALF] = t_ref[h]
    gather = Gather(links, a, o_ref)
    weight = WeightBlock(links, up_ref, pair, upo_ref)
    n = n_ref[...].reshape(LEN, D)
    last = links.rank == 7
    start = pl.multiple_of(48 - 16 * x + 128 * c, 16)
    for k in range(3):
        for h in range(2):
            columns = slice(h * HALF, (h + 1) * HALF)
            rows = [tails_ref[h, k], wq_ref[h, 0, k], wq_ref[h, 1, k], jnp.zeros((48, HALF), BF)]
            room[:, columns] = jnp.concatenate([r.astype(F32) for r in rows], axis=0)
        mine = room[pl.ds(start, SLOT)].astype(BF)
        low = slice(k * SLOT, k * SLOT + 128)
        high = slice(k * SLOT + 128, (k + 1) * SLOT)
        w_ref[low] = mine[:128]
        w_ref[high] = jnp.where(last, mine[128:], BF(0))
        rows = slice(k * SLOT, (k + 1) * SLOT)
        qkv_ref[k] = (dot(w_ref[rows], n, ((1,), (1,))) + bias_ref[rows]).astype(BF)
    gather.relay()
    for h in range(SLOT // HDIM):
        attend_head(qkv_ref, h, m_ref, p_ref)
        if h == 0:
            weight.turn()
        if h == 1:
            gather.middle()
    own = links.rank
    columns = pl.ds(pl.multiple_of(own * TOK, TOK), TOK)
    links.keep(m_ref.at[:, columns], f_ref.at[own])
    for target, rank in links.line():
        columns = pl.ds(pl.multiple_of(rank * TOK, TOK), TOK)
        links.push(m_ref.at[:, columns], f_ref.at[own], target)
    weight.between_cores()
    gather.last()
    links.finish()


def attend(tangent, rows, wq, tails, bias, up):
    return call(
        attend_kernel,
        "attend",
        3,
        (tangent, rows, wq, tails, bias, up),
        "vvvvvh",
        [
            ("v", (3, SLOT, LEN), BF),
            ("v", (3 * SLOT, D), BF),
            ("v", (SLOT, LEN), BF),
            ("v", (SLOT // HDIM, LEN, LEN), BF),
            ("v", (8, SLOT, TOK), BF),
            ("v", (8, TOK, D), BF),
            ("v", (2, *QUARTERS), BF),
        ],
        [pltpu.VMEM((TOK, D), BF), pltpu.VMEM((368, D), F32), pltpu.VMEM((2, *QUARTERS), BF)],
        20,
    )


def second_kernel(f_ref, wo_ref, i_ref, cols_ref, down_ref, o_ref, downo_ref, m_ref, r_ref, cent_ref, inv_ref, n, pair, *sems):
    links = Links(*sems)
    links.greet(targets(links, "x", "y", "c", "z"))
    weight = WeightBlock(links, down_ref, pair, downo_ref)
    for rank in range(7):
        m_ref[128 * rank : 128 * (rank + 1)] = f_ref[rank, :128]
    m_ref[896:] = f_ref[7]
    columns = jnp.concatenate([cols_ref[0], cols_ref[1]], axis=1)
    attended = [dot(m_ref[...], wo_ref[h], ((0,), (0,))) for h in range(2)]
    residual = i_ref[...] + (jnp.concatenate(attended, axis=1) + columns[0:1])
    r_ref[...] = residual + columns[5:6]
    n[...], cent_ref[...], inv_ref[...] = normed(residual, columns[3:4], columns[4:5])
    gather = Gather(links, n, o_ref)
    weight.turn()
    gather.relay()
    gather.middle()
    weight.between_cores()
    gather.last()
    links.finish()


def second(found, wo, inputs, columns, down):
    return call(
        second_kernel,
        "second",
        4,
        (found, wo, inputs, columns, down),
        "vvvvh",
        [
            ("v", (8, TOK, D), BF),
            ("v", (2, *QUARTERS), BF),
            ("v", (D, TOK), BF),
            ("v", (TOK, D), F32),
            ("v", (TOK, D), F32),
            ("v", (TOK, 1), F32),
        ],
        [pltpu.VMEM((TOK, D), BF), pltpu.VMEM((2, *QUARTERS), BF)],
    )


def hidden_kernel(n_ref, t_ref, up_ref, down_ref, b_ref, low_ref, dn_ref, gup_ref, gdown_ref, gb_ref, up, down, up_sum, down_sum):
    step = pl.program_id(0)

    @pl.when(step == 0)
    def _():
        for h in range(2):
            up[:, h * HALF : (h + 1) * HALF] = up_ref[h]
            down[:, h * HALF : (h + 1) * HALF] = down_ref[h]
        up_sum[...] = jnp.zeros_like(up_sum)
        down_sum[...] = jnp.zeros_like(down_sum)
        gb_ref[...] = jnp.zeros_like(gb_ref)

    n = n_ref[...].reshape(BLOCK, D)
    t = t_ref[...].reshape(BLOCK, D)
    pre = dot(n, up[...], ((1,), (1,))) + b_ref[...]
    cumulative = 0.5 * (1.0 + lax.erf(pre * 0.7071067811865476))
    density = jnp.exp(-0.5 * pre * pre) * 0.3989422804014327
    active = (pre * cumulative).astype(BF)
    slope = cumulative + pre * density
    low_ref[...] = dot(active, down[...], ((1,), (0,))).astype(BF).reshape(low_ref.shape)
    d_pre = (dot(t, down[...], ((1,), (1,))) * slope).astype(BF)
    dn_ref[...] = dot(d_pre, up[...], ((1,), (0,))).astype(BF).reshape(dn_ref.shape)
    down_sum[...] += dot(active, t, ((0,), (0,)))
    up_sum[...] += dot(d_pre, n, ((0,), (0,)))
    gb_ref[...] += jnp.sum(d_pre.astype(F32), axis=0, keepdims=True)

    @pl.when(step == pl.num_programs(0) - 1)
    def _():
        for h in range(2):
            for out, total in ((gup_ref, up_sum), (gdown_ref, down_sum)):
                for j in range(8):
                    out[h, j] = pack(total[j * PART : (j + 1) * PART, h * HALF : (h + 1) * HALF]).astype(BF)


def hidden_part(second_rows, tangent_rows, up, down, bias):
    rows = pl.BlockSpec((BLOCK // TOK, TOK, D), lambda i: (i, 0, 0))
    weight = pl.BlockSpec((2, HALF, HALF), lambda i: (0, 0, 0))
    grad = pl.BlockSpec((2, *PIECES), lambda i: (0, 0, 0, 0))
    one = pl.BlockSpec((1, HALF), lambda i: (0, 0))
    return pl.pallas_call(
        hidden_kernel,
        grid=(LEN // BLOCK,),
        in_specs=[rows, rows, weight, weight, one],
        out_specs=(rows, rows, grad, grad, one),
        out_shape=(
            jax.ShapeDtypeStruct((8, TOK, D), BF),
            jax.ShapeDtypeStruct((8, TOK, D), BF),
            jax.ShapeDtypeStruct((2, *PIECES), BF),
            jax.ShapeDtypeStruct((2, *PIECES), BF),
            jax.ShapeDtypeStruct((1, HALF), F32),
        ),
        scratch_shapes=[pltpu.VMEM((HALF, D), BF)] * 2 + [pltpu.VMEM((HALF, D), F32)] * 2,
        compiler_params=pltpu.CompilerParams(vmem_limit_bytes=32 << 20),
        name="hidden_part",
    )(second_rows, tangent_rows, up, down, bias)


def norm_back(upstream, centred, inverse, gain):
    scaled = upstream * gain
    result = inverse * (
        scaled
        - jnp.mean(scaled, axis=1, keepdims=True)
        - centred * jnp.mean(scaled * centred, axis=1, keepdims=True)
    )
    return result, jnp.sum(upstream * centred, axis=0, keepdims=True), jnp.sum(upstream, axis=0, keepdims=True)


def third_kernel(p_ref, g_ref, t_ref, cent_ref, inv_ref, gain_ref, wo_ref, d_ref, a_ref, dm_ref, v_ref, piece_ref, near, out, came, parts, found, *sems):
    links = Links(*sems)
    links.greet(targets(links, "x", "c", "plane"))
    grads = GradScatter(links, parts, found)
    kept, swap = grads.between_cores(links, g_ref, parts)
    scatter = Scatter(links, p_ref, near, out, came)
    links.stored(kept)
    links.arrived(swap)
    grads.start()
    scatter.forward()
    part, gain, shift = norm_back(scatter.total(), cent_ref[...], inv_ref[...], gain_ref[...])
    tangent = jnp.concatenate([t_ref[0], t_ref[1]], axis=1).astype(F32)
    d_residual = tangent + part
    d_ref[...] = d_residual
    rounded = d_residual.astype(BF)
    a_ref[...] = rounded
    d_mixed = [dot(wo_ref[h], rounded[:, h * HALF : (h + 1) * HALF], ((1,), (1,))) for h in range(2)]
    dm_ref[...] = (d_mixed[0] + d_mixed[1]).astype(BF)
    v_ref[0] = jnp.sum(d_residual.astype(BF).astype(F32), axis=0, keepdims=True)
    v_ref[1] = gain
    v_ref[2] = shift
    v_ref[3] = jnp.sum(tangent, axis=0, keepdims=True)
    piece_ref[...] = grads.total()
    links.finish()


def third(d_normed, grad, tangent, centred, inverse, gain, wo):
    return call(
        third_kernel,
        "third",
        5,
        (d_normed, grad, tangent, centred, inverse, gain, wo),
        "vvvvvvv",
        [
            ("v", (TOK, D), F32),
            ("v", (TOK, D), BF),
            ("v", (D, TOK), BF),
            ("v", (4, 1, D), F32),
            ("v", (PACKED, 128), BF),
        ],
        SCATTER_ROOM + GRADS_ROOM,
        16,
    )


def attend_back_head(qkv_ref, h, u_ref, p_ref, d_ref, dk_sum, dv_sum):
    head = pl.ds(h * HDIM, HDIM)
    for i in range(LEN // BLOCK):
        low, high = i * BLOCK, (i + 1) * BLOCK
        q = qkv_ref[0, head, low:high] * BF(HDIM**-0.5)
        u = u_ref[head, low:high]
        p = p_ref[h, :high, low:high]
        wide = p.astype(F32)
        dp = dot(qkv_ref[2, head, :high], u, ((0,), (0,)))
        centre = jnp.sum(wide * dp, axis=0, keepdims=True)
        ds = (wide * (dp - centre)).astype(BF)
        d_ref[head, low:high] = (dot(qkv_ref[1, head, :high], ds, ((1,), (0,))) * HDIM**-0.5).astype(BF)
        dk = dot(q, ds, ((1,), (1,)))
        dv = dot(u, p, ((1,), (1,)))
        if i:
            dk_sum[:, :low] += dk[:, :low]
            dv_sum[:, :low] += dv[:, :low]
        dk_sum[:, low:high] = dk[:, low:]
        dv_sum[:, low:high] = dv[:, low:]
    d_ref[pl.ds(SLOT + h * HDIM, HDIM)] = dk_sum[...].astype(BF)
    d_ref[pl.ds(2 * SLOT + h * HDIM, HDIM)] = dv_sum[...].astype(BF)


def back_kernel(m_ref, a_ref, qkv_ref, p_ref, g_ref, mixed_ref, n_ref, w_ref, down_ref, piece_ref, dn_ref, chip_ref, tail_ref, b_ref, gdown_ref, u, d, dk_sum, dv_sum, o, own_grads, parts, found, *sems):
    links = Links(*sems)
    c = links.c
    links.greet(targets(links, "line", "plane"))
    own = links.rank
    columns = pl.ds(pl.multiple_of(own * TOK, TOK), TOK)

    def rows(rank):
        return pl.ds(pl.multiple_of(rank * 2 * HDIM, 2 * HDIM), SLOT)

    mine = links.keep(m_ref.at[rows(own)], u.at[:, columns])
    others = [links.push(m_ref.at[rows(rank)], u.at[:, columns], target) for target, rank in links.line()]
    gather = Gather(links, a_ref, o)
    grads = GradScatter(links, parts, found)
    kept, swap = grads.between_cores(links, g_ref, parts)
    links.stored(kept)
    links.arrived(swap)
    grads.start()
    spread_grads(links, down_ref, gdown_ref)
    links.stored(mine)
    for copy in others:
        links.arrived(copy)
    n = n_ref[...].reshape(LEN, D)

    def weight_grad(left, right, k, rows):
        grad = dot(left, right, ((1,), (0,)))
        for h in range(2):
            own_grads[h, k, rows] = grad[:, h * HALF : (h + 1) * HALF].astype(BF)

    def between_cores(which):
        links.keep(own_grads.at[(c, *which)], chip_ref.at[(c, *which)])
        return len(links.kept) - 1, links.push(own_grads.at[(1 - c, *which)], chip_ref.at[(c, *which)], links.sibling)

    def done(copies):
        links.stored(copies[0])
        links.arrived(copies[1])

    attend_back_head(qkv_ref, 0, u, p_ref, d, dk_sum, dv_sum)
    gather.relay()
    for k in range(3):
        weight_grad(d[k * SLOT : k * SLOT + HDIM], n, k, slice(0, HDIM))
    first_rows = between_cores((pl.ds(0, 3), pl.ds(0, HDIM)))
    attend_back_head(qkv_ref, 1, u, p_ref, d, dk_sum, dv_sum)
    done(first_rows)
    links.push(chip_ref.at[0, pl.ds(0, 3), pl.ds(0, HDIM)], tail_ref.at[pl.ds(0, 3)], links.along_x(3))
    gather.middle()
    attend_back_head(qkv_ref, 2, u, p_ref, d, dk_sum, dv_sum)
    gather.last()
    for k in range(3):
        weight_grad(d[k * SLOT + HDIM : (k + 1) * SLOT], n, k, slice(HDIM, SLOT))
    between_cores((pl.ds(0, 3), pl.ds(HDIM, SLOT - HDIM)))
    gather.complete()
    weight_grad(mixed_ref[...], o[...].reshape(LEN, D), 3, slice(0, SLOT))
    out_rows = between_cores((3,))
    for i in range(LEN // BLOCK):
        block = dot(d[:, i * BLOCK : (i + 1) * BLOCK], w_ref[...], ((0,), (0,))).astype(BF)
        dn_ref[2 * i : 2 * i + 2] = block.reshape(2, TOK, D)
        if i == 0:
            done(out_rows)
            links.push(chip_ref.at[0, 3, pl.ds(0, HDIM)], tail_ref.at[3], links.along_x(3))
    b_ref[...] = jnp.sum(d[...].astype(F32), axis=1, keepdims=True)
    piece_ref[...] = grads.total()
    links.finish()


def back(d_mixed, d_attended, qkv, probs, grad, mixed, rows, weight, down_piece):
    return call(
        back_kernel,
        "back",
        6,
        (d_mixed, d_attended, qkv, probs, grad, mixed, rows, weight, down_piece),
        "vvvvvvvvv",
        [
            ("v", (PACKED, 128), BF),
            ("v", (8, TOK, D), BF),
            ("v", (2, 4, SLOT, HALF), BF),
            ("v", (4, HDIM, HALF), BF),
            ("v", (3 * SLOT, 1), F32),
            ("v", PIECES, BF),
        ],
        [pltpu.VMEM((SLOT, LEN), BF), pltpu.VMEM((3 * SLOT, LEN), BF)]
        + [pltpu.VMEM((HDIM, LEN), F32)] * 2
        + [pltpu.VMEM((8, TOK, D), BF), pltpu.VMEM((2, 4, SLOT, HALF), BF)]
        + GRADS_ROOM,
        24,
    )


def fourth_kernel(p_ref, chip, tail, r_ref, cent_ref, inv_ref, gain_ref, gdown_ref, i_ref, v_ref, piece_ref, fdown_ref, near, out, came, whole, exact, parts, found, *sems):
    links = Links(*sems)
    x = links.x
    links.greet(targets(links, "x", "c", "plane"))
    scatter = Scatter(links, p_ref, near, out, came)
    whole[:, pl.ds(0, 128)] = chip[0, :, pl.ds(0, 128)]
    whole[:, pl.ds(128, 128)] = chip[1, :, pl.ds(0, 128)]
    whole[:, pl.ds(256, 64)] = jnp.where(x == 3, chip[1, :, pl.ds(128, 64)], tail[...])
    links.stored(links.keep(whole.at[:, pl.ds(pl.multiple_of(16 * x, 16), 272)], exact))
    for k in range(4):
        rows = exact[k].astype(F32)
        for j in range(4):
            parts[j // 2, 2 * k + j % 2] = pack(rows[j * PART : (j + 1) * PART]).astype(BF)
    grads = GradScatter(links, parts, found)
    grads.start()
    scatter.forward()
    unpack(gdown_ref, fdown_ref)
    part, gain, shift = norm_back(scatter.total(), cent_ref[...], inv_ref[...], gain_ref[...])
    result = (r_ref[...] + part).astype(BF)
    i_ref[0] = result[:, :HALF]
    i_ref[1] = result[:, HALF:]
    v_ref[0] = gain
    v_ref[1] = shift
    piece_ref[...] = grads.total()
    links.finish()


def fourth(d_normed, chip, tail, residual, centred, inverse, gain, down_grad):
    return call(
        fourth_kernel,
        "fourth",
        7,
        (d_normed, chip, tail, residual, centred, inverse, gain, down_grad),
        "vvvvvvvv",
        [
            ("v", (2, TOK, HALF), BF),
            ("v", (2, 1, D), F32),
            ("v", (PACKED, 128), BF),
            ("v", (HALF, HALF), F32),
        ],
        SCATTER_ROOM + [pltpu.VMEM((4, 320, HALF), BF), pltpu.VMEM((4, 272, HALF), BF)] + GRADS_ROOM,
        16,
    )


WIDE = 1792


def leave_kernel(p_ref, r_ref, i_ref, g_ref, v2_ref, v1_ref, vb_ref, b_ref, gup_ref, oo_ref, io_ref, go_ref, vo_ref, fup_ref, near, out, came, found, found_up, halves_o, pair_o, pair_i, v_all, v_line, v_own, v_plane, v_sum, *sems):
    links = Links(*sems)
    y, zh, zl, c = links.y, links.zh, links.zl, links.c
    links.greet(targets(links, "line", "plane"))
    scatter = Scatter(links, p_ref, near, out, came)
    v_all[0] = v2_ref[0]
    v_all[1:3] = v1_ref[...]
    v_all[3:6] = v2_ref[1:4]
    v_all[6:8] = vb_ref[...]
    line = [links.push(v_all.at[rank], v_line.at[n], target) for n, (target, rank) in enumerate(links.line())]

    def between_cores(src, pair):
        return links.keep(src.at[c], pair.at[c]), links.push(src.at[1 - c], pair.at[c], links.sibling)

    def to_partner(pair, dst, copies):
        links.stored(copies[0])
        links.arrived(copies[1])
        links.push(pair.at[1 - zh], dst.at[zh], links.partner)
        links.keep(pair.at[zh], dst.at[zh])

    copies = between_cores(i_ref, pair_i)
    scatter.forward()
    to_partner(pair_i, io_ref, copies)
    total = v_all[links.rank]
    for n, copy in enumerate(line):
        links.arrived(copy)
        total += v_line[n]
    v_own[...] = jnp.zeros_like(v_own)
    v_own[:, :D] = total
    v_own[:, 1152 : 1152 + HALF] = b_ref[...]
    place = (2 * zh + zl) * 4 + y
    kept = links.keep(v_own, v_plane.at[place])
    plane = [links.push(v_own, v_plane.at[place], target) for target, _, _ in links.plane()]
    up_grads = spread_grads(links, gup_ref, found_up)
    grads = spread_grads(links, g_ref, found)
    links.stored(kept)
    for copy in plane:
        links.arrived(copy)
    total = v_plane[0]
    for n in range(1, 16):
        total += v_plane[n]
    v_sum[...] = total
    links.keep(v_sum, vo_ref.at[links.rank])
    for target, _ in links.line():
        links.push(v_sum, vo_ref.at[links.rank], target)
    result = (scatter.total() + r_ref[...]).astype(BF)
    halves_o[0] = result[:, :HALF]
    halves_o[1] = result[:, HALF:]
    to_partner(pair_o, oo_ref, between_cores(halves_o, pair_o))
    spread_done(links, up_grads)
    unpack(found_up, fup_ref)
    spread_done(links, grads)
    unpack(found, go_ref)
    links.finish()


def leave(lowered, residual, in_grad, piece, *vectors, up_piece):
    pair = pltpu.VMEM((2, TOK, HALF), BF)
    return call(
        leave_kernel,
        "leave",
        8,
        (lowered, residual, in_grad, piece, *vectors, up_piece),
        "vvvvvvvvv",
        [
            ("v", (2, TOK, HALF), BF),
            ("v", (2, TOK, HALF), BF),
            ("v", (HALF, HALF), F32),
            ("v", (8, 1, WIDE), F32),
            ("v", (HALF, HALF), F32),
        ],
        SCATTER_ROOM
        + [pltpu.VMEM(PIECES, BF), pltpu.VMEM(PIECES, BF), pair, pair, pair]
        + [pltpu.VMEM((8, 1, D), F32), pltpu.VMEM((7, 1, D), F32), pltpu.VMEM((1, WIDE), F32)]
        + [pltpu.VMEM((16, 1, WIDE), F32), pltpu.VMEM((1, WIDE), F32)],
        16,
    )


def per_device(
    block_in,
    query_key_value_weight,
    bias_qv,
    output_weight,
    bias_out,
    gain_one,
    shift_one,
    gain_two,
    shift_two,
    up_weight,
    bias_up,
    down_weight,
    bias_down,
    out_grad,
):
    x, zh, c = (lax.axis_index(a) for a in ("x", "zh", "c"))
    rank = 2 * x + c
    last = rank == 7
    real = jnp.logical_or(jnp.arange(SLOT) < 128, last)

    columns = [a[None] for a in (bias_out, gain_one, shift_one, gain_two, shift_two, bias_down)]
    tail = jnp.pad(query_key_value_weight[:, 88:], ((0, 1), (0, 0), (0, 0)))
    wo4, columns, tail, inputs, normed_one, centred_one, inverse_one = enter(block_in, output_weight, tail, columns)
    rows = jnp.concatenate([bias_qv.reshape(-1), bias_up, jnp.zeros((208,), F32)]).reshape(8, 128)
    first_rows, tangent, wq, tails, rows, wo = first(
        normed_one, out_grad, query_key_value_weight, tail, rows, wo4
    )
    rows = rows.reshape(3, 1024)
    bias_up = lax.dynamic_slice(rows, (c, 272), (1, HALF))
    qv = rows[:, :272].reshape(3, 2, 136)
    qv = jnp.concatenate([qv[2, :, 88:], qv[0], qv[1], jnp.zeros((2, 48), F32)], axis=1)
    qv = lax.dynamic_slice_in_dim(qv, 48 - 16 * x + 128 * c, SLOT, 1)
    qv = jnp.where(real[None], qv, 0.0)
    bias_qkv = jnp.concatenate([qv[0], jnp.zeros_like(qv[0]), qv[1]])[:, None]

    qkv, weight_qkv, mixed, probs, found, tangent_rows, up = attend(
        tangent, first_rows, wq, tails, bias_qkv, up_weight.reshape(QUARTERS)
    )
    wo = wo.reshape(2, D, HALF)

    second_rows, down, _, residual, centred_two, inverse_two = second(
        found, wo, inputs, columns, down_weight.reshape(QUARTERS)
    )
    lowered, d_normed_two, up_grad, down_grad, grad_bias_up = hidden_part(
        second_rows,
        tangent_rows,
        up.reshape(2, HALF, HALF),
        down.reshape(2, HALF, HALF),
        bias_up,
    )
    gains = jnp.concatenate([columns[0], columns[1]], axis=1)
    d_residual, d_attended, d_mixed, sums_two, down_piece = third(
        d_normed_two, down_grad, tangent, centred_two, inverse_two, gains[3:4], wo
    )

    up_piece, d_normed_one, chip, tail, bias_sums, down_grad = back(
        d_mixed, d_attended, qkv, probs, up_grad, mixed, first_rows, weight_qkv, down_piece
    )
    in_grad, sums_one, piece, down_grad = fourth(
        d_normed_one, chip, tail, d_residual, centred_one, inverse_one, gains[1:2], down_grad
    )

    bias_sums = bias_sums.reshape(3, SLOT)
    bias_sums = jnp.where(real[None], jnp.stack([bias_sums[0], bias_sums[2]]), 0.0)
    wide = lax.dynamic_update_slice(jnp.zeros((2, D), F32), bias_sums, (0, 128 * rank))
    block_out, in_grad, grads, vectors, up_grad = leave(
        lowered, residual, in_grad, piece, sums_two, sums_one, wide[:, None], grad_bias_up, up_piece=up_piece
    )
    grads = grads.reshape(4, 136, HALF)
    row = 2 * x + zh
    vectors = vectors[:, 0]
    grad_bias_up = lax.dynamic_index_in_dim(vectors, row, 0, keepdims=False)[1152 : 1152 + HALF]
    six = lax.dynamic_slice_in_dim(vectors[:6], HALF * c, HALF, 1)
    grad_bias_out, grad_gain_one, grad_shift_one, grad_gain_two, grad_shift_two, grad_bias_down = six
    grad_bias_qv = lax.dynamic_slice_in_dim(vectors[6:], 136 * row, 136, 1)

    return (
        block_out,
        in_grad.astype(F32),
        grads[:3],
        grad_bias_qv,
        grads[3],
        grad_bias_out,
        grad_gain_one,
        grad_shift_one,
        grad_gain_two,
        grad_shift_two,
        up_grad,
        grad_bias_up,
        down_grad,
        grad_bias_down,
    )


def solution(mesh):
    finer = Mesh(mesh.devices.reshape(2, 4, 4, 2, 2), ALL)
    return jax.shard_map(
        per_device,
        mesh=finer,
        in_specs=(
            P(DP, ROW, "c"),
            P(None, ROW, "c"),
            P(None, ROW),
            P(ROW, "c"),
            P("c"),
            P("c"),
            P("c"),
            P("c"),
            P("c"),
            P(ROW, "c"),
            P(ROW),
            P(ROW, "c"),
            P("c"),
            P(DP, ROW, "c"),
        ),
        out_specs=(
            P(DP, ROW, "c"),
            P(DP, ROW, "c"),
            P(None, ROW, "c"),
            P(None, ROW),
            P(ROW, "c"),
            P("c"),
            P("c"),
            P("c"),
            P("c"),
            P("c"),
            P(ROW, "c"),
            P(ROW),
            P(ROW, "c"),
            P("c"),
        ),
        check_vma=False,
    )
```

```python
import functools

import jax
import jax.numpy as jnp
from jax import lax
from jax.experimental import pallas as pl
from jax.experimental.pallas import tpu as pltpu
from jax.sharding import Mesh
from jax.sharding import PartitionSpec as P


HDIM = 64
D = 1088
HALF = D // 2
TOK = 128
LEN = 1024
SLOT = 192
EPSILON = 1e-05
MASKED = -1e30
DP = ("zl", "y")
ROW = ("x", "zh")
ALL = ("zl", "y", "x", "zh", "c")
MESH = pl.DeviceIdType.MESH
PART = 68
BF = jnp.bfloat16
F32 = jnp.float32


class Links:
    def __init__(self, send, recv, local):
        self.send, self.recv, self.local = send, recv, local
        self.pushed, self.kept = [], []
        self.x, self.c, self.y = lax.axis_index("x"), lax.axis_index("c"), lax.axis_index("y")
        self.zh, self.zl = lax.axis_index("zh"), lax.axis_index("zl")
        self.rank = 2 * self.x + self.c
        self.sibling = {"c": 1 - self.c}
        self.partner = {"zh": 1 - self.zh}

    def along_x(self, k):
        return {"x": lax.rem(self.x + k, 4)}

    def along_y(self, k):
        return {"y": lax.rem(self.y + k, 4)}

    def line(self):
        found = []
        for k, j in ((2, 0), (2, 1), (1, 0), (1, 1), (3, 0), (3, 1), (0, 1)):
            found.append((lax.rem(self.x + k, 4), lax.rem(self.c + j, 2)))
        return [({"x": x, "c": c}, 2 * x + c) for x, c in found]

    def plane(self, both=True):
        found = []
        for h in (1, 0) if both else (0,):
            for l in (1, 0):
                for k in (2, 1, 3, 0):
                    if h or l or k:
                        y, zl = lax.rem(self.y + k, 4), lax.rem(self.zl + l, 2)
                        zh = lax.rem(self.zh + h, 2)
                        found.append(({"y": y, "zl": zl, "zh": zh}, zh, 2 * y + zl))
        return found

    def greet(self, targets):
        barrier = pltpu.get_barrier_semaphore()
        for target in targets:
            pl.semaphore_signal(barrier, inc=1, device_id=target, device_id_type=MESH)
        pl.semaphore_wait(barrier, len(targets))

    def push(self, src, dst, target):
        n = len(self.pushed)
        copy = pltpu.make_async_remote_copy(
            src_ref=src,
            dst_ref=dst,
            send_sem=self.send.at[n],
            recv_sem=self.recv.at[n],
            device_id=target,
            device_id_type=MESH,
        )
        copy.start()
        self.pushed.append([copy, False])
        return n

    def arrived(self, n):
        if not self.pushed[n][1]:
            self.pushed[n][0].wait_recv()
            self.pushed[n][1] = True

    def keep(self, src, dst):
        n = len(self.kept)
        copy = pltpu.make_async_copy(src, dst, self.local.at[n])
        copy.start()
        self.kept.append([copy, False])
        return n

    def stored(self, n):
        if not self.kept[n][1]:
            self.kept[n][0].wait()
            self.kept[n][1] = True

    def finish(self):
        for n in range(len(self.kept)):
            self.stored(n)
        for n in range(len(self.pushed)):
            self.arrived(n)
        for copy, _ in self.pushed:
            copy.wait_send()


SEMS = [pltpu.SemaphoreType.DMA((64,)), pltpu.SemaphoreType.DMA((64,)), pltpu.SemaphoreType.DMA((32,))]
SPACES = {"v": pltpu.VMEM, "h": pl.ANY}


def call(kernel, name, cid, args, spaces, outs, scratch=(), mib=12):
    return pl.pallas_call(
        kernel,
        out_shape=tuple(jax.ShapeDtypeStruct(shape, dtype) for _, shape, dtype in outs),
        in_specs=[pl.BlockSpec(memory_space=SPACES[s]) for s in spaces],
        out_specs=tuple(pl.BlockSpec(memory_space=SPACES[s]) for s, _, _ in outs),
        scratch_shapes=[*scratch, *SEMS],
        compiler_params=pltpu.CompilerParams(
            collective_id=cid, has_side_effects=True, vmem_limit_bytes=mib << 20
        ),
        name=name,
    )(*args)


def top(ref):
    return ref.at[pl.ds(0, TOK // 2)]


def bottom(ref):
    return ref.at[pl.ds(TOK // 2, TOK // 2)]


class Gather:
    def __init__(self, links, a_ref, o_ref):
        self.links, self.o = links, o_ref
        own = o_ref.at[links.rank]
        self.kept = links.keep(a_ref, own)
        right, left = links.along_x(1), links.along_x(3)
        self.ahead = [links.push(top(a_ref), top(own), right)]
        self.back = [links.push(bottom(a_ref), bottom(own), left)]
        self.ahead.append(links.push(bottom(a_ref), bottom(own), right))
        self.back.append(links.push(top(a_ref), top(own), left))
        self.near = [links.push(a_ref, own, links.sibling)]

    def slot(self, k):
        return self.o.at[2 * lax.rem(self.links.x + 4 - k, 4) + self.links.c]

    def share(self, piece):
        self.near.append(self.links.push(piece, piece, self.links.sibling))

    def relay(self):
        links = self.links
        links.arrived(self.ahead[0])
        self.far = [links.push(top(self.slot(1)), top(self.slot(1)), links.along_x(1))]
        links.arrived(self.back[0])
        self.far.append(links.push(bottom(self.slot(3)), bottom(self.slot(3)), links.along_x(3)))
        self.share(top(self.slot(1)))
        self.share(bottom(self.slot(3)))

    def middle(self):
        links = self.links
        links.arrived(self.ahead[1])
        self.share(bottom(self.slot(1)))
        links.arrived(self.back[1])
        self.share(top(self.slot(3)))

    def last(self):
        links = self.links
        links.arrived(self.far[0])
        self.share(top(self.slot(2)))
        links.arrived(self.far[1])
        self.share(bottom(self.slot(2)))

    def complete(self):
        self.links.stored(self.kept)
        for copy in self.near:
            self.links.arrived(copy)


class Scatter:
    def __init__(self, links, p_ref, near, out, came):
        self.links, self.p, self.near, self.out, self.came = links, p_ref, near, out, came
        self.swaps = {}
        for k in (2, 1, 3, 0):
            to = lax.rem(links.x + k, 4)
            self.swaps[k] = links.push(p_ref.at[2 * to + 1 - links.c], near.at[k], links.sibling)

    def both(self, k):
        links = self.links
        links.arrived(self.swaps[k])
        to = lax.rem(links.x + k, 4)
        return self.p[2 * to + links.c].astype(F32) + self.near[k].astype(F32)

    def forward(self):
        links, out, came = self.links, self.out, self.came
        right, left = links.along_x(1), links.along_x(3)
        out[2] = self.both(2).astype(BF)
        ahead = links.push(top(out.at[2]), top(came.at[2]), right)
        back = links.push(bottom(out.at[2]), bottom(came.at[2]), left)
        half = TOK // 2
        one = self.both(1)
        out[1, half:] = one[half:].astype(BF)
        self.sends = [links.push(bottom(out.at[1]), bottom(came.at[1]), right)]
        three = self.both(3)
        out[3, :half] = three[:half].astype(BF)
        self.sends.append(links.push(top(out.at[3]), top(came.at[3]), left))
        links.arrived(ahead)
        out[1, :half] = (one[:half] + came[2, :half].astype(F32)).astype(BF)
        self.sends.append(links.push(top(out.at[1]), top(came.at[1]), right))
        links.arrived(back)
        out[3, half:] = (three[half:] + came[2, half:].astype(F32)).astype(BF)
        self.sends.append(links.push(bottom(out.at[3]), bottom(came.at[3]), left))

    def total(self):
        total = self.both(0)
        for copy in self.sends:
            self.links.arrived(copy)
        return total + self.came[1].astype(F32) + self.came[3].astype(F32)


SCATTER_ROOM = [pltpu.VMEM((4, TOK, D), BF)] * 3
PACKED = PART * HALF // 128
PIECES = (8, PACKED, 128)
GRADS_ROOM = [pltpu.VMEM((2, *PIECES), BF), pltpu.VMEM((16, PACKED, 128), BF)]


def pack(rows):
    tiles = [rows[:, 128 * t : 128 * (t + 1)] for t in range(4)]
    rest = jnp.concatenate([rows[17 * q : 17 * (q + 1), 512:] for q in range(4)], axis=1)
    return jnp.concatenate([*tiles, rest], axis=0)


def unpack(piece):
    tiles = [piece[PART * t : PART * (t + 1)] for t in range(4)]
    rest = [piece[4 * PART :, 32 * q : 32 * (q + 1)] for q in range(4)]
    return jnp.concatenate([*tiles, jnp.concatenate(rest, axis=0)], axis=1)


class GradScatter:
    def __init__(self, links, parts, came):
        self.links, self.parts, self.came = links, parts, came

    @staticmethod
    def between_cores(links, own, parts):
        kept = links.keep(own.at[links.c], parts.at[links.c])
        swap = links.push(own.at[1 - links.c], parts.at[links.c], links.sibling)
        return kept, swap

    def start(self):
        self.sends = [
            self.links.push(self.parts.at[zh, piece], self.came.at[n + 1], target)
            for n, (target, zh, piece) in enumerate(self.links.plane())
        ]

    def total(self):
        links = self.links
        total = self.parts[links.zh, 2 * links.y + links.zl].astype(F32)
        for n, send in enumerate(self.sends):
            links.arrived(send)
            total += self.came[n + 1].astype(F32)
        return total.astype(BF)


class Spread:
    def __init__(self, links, piece_ref, o_ref):
        self.links, self.o = links, o_ref
        slot = o_ref.at[2 * links.y + links.zl]
        self.other = links.push(piece_ref, slot, {"zl": 1 - links.zl})
        self.kept = links.keep(piece_ref, slot)
        self.copies = [links.push(piece_ref, slot, links.along_y(k)) for k in (2, 1, 3)]

    def turn(self):
        links = self.links
        links.arrived(self.other)
        slot = self.o.at[2 * links.y + 1 - links.zl]
        self.copies += [links.push(slot, slot, links.along_y(k)) for k in (2, 1, 3)]


def targets(links, *groups):
    found = []
    for group in groups:
        if group == "x":
            found += [links.along_x(k) for k in (1, 2, 3)]
        if group == "y":
            found += [links.along_y(k) for k in (1, 2, 3)]
        if group == "c":
            found.append(links.sibling)
        if group == "z":
            found.append(links.partner)
        if group == "line":
            found += [target for target, _ in links.line()]
        if group == "plane":
            found += [target for target, _, _ in links.plane()]
    return found


def normed(values, gain, shift):
    centre = jnp.mean(values, axis=1, keepdims=True)
    second_moment = jnp.mean(values * values, axis=1, keepdims=True)
    inverse = lax.rsqrt(second_moment - centre * centre + EPSILON)
    centred = (values - centre) * inverse
    return (centred * gain + shift).astype(BF), centred, inverse


def enter_kernel(a_ref, t_ref, wo_ref, w_ref, b0, b1, b2, b3, b4, b5, wo4_ref, colso_ref, tailo_ref, i_ref, n_ref, cent_ref, inv_ref, t32_ref, pair, tpair, tok, ttok, cols, tail, *sems):
    links = Links(*sems)
    x, y, zh, c = links.x, links.y, links.zh, links.c
    right, left = lax.rem(x + 1, 4), lax.rem(x + 3, 4)
    diagonal = [{"x": right, "zh": 1 - zh}, {"x": left, "zh": 1 - zh}]
    links.greet(targets(links, "x", "c", "z") + diagonal)
    other = links.push(a_ref.at[1 - zh], pair.at[zh], links.partner)
    mine = links.keep(a_ref.at[zh], pair.at[zh])
    t_other = links.push(t_ref.at[1 - zh], tpair.at[zh], links.partner)
    t_mine = links.keep(t_ref.at[zh], tpair.at[zh])
    cols[...] = jnp.concatenate([b[...].reshape(1, HALF) for b in (b0, b1, b2, b3, b4, b5, b5, b5)], axis=0)
    swap = links.push(cols, colso_ref.at[c], links.sibling)
    own = links.keep(cols, colso_ref.at[c])
    for k in (2, 1, 3):
        links.push(wo_ref, wo4_ref.at[x], links.along_x(k))
    links.keep(wo_ref, wo4_ref.at[x])
    tail[...] = w_ref[jnp.minimum(y, 2), 88:]
    shifts = [
        pltpu.make_async_remote_copy(
            src_ref=tail,
            dst_ref=tailo_ref,
            send_sem=links.send.at[50 + i],
            recv_sem=links.recv.at[50],
            device_id=target,
            device_id_type=MESH,
        )
        for i, target in enumerate(({"x": right}, diagonal[0]))
    ]

    @pl.when(zh == 1)
    def _():
        for copy in shifts:
            copy.start()

    links.stored(mine)
    links.arrived(other)
    got = links.push(pair.at[1 - c], tok.at[c], links.sibling)
    kept = links.keep(pair.at[c], tok.at[c])
    links.stored(t_mine)
    links.arrived(t_other)
    t_got = links.push(tpair.at[1 - c], ttok.at[c], links.sibling)
    t_kept = links.keep(tpair.at[c], ttok.at[c])
    links.arrived(swap)
    links.stored(own)
    links.stored(kept)
    links.arrived(got)

    def whole(halves):
        return jnp.concatenate([halves[0].astype(F32), halves[1].astype(F32)], axis=0).T

    values = whole(tok)
    i_ref[...] = values
    gains = jnp.concatenate([colso_ref[0], colso_ref[1]], axis=1)
    n_ref[...], cent_ref[...], inv_ref[...] = normed(values, gains[1:2], gains[2:3])
    links.stored(t_kept)
    links.arrived(t_got)
    t32_ref[...] = whole(ttok).astype(BF)
    links.finish()
    shifts[0].wait_recv()

    @pl.when(zh == 1)
    def _():
        for copy in shifts:
            copy.wait_send()


def enter(block_in, out_grad, output_weight, w, columns):
    halves = pltpu.VMEM((2, HALF, TOK), BF)
    return call(
        enter_kernel,
        "enter",
        1,
        (block_in, out_grad, output_weight, w, *columns),
        "hhhvvvvvvv",
        [
            ("v", (4, 136, HALF), BF),
            ("v", (2, 8, HALF), F32),
            ("v", (48, HALF), BF),
            ("v", (TOK, D), F32),
            ("v", (TOK, D), BF),
            ("v", (TOK, D), F32),
            ("v", (TOK, 1), F32),
            ("v", (TOK, D), BF),
        ],
        [halves] * 4 + [pltpu.VMEM((8, HALF), F32), pltpu.VMEM((48, HALF), BF)],
    )


def first_kernel(n_ref, w_ref, tail_ref, qv_ref, up_ref, wo4_ref, o_ref, wq_ref, tails_ref, qvo_ref, b_ref, woo_ref, mid, ups, *sems):
    links = Links(*sems)
    x, y, zh, c = links.x, links.y, links.zh, links.c
    right, left = lax.rem(x + 1, 4), lax.rem(x + 3, 4)
    diagonal = [{"x": right, "zh": 1 - zh}, {"x": left, "zh": 1 - zh}]
    links.greet(targets(links, "x", "y", "c", "z") + diagonal)
    gather = Gather(links, n_ref, o_ref)
    wo_own = links.push(wo4_ref.at[y], mid, links.partner)
    w_other = links.push(w_ref, wq_ref.at[c, zh], links.partner)
    links.keep(w_ref, wq_ref.at[c, zh])
    links.push(w_ref, wq_ref.at[c, zh], links.sibling)
    links.push(qv_ref, qvo_ref.at[zh], links.partner)
    links.keep(qv_ref, qvo_ref.at[zh])
    up_other = links.push(up_ref, ups.at[zh], links.partner)
    up_mine = links.keep(up_ref, ups.at[zh])
    slot = tails_ref.at[c, y]
    links.keep(tail_ref, slot)
    links.push(tail_ref, slot, links.sibling)
    tails = [links.push(tail_ref, slot, links.along_y(k)) for k in (2, 1, 3)]
    shifts = [
        pltpu.make_async_remote_copy(
            src_ref=qv_ref,
            dst_ref=qvo_ref.at[2],
            send_sem=links.send.at[50 + i],
            recv_sem=links.recv.at[50],
            device_id=target,
            device_id_type=MESH,
        )
        for i, target in enumerate(({"x": right}, diagonal[0]))
    ]

    @pl.when(zh == 1)
    def _():
        for copy in shifts:
            copy.start()

    links.keep(wo4_ref, woo_ref.at[c, :, zh])
    links.push(wo4_ref, woo_ref.at[c, :, zh], links.sibling)
    for k, copy in zip((2, 1, 3), tails):
        links.arrived(copy)
        slot = tails_ref.at[c, lax.rem(y + 4 - k, 4)]
        links.push(slot, slot, links.sibling)
    gather.relay()
    links.stored(up_mine)
    links.arrived(up_other)
    b_ref[...] = ups[c]
    links.arrived(wo_own)
    slot = woo_ref.at[c, y, 1 - zh]
    links.keep(mid, slot)
    round_y = [links.push(mid, slot, links.along_y(k)) for k in (2, 1, 3)]
    links.push(mid, slot, links.sibling)
    gather.middle()
    for k, copy in zip((2, 1, 3), round_y):
        links.arrived(copy)
        slot = woo_ref.at[c, lax.rem(y + 4 - k, 4), 1 - zh]
        links.push(slot, slot, links.sibling)
    links.arrived(w_other)
    slot = wq_ref.at[c, 1 - zh]
    links.push(slot, slot, links.sibling)
    gather.last()
    links.finish()
    shifts[0].wait_recv()

    @pl.when(zh == 1)
    def _():
        for copy in shifts:
            copy.wait_send()


def first(normed, w, tail, qv, up, wo4):
    return call(
        first_kernel,
        "first",
        2,
        (normed, w, tail, qv, up, wo4),
        "vhvvvv",
        [
            ("v", (8, TOK, D), BF),
            ("v", (2, 2, 3, 136, HALF), BF),
            ("v", (2, 4, 48, HALF), BF),
            ("v", (3, 2, 136), F32),
            ("v", (1, HALF), F32),
            ("v", (2, 4, 2, 136, HALF), BF),
        ],
        [pltpu.VMEM((136, HALF), BF), pltpu.VMEM((2, 1, HALF), F32)],
    )


class WeightBlock:
    def __init__(self, links, w_ref, pair, o_ref):
        self.links, self.pair, self.o = links, pair, o_ref
        self.other = links.push(w_ref.at[links.y], pair.at[links.zh, links.y], links.partner)
        self.kept = links.keep(w_ref, pair.at[links.zh])

    def turn(self):
        links = self.links
        links.arrived(self.other)
        slot = self.pair.at[1 - links.zh, links.y]
        self.round = [links.push(slot, slot, links.along_y(k)) for k in (2, 1, 3)]

    def between_cores(self):
        links = self.links
        links.stored(self.kept)
        for copy in self.round:
            links.arrived(copy)
        links.push(self.pair.at[1 - links.c], self.o.at[links.c], links.sibling)
        links.keep(self.pair.at[links.c], self.o.at[links.c])


QUARTERS = (4, 136, HALF)

BLOCK = 256


def dot(a, b, dims):
    return lax.dot_general(a, b, (dims, ((), ())), preferred_element_type=F32)


def attend_head(qkv_ref, h, m_ref, p_ref):
    keys = lax.broadcasted_iota(jnp.int32, (BLOCK, BLOCK), 0)
    queries = lax.broadcasted_iota(jnp.int32, (BLOCK, BLOCK), 1)
    head = pl.ds(h * HDIM, HDIM)
    for i in range(LEN // BLOCK):
        low, high = i * BLOCK, (i + 1) * BLOCK
        q = qkv_ref[0, head, low:high] * BF(HDIM**-0.5)
        parts = [dot(qkv_ref[1, head, low:high], q, ((0,), (0,)))]
        parts[0] = jnp.where(keys <= queries, parts[0], MASKED)
        if i:
            parts.insert(0, dot(qkv_ref[1, head, :low], q, ((0,), (0,))))
        highest = functools.reduce(jnp.maximum, [jnp.max(s, axis=0, keepdims=True) for s in parts])
        parts = [jnp.exp(s - highest) for s in parts]
        share = 1.0 / sum(jnp.sum(s, axis=0, keepdims=True) for s in parts)
        parts = [(s * share).astype(BF) for s in parts]
        p_ref[h, low:high, low:high] = parts[-1]
        mixed = dot(qkv_ref[2, head, low:high], parts[-1], ((1,), (0,)))
        if i:
            p_ref[h, :low, low:high] = parts[0]
            mixed += dot(qkv_ref[2, head, :low], parts[0], ((1,), (0,)))
        m_ref[head, low:high] = mixed.astype(BF)


def attend_kernel(t_ref, n_ref, wq_ref, tails_ref, qv_ref, up_ref, qkv_ref, w_ref, m_ref, p_ref, f_ref, o_ref, upo_ref, room, pair, *sems):
    links = Links(*sems)
    x, c = links.x, links.c
    links.greet(targets(links, "line", "y", "z"))
    gather = Gather(links, t_ref, o_ref)
    weight = WeightBlock(links, up_ref, pair, upo_ref)
    n = n_ref[...].reshape(LEN, D)
    last = links.rank == 7
    start = pl.multiple_of(48 - 16 * x + 128 * c, 16)
    parts = [qv_ref[2][:, 88:], qv_ref[0], qv_ref[1], jnp.zeros((2, 64), F32)]
    bias = jnp.concatenate([jnp.concatenate(parts, axis=1), jnp.zeros((6, 384), F32)], axis=0)
    bias = pltpu.roll(bias, 384 - start, 1)[:, :256].T[:SLOT]
    real = jnp.logical_or(lax.broadcasted_iota(jnp.int32, (SLOT, 1), 0) < 128, last)
    bias = [jnp.where(real, bias[:, 0:1], 0.0), 0.0, jnp.where(real, bias[:, 1:2], 0.0)]
    for k in range(3):
        for h in range(2):
            columns = slice(h * HALF, (h + 1) * HALF)
            rows = [tails_ref[h, k], wq_ref[h, 0, k], wq_ref[h, 1, k], jnp.zeros((48, HALF), BF)]
            room[:, columns] = jnp.concatenate([r.astype(F32) for r in rows], axis=0)
        mine = room[pl.ds(start, SLOT)].astype(BF)
        low = slice(k * SLOT, k * SLOT + 128)
        high = slice(k * SLOT + 128, (k + 1) * SLOT)
        w_ref[low] = mine[:128]
        w_ref[high] = jnp.where(last, mine[128:], BF(0))
        rows = slice(k * SLOT, (k + 1) * SLOT)
        qkv_ref[k] = (dot(w_ref[rows], n, ((1,), (1,))) + bias[k]).astype(BF)
    gather.relay()
    for h in range(SLOT // HDIM):
        attend_head(qkv_ref, h, m_ref, p_ref)
        if h == 0:
            weight.turn()
        if h == 1:
            gather.middle()
    own = links.rank
    columns = pl.ds(pl.multiple_of(own * TOK, TOK), TOK)
    links.keep(m_ref.at[:, columns], f_ref.at[own])
    for target, rank in links.line():
        columns = pl.ds(pl.multiple_of(rank * TOK, TOK), TOK)
        links.push(m_ref.at[:, columns], f_ref.at[own], target)
    weight.between_cores()
    gather.last()
    links.finish()


def attend(tangent, rows, wq, tails, bias, up):
    return call(
        attend_kernel,
        "attend",
        3,
        (tangent, rows, wq, tails, bias, up),
        "vvvvvh",
        [
            ("v", (3, SLOT, LEN), BF),
            ("v", (3 * SLOT, D), BF),
            ("v", (SLOT, LEN), BF),
            ("v", (SLOT // HDIM, LEN, LEN), BF),
            ("v", (8, SLOT, TOK), BF),
            ("v", (8, TOK, D), BF),
            ("v", (2, *QUARTERS), BF),
        ],
        [pltpu.VMEM((368, D), F32), pltpu.VMEM((2, *QUARTERS), BF)],
        20,
    )


def second_kernel(f_ref, wo_ref, i_ref, cols_ref, down_ref, o_ref, downo_ref, r_ref, cent_ref, inv_ref, m_ref, n, pair, *sems):
    links = Links(*sems)
    links.greet(targets(links, "x", "y", "c", "z"))
    weight = WeightBlock(links, down_ref, pair, downo_ref)
    for rank in range(7):
        m_ref[128 * rank : 128 * (rank + 1)] = f_ref[rank, :128]
    m_ref[896:] = f_ref[7]
    columns = jnp.concatenate([cols_ref[0], cols_ref[1]], axis=1)
    attended = [dot(m_ref[...], wo_ref[h], ((0,), (0,))) for h in range(2)]
    residual = i_ref[...] + (jnp.concatenate(attended, axis=1) + columns[0:1])
    r_ref[...] = residual + columns[5:6]
    n[...], cent_ref[...], inv_ref[...] = normed(residual, columns[3:4], columns[4:5])
    gather = Gather(links, n, o_ref)
    weight.turn()
    gather.relay()
    gather.middle()
    weight.between_cores()
    gather.last()
    links.finish()


def second(found, wo, inputs, columns, down):
    return call(
        second_kernel,
        "second",
        4,
        (found, wo, inputs, columns, down),
        "vvvvh",
        [
            ("v", (8, TOK, D), BF),
            ("v", (2, *QUARTERS), BF),
            ("v", (TOK, D), F32),
            ("v", (TOK, D), F32),
            ("v", (TOK, 1), F32),
        ],
        [pltpu.VMEM((D, TOK), BF), pltpu.VMEM((TOK, D), BF), pltpu.VMEM((2, *QUARTERS), BF)],
    )


def hidden_kernel(n_ref, t_ref, up_ref, down_ref, b_ref, low_ref, dn_ref, gup_ref, gdown_ref, gb_ref, up, down, up_sum, down_sum):
    step = pl.program_id(0)

    @pl.when(step == 0)
    def _():
        for h in range(2):
            up[:, h * HALF : (h + 1) * HALF] = up_ref[h]
            down[:, h * HALF : (h + 1) * HALF] = down_ref[h]
        up_sum[...] = jnp.zeros_like(up_sum)
        down_sum[...] = jnp.zeros_like(down_sum)
        gb_ref[...] = jnp.zeros_like(gb_ref)

    n = n_ref[...].reshape(BLOCK, D)
    t = t_ref[...].reshape(BLOCK, D)
    pre = dot(n, up[...], ((1,), (1,))) + b_ref[...]
    cumulative = 0.5 * (1.0 + lax.erf(pre * 0.7071067811865476))
    density = jnp.exp(-0.5 * pre * pre) * 0.3989422804014327
    active = (pre * cumulative).astype(BF)
    slope = cumulative + pre * density
    low_ref[...] = dot(active, down[...], ((1,), (0,))).astype(BF).reshape(low_ref.shape)
    d_pre = (dot(t, down[...], ((1,), (1,))) * slope).astype(BF)
    dn_ref[...] = dot(d_pre, up[...], ((1,), (0,))).astype(BF).reshape(dn_ref.shape)
    down_sum[...] += dot(active, t, ((0,), (0,)))
    up_sum[...] += dot(d_pre, n, ((0,), (0,)))
    gb_ref[...] += jnp.sum(d_pre.astype(F32), axis=0, keepdims=True)

    @pl.when(step == pl.num_programs(0) - 1)
    def _():
        for h in range(2):
            for out, total in ((gup_ref, up_sum), (gdown_ref, down_sum)):
                for j in range(8):
                    out[h, j] = pack(total[j * PART : (j + 1) * PART, h * HALF : (h + 1) * HALF]).astype(BF)


def hidden_part(second_rows, tangent_rows, up, down, bias):
    rows = pl.BlockSpec((BLOCK // TOK, TOK, D), lambda i: (i, 0, 0))
    weight = pl.BlockSpec((2, HALF, HALF), lambda i: (0, 0, 0))
    grad = pl.BlockSpec((2, *PIECES), lambda i: (0, 0, 0, 0))
    one = pl.BlockSpec((1, HALF), lambda i: (0, 0))
    return pl.pallas_call(
        hidden_kernel,
        grid=(LEN // BLOCK,),
        in_specs=[rows, rows, weight, weight, one],
        out_specs=(rows, rows, grad, grad, one),
        out_shape=(
            jax.ShapeDtypeStruct((8, TOK, D), BF),
            jax.ShapeDtypeStruct((8, TOK, D), BF),
            jax.ShapeDtypeStruct((2, *PIECES), BF),
            jax.ShapeDtypeStruct((2, *PIECES), BF),
            jax.ShapeDtypeStruct((1, HALF), F32),
        ),
        scratch_shapes=[pltpu.VMEM((HALF, D), BF)] * 2 + [pltpu.VMEM((HALF, D), F32)] * 2,
        compiler_params=pltpu.CompilerParams(vmem_limit_bytes=32 << 20),
        name="hidden_part",
    )(second_rows, tangent_rows, up, down, bias)


def norm_back(upstream, centred, inverse, gain):
    scaled = upstream * gain
    result = inverse * (
        scaled
        - jnp.mean(scaled, axis=1, keepdims=True)
        - centred * jnp.mean(scaled * centred, axis=1, keepdims=True)
    )
    return result, jnp.sum(upstream * centred, axis=0, keepdims=True), jnp.sum(upstream, axis=0, keepdims=True)


def third_kernel(p_ref, g_ref, t_ref, cent_ref, inv_ref, cols_ref, wo_ref, d_ref, a_ref, dm_ref, v_ref, piece_ref, near, out, came, parts, found, *sems):
    links = Links(*sems)
    links.greet(targets(links, "x", "c", "plane"))
    grads = GradScatter(links, parts, found)
    kept, swap = grads.between_cores(links, g_ref, parts)
    scatter = Scatter(links, p_ref, near, out, came)
    links.stored(kept)
    links.arrived(swap)
    grads.start()
    scatter.forward()
    gains = jnp.concatenate([cols_ref[0], cols_ref[1]], axis=1)
    part, gain, shift = norm_back(scatter.total(), cent_ref[...], inv_ref[...], gains[3:4])
    tangent = t_ref[...].astype(F32)
    d_residual = tangent + part
    d_ref[...] = d_residual
    rounded = d_residual.astype(BF)
    a_ref[...] = rounded
    d_mixed = [dot(wo_ref[h], rounded[:, h * HALF : (h + 1) * HALF], ((1,), (1,))) for h in range(2)]
    dm_ref[...] = (d_mixed[0] + d_mixed[1]).astype(BF)
    v_ref[0] = jnp.sum(d_residual.astype(BF).astype(F32), axis=0, keepdims=True)
    v_ref[1] = gain
    v_ref[2] = shift
    v_ref[3] = jnp.sum(tangent, axis=0, keepdims=True)
    piece_ref[...] = grads.total()
    links.finish()


def third(d_normed, grad, tangent, centred, inverse, gain, wo):
    return call(
        third_kernel,
        "third",
        5,
        (d_normed, grad, tangent, centred, inverse, gain, wo),
        "vvvvvvv",
        [
            ("v", (TOK, D), F32),
            ("v", (TOK, D), BF),
            ("v", (D, TOK), BF),
            ("v", (4, 1, D), F32),
            ("v", (PACKED, 128), BF),
        ],
        SCATTER_ROOM + GRADS_ROOM,
        16,
    )


def attend_back_head(qkv_ref, h, u_ref, p_ref, d_ref, dk_sum, dv_sum):
    head = pl.ds(h * HDIM, HDIM)
    for i in range(LEN // BLOCK):
        low, high = i * BLOCK, (i + 1) * BLOCK
        q = qkv_ref[0, head, low:high] * BF(HDIM**-0.5)
        u = u_ref[head, low:high]
        p = p_ref[h, :high, low:high]
        wide = p.astype(F32)
        dp = dot(qkv_ref[2, head, :high], u, ((0,), (0,)))
        centre = jnp.sum(wide * dp, axis=0, keepdims=True)
        ds = (wide * (dp - centre)).astype(BF)
        d_ref[head, low:high] = (dot(qkv_ref[1, head, :high], ds, ((1,), (0,))) * HDIM**-0.5).astype(BF)
        dk = dot(q, ds, ((1,), (1,)))
        dv = dot(u, p, ((1,), (1,)))
        if i:
            dk_sum[:, :low] += dk[:, :low]
            dv_sum[:, :low] += dv[:, :low]
        dk_sum[:, low:high] = dk[:, low:]
        dv_sum[:, low:high] = dv[:, low:]
    d_ref[pl.ds(SLOT + h * HDIM, HDIM)] = dk_sum[...].astype(BF)
    d_ref[pl.ds(2 * SLOT + h * HDIM, HDIM)] = dv_sum[...].astype(BF)


def back_kernel(m_ref, a_ref, qkv_ref, p_ref, g_ref, mixed_ref, n_ref, w_ref, down_ref, piece_ref, dn_ref, chip_ref, tail_ref, vb_ref, gdown_ref, u, d, dk_sum, dv_sum, o, own_grads, parts, found, *sems):
    links = Links(*sems)
    c = links.c
    links.greet(targets(links, "line", "plane"))
    own = links.rank
    columns = pl.ds(pl.multiple_of(own * TOK, TOK), TOK)

    def rows(rank):
        return pl.ds(pl.multiple_of(rank * 2 * HDIM, 2 * HDIM), SLOT)

    mine = links.keep(m_ref.at[rows(own)], u.at[:, columns])
    others = [links.push(m_ref.at[rows(rank)], u.at[:, columns], target) for target, rank in links.line()]
    gather = Gather(links, a_ref, o)
    grads = GradScatter(links, parts, found)
    kept, swap = grads.between_cores(links, g_ref, parts)
    links.stored(kept)
    links.arrived(swap)
    grads.start()
    spread = Spread(links, down_ref, gdown_ref)
    links.stored(mine)
    for copy in others:
        links.arrived(copy)
    n = n_ref[...].reshape(LEN, D)

    def weight_grad(left, right, k, rows):
        grad = dot(left, right, ((1,), (0,)))
        for h in range(2):
            own_grads[h, k, rows] = grad[:, h * HALF : (h + 1) * HALF].astype(BF)

    def between_cores(which):
        kept = links.keep(own_grads.at[(c, *which)], chip_ref.at[(c, *which)])
        return kept, links.push(own_grads.at[(1 - c, *which)], chip_ref.at[(c, *which)], links.sibling)

    def done(copies):
        links.stored(copies[0])
        links.arrived(copies[1])

    attend_back_head(qkv_ref, 0, u, p_ref, d, dk_sum, dv_sum)
    gather.relay()
    spread.turn()
    for k in range(3):
        weight_grad(d[k * SLOT : k * SLOT + HDIM], n, k, slice(0, HDIM))
    first_rows = between_cores((pl.ds(0, 3), pl.ds(0, HDIM)))
    attend_back_head(qkv_ref, 1, u, p_ref, d, dk_sum, dv_sum)
    done(first_rows)
    links.push(chip_ref.at[0, pl.ds(0, 3), pl.ds(0, HDIM)], tail_ref.at[pl.ds(0, 3)], links.along_x(3))
    gather.middle()
    attend_back_head(qkv_ref, 2, u, p_ref, d, dk_sum, dv_sum)
    gather.last()
    for k in range(3):
        weight_grad(d[k * SLOT + HDIM : (k + 1) * SLOT], n, k, slice(HDIM, SLOT))
    between_cores((pl.ds(0, 3), pl.ds(HDIM, SLOT - HDIM)))
    gather.complete()
    weight_grad(mixed_ref[...], o[...].reshape(LEN, D), 3, slice(0, SLOT))
    out_rows = between_cores((3,))
    for i in range(LEN // BLOCK):
        block = dot(d[:, i * BLOCK : (i + 1) * BLOCK], w_ref[...], ((0,), (0,))).astype(BF)
        dn_ref[2 * i : 2 * i + 2] = block.reshape(2, TOK, D)
        if i == 0:
            done(out_rows)
            links.push(chip_ref.at[0, 3, pl.ds(0, HDIM)], tail_ref.at[3], links.along_x(3))
    ones = jnp.ones((8, LEN), BF)
    vb_ref[...] = jnp.zeros_like(vb_ref)
    real = jnp.logical_or(lax.broadcasted_iota(jnp.int32, (1, SLOT), 1) < 128, own == 7)
    for i, k in enumerate((0, 2)):
        total = dot(ones, d[k * SLOT : (k + 1) * SLOT], ((1,), (1,)))[0:1]
        vb_ref[i, :, pl.ds(pl.multiple_of(own * 128, 128), SLOT)] = jnp.where(real, total, 0.0)
    piece_ref[...] = grads.total()
    links.finish()


def back(d_mixed, d_attended, qkv, probs, grad, mixed, rows, weight, down_piece):
    return call(
        back_kernel,
        "back",
        6,
        (d_mixed, d_attended, qkv, probs, grad, mixed, rows, weight, down_piece),
        "vvvvvvvvv",
        [
            ("v", (PACKED, 128), BF),
            ("v", (8, TOK, D), BF),
            ("v", (2, 4, SLOT, HALF), BF),
            ("v", (4, HDIM, HALF), BF),
            ("v", (2, 1, D), F32),
            ("v", PIECES, BF),
        ],
        [pltpu.VMEM((SLOT, LEN), BF), pltpu.VMEM((3 * SLOT, LEN), BF)]
        + [pltpu.VMEM((HDIM, LEN), F32)] * 2
        + [pltpu.VMEM((8, TOK, D), BF), pltpu.VMEM((2, 4, SLOT, HALF), BF)]
        + GRADS_ROOM,
        24,
    )


def fourth_kernel(p_ref, chip, tail, r_ref, cent_ref, inv_ref, cols_ref, i_ref, v_ref, piece_ref, near, out, came, whole, exact, parts, found, *sems):
    links = Links(*sems)
    x = links.x
    links.greet(targets(links, "x", "c", "plane"))
    scatter = Scatter(links, p_ref, near, out, came)
    whole[:, pl.ds(0, 128)] = chip[0, :, pl.ds(0, 128)]
    whole[:, pl.ds(128, 128)] = chip[1, :, pl.ds(0, 128)]
    whole[:, pl.ds(256, 64)] = jnp.where(x == 3, chip[1, :, pl.ds(128, 64)], tail[...])
    links.stored(links.keep(whole.at[:, pl.ds(pl.multiple_of(16 * x, 16), 272)], exact))
    for k in range(4):
        rows = exact[k].astype(F32)
        for j in range(4):
            parts[j // 2, 2 * k + j % 2] = pack(rows[j * PART : (j + 1) * PART]).astype(BF)
    grads = GradScatter(links, parts, found)
    grads.start()
    scatter.forward()
    gains = jnp.concatenate([cols_ref[0], cols_ref[1]], axis=1)
    part, gain, shift = norm_back(scatter.total(), cent_ref[...], inv_ref[...], gains[1:2])
    result = (r_ref[...] + part).T.astype(BF)
    i_ref[0] = result[:HALF]
    i_ref[1] = result[HALF:]
    v_ref[0] = gain
    v_ref[1] = shift
    piece_ref[...] = grads.total()
    links.finish()


def fourth(d_normed, chip, tail, residual, centred, inverse, columns):
    return call(
        fourth_kernel,
        "fourth",
        7,
        (d_normed, chip, tail, residual, centred, inverse, columns),
        "vvvvvvv",
        [
            ("v", (2, HALF, TOK), BF),
            ("v", (2, 1, D), F32),
            ("v", (PACKED, 128), BF),
        ],
        SCATTER_ROOM + [pltpu.VMEM((4, 320, HALF), BF), pltpu.VMEM((4, 272, HALF), BF)] + GRADS_ROOM,
        16,
    )


WIDE = 1792


def leave_kernel(p_ref, r_ref, i_ref, g_ref, v2_ref, v1_ref, vb_ref, b_ref, gup_ref, oo_ref, io_ref, found, vo_ref, found_up, near, out, came, halves_o, pair_o, pair_i, v_all, v_line, v_own, v_plane, v_sum, *sems):
    links = Links(*sems)
    y, zh, zl, c = links.y, links.zh, links.zl, links.c
    links.greet(targets(links, "line", "plane"))
    scatter = Scatter(links, p_ref, near, out, came)
    v_all[0] = v2_ref[0]
    v_all[1:3] = v1_ref[...]
    v_all[3:6] = v2_ref[1:4]
    v_all[6:8] = vb_ref[...]
    line = [links.push(v_all.at[rank], v_line.at[n], target) for n, (target, rank) in enumerate(links.line())]

    def between_cores(src, pair):
        return links.keep(src.at[c], pair.at[c]), links.push(src.at[1 - c], pair.at[c], links.sibling)

    def to_partner(pair, dst, copies):
        links.stored(copies[0])
        links.arrived(copies[1])
        links.push(pair.at[1 - zh], dst.at[zh], links.partner)
        links.keep(pair.at[zh], dst.at[zh])

    spreads = [Spread(links, gup_ref, found_up), Spread(links, g_ref, found)]
    copies = between_cores(i_ref, pair_i)
    scatter.forward()
    to_partner(pair_i, io_ref, copies)
    for spread in spreads:
        spread.turn()
    total = v_all[links.rank]
    for n, copy in enumerate(line):
        links.arrived(copy)
        total += v_line[n]
    v_own[...] = jnp.zeros_like(v_own)
    v_own[:, :D] = total
    v_own[:, 1152 : 1152 + HALF] = b_ref[...]
    place = (2 * zh + zl) * 4 + y
    kept = links.keep(v_own, v_plane.at[place])
    plane = [links.push(v_own, v_plane.at[place], target) for target, _, _ in links.plane()]
    links.stored(kept)
    for copy in plane:
        links.arrived(copy)
    total = v_plane[0]
    for n in range(1, 16):
        total += v_plane[n]
    v_sum[...] = total
    links.keep(v_sum, vo_ref.at[links.rank])
    for target, _ in links.line():
        links.push(v_sum, vo_ref.at[links.rank], target)
    result = (scatter.total() + r_ref[...]).T.astype(BF)
    halves_o[0] = result[:HALF]
    halves_o[1] = result[HALF:]
    to_partner(pair_o, oo_ref, between_cores(halves_o, pair_o))
    links.finish()


def leave(lowered, residual, in_grad, piece, *vectors, up_piece):
    pair = pltpu.VMEM((2, HALF, TOK), BF)
    return call(
        leave_kernel,
        "leave",
        8,
        (lowered, residual, in_grad, piece, *vectors, up_piece),
        "vvvvvvvvv",
        [
            ("v", (2, HALF, TOK), BF),
            ("v", (2, HALF, TOK), BF),
            ("v", PIECES, BF),
            ("v", (8, 1, WIDE), F32),
            ("v", PIECES, BF),
        ],
        SCATTER_ROOM
        + [pair, pair, pair]
        + [pltpu.VMEM((8, 1, D), F32), pltpu.VMEM((7, 1, D), F32), pltpu.VMEM((1, WIDE), F32)]
        + [pltpu.VMEM((16, 1, WIDE), F32), pltpu.VMEM((1, WIDE), F32)],
        16,
    )


def finish_kernel(o_ref, i_ref, g_ref, up_ref, down_ref, block_ref, in_ref, qkv_ref, out_ref, fup_ref, fdown_ref):
    block_ref[...] = o_ref[...]
    in_ref[...] = i_ref[...].astype(F32)
    for j in range(8):
        rows = slice(PART * (j % 2), PART * (j % 2 + 1))
        piece = unpack(g_ref[j].astype(F32))
        if j < 6:
            qkv_ref[j // 2, rows] = piece
        else:
            out_ref[rows] = piece
        rows = slice(PART * j, PART * (j + 1))
        fup_ref[rows] = unpack(up_ref[j].astype(F32))
        fdown_ref[rows] = unpack(down_ref[j].astype(F32))


def finish(block_out, in_grad, grads, up_grad, down_grad):
    whole = pl.BlockSpec(memory_space=pltpu.VMEM)
    return pl.pallas_call(
        finish_kernel,
        out_shape=(
            jax.ShapeDtypeStruct((2, HALF, TOK), BF),
            jax.ShapeDtypeStruct((2, HALF, TOK), F32),
            jax.ShapeDtypeStruct((3, 136, HALF), F32),
            jax.ShapeDtypeStruct((136, HALF), F32),
            jax.ShapeDtypeStruct((HALF, HALF), F32),
            jax.ShapeDtypeStruct((HALF, HALF), F32),
        ),
        in_specs=[whole] * 5,
        out_specs=(whole,) * 6,
        compiler_params=pltpu.CompilerParams(vmem_limit_bytes=16 << 20),
        name="finish",
    )(block_out, in_grad, grads, up_grad, down_grad)


def per_device(
    block_in,
    query_key_value_weight,
    bias_qv,
    output_weight,
    bias_out,
    gain_one,
    shift_one,
    gain_two,
    shift_two,
    up_weight,
    bias_up,
    down_weight,
    bias_down,
    out_grad,
):
    x, zh, c = (lax.axis_index(a) for a in ("x", "zh", "c"))

    columns = (bias_out, gain_one, shift_one, gain_two, shift_two, bias_down)
    wo4, columns, tail, inputs, normed_one, centred_one, inverse_one, tangent = enter(
        jnp.transpose(block_in, (0, 2, 1)),
        jnp.transpose(out_grad, (0, 2, 1)),
        output_weight,
        query_key_value_weight,
        columns,
    )
    first_rows, wq, tails, qv, bias_up, wo = first(
        normed_one, query_key_value_weight, tail, bias_qv, bias_up[None], wo4
    )

    qkv, weight_qkv, mixed, probs, found, tangent_rows, up = attend(
        tangent, first_rows, wq, tails, qv, up_weight.reshape(QUARTERS)
    )
    wo = wo.reshape(2, D, HALF)

    second_rows, down, residual, centred_two, inverse_two = second(
        found, wo, inputs, columns, down_weight.reshape(QUARTERS)
    )
    lowered, d_normed_two, up_grad, down_grad, grad_bias_up = hidden_part(
        second_rows,
        tangent_rows,
        up.reshape(2, HALF, HALF),
        down.reshape(2, HALF, HALF),
        bias_up,
    )
    d_residual, d_attended, d_mixed, sums_two, down_piece = third(
        d_normed_two, down_grad, tangent, centred_two, inverse_two, columns, wo
    )

    up_piece, d_normed_one, chip, tail, bias_sums, down_grad = back(
        d_mixed, d_attended, qkv, probs, up_grad, mixed, first_rows, weight_qkv, down_piece
    )
    in_grad, sums_one, piece = fourth(d_normed_one, chip, tail, d_residual, centred_one, inverse_one, columns)

    block_out, in_grad, grads, vectors, up_grad = leave(
        lowered, residual, in_grad, piece, sums_two, sums_one, bias_sums, grad_bias_up, up_piece=up_piece
    )
    block_out, in_grad, grad_qkv, grad_out, up_grad, down_grad = finish(block_out, in_grad, grads, up_grad, down_grad)
    row = 2 * x + zh
    vectors = vectors[:, 0]
    grad_bias_up = lax.dynamic_index_in_dim(vectors, row, 0, keepdims=False)[1152 : 1152 + HALF]
    six = lax.dynamic_slice_in_dim(vectors[:6], HALF * c, HALF, 1)
    grad_bias_out, grad_gain_one, grad_shift_one, grad_gain_two, grad_shift_two, grad_bias_down = six
    grad_bias_qv = lax.dynamic_slice_in_dim(vectors[6:], 136 * row, 136, 1)

    return (
        jnp.transpose(block_out, (0, 2, 1)),
        jnp.transpose(in_grad, (0, 2, 1)),
        grad_qkv,
        grad_bias_qv,
        grad_out,
        grad_bias_out,
        grad_gain_one,
        grad_shift_one,
        grad_gain_two,
        grad_shift_two,
        up_grad,
        grad_bias_up,
        down_grad,
        grad_bias_down,
    )


def solution(mesh):
    finer = Mesh(mesh.devices.reshape(2, 4, 4, 2, 2), ALL)
    return jax.shard_map(
        per_device,
        mesh=finer,
        in_specs=(
            P(DP, ROW, "c"),
            P(None, ROW, "c"),
            P(None, ROW),
            P(ROW, "c"),
            P("c"),
            P("c"),
            P("c"),
            P("c"),
            P("c"),
            P(ROW, "c"),
            P(ROW),
            P(ROW, "c"),
            P("c"),
            P(DP, ROW, "c"),
        ),
        out_specs=(
            P(DP, ROW, "c"),
            P(DP, ROW, "c"),
            P(None, ROW, "c"),
            P(None, ROW),
            P(ROW, "c"),
            P("c"),
            P("c"),
            P("c"),
            P("c"),
            P("c"),
            P(ROW, "c"),
            P(ROW),
            P(ROW, "c"),
            P("c"),
        ),
        check_vma=False,
    )
```

```python
import functools

import jax
import jax.numpy as jnp
from jax import lax
from jax.experimental import pallas as pl
from jax.experimental.pallas import tpu as pltpu
from jax.sharding import Mesh
from jax.sharding import PartitionSpec as P


HDIM = 64
D = 1088
HALF = D // 2
TOK = 128
LEN = 1024
SLOT = 192
EPSILON = 1e-05
MASKED = -1e30
DP = ("zl", "y")
ROW = ("x", "zh")
ALL = ("zl", "y", "x", "zh", "c")
MESH = pl.DeviceIdType.MESH
PART = 68
BF = jnp.bfloat16
F32 = jnp.float32


class Links:
    def __init__(self, send, recv, local):
        self.send, self.recv, self.local = send, recv, local
        self.pushed, self.kept = [], []
        self.x, self.c, self.y = lax.axis_index("x"), lax.axis_index("c"), lax.axis_index("y")
        self.zh, self.zl = lax.axis_index("zh"), lax.axis_index("zl")
        self.rank = 2 * self.x + self.c
        self.sibling = {"c": 1 - self.c}
        self.partner = {"zh": 1 - self.zh}

    def along_x(self, k):
        return {"x": lax.rem(self.x + k, 4)}

    def along_y(self, k):
        return {"y": lax.rem(self.y + k, 4)}

    def line(self):
        found = []
        for k, j in ((2, 0), (2, 1), (1, 0), (1, 1), (3, 0), (3, 1), (0, 1)):
            found.append((lax.rem(self.x + k, 4), lax.rem(self.c + j, 2)))
        return [({"x": x, "c": c}, 2 * x + c) for x, c in found]

    def plane(self, both=True):
        found = []
        for h in (1, 0) if both else (0,):
            for l in (1, 0):
                for k in (2, 1, 3, 0):
                    if h or l or k:
                        y, zl = lax.rem(self.y + k, 4), lax.rem(self.zl + l, 2)
                        zh = lax.rem(self.zh + h, 2)
                        found.append(({"y": y, "zl": zl, "zh": zh}, zh, 2 * y + zl))
        return found

    def greet(self, targets):
        barrier = pltpu.get_barrier_semaphore()
        for target in targets:
            pl.semaphore_signal(barrier, inc=1, device_id=target, device_id_type=MESH)
        pl.semaphore_wait(barrier, len(targets))

    def push(self, src, dst, target):
        n = len(self.pushed)
        copy = pltpu.make_async_remote_copy(
            src_ref=src,
            dst_ref=dst,
            send_sem=self.send.at[n],
            recv_sem=self.recv.at[n],
            device_id=target,
            device_id_type=MESH,
        )
        copy.start()
        self.pushed.append([copy, False])
        return n

    def arrived(self, n):
        if not self.pushed[n][1]:
            self.pushed[n][0].wait_recv()
            self.pushed[n][1] = True

    def keep(self, src, dst):
        n = len(self.kept)
        copy = pltpu.make_async_copy(src, dst, self.local.at[n])
        copy.start()
        self.kept.append([copy, False])
        return n

    def stored(self, n):
        if not self.kept[n][1]:
            self.kept[n][0].wait()
            self.kept[n][1] = True

    def finish(self):
        for n in range(len(self.kept)):
            self.stored(n)
        for n in range(len(self.pushed)):
            self.arrived(n)
        for copy, _ in self.pushed:
            copy.wait_send()


SEMS = [pltpu.SemaphoreType.DMA((64,)), pltpu.SemaphoreType.DMA((64,)), pltpu.SemaphoreType.DMA((32,))]
SPACES = {"v": pltpu.VMEM, "h": pltpu.HBM}


def call(kernel, name, cid, args, spaces, outs, scratch=(), mib=12):
    return pl.pallas_call(
        kernel,
        out_shape=tuple(jax.ShapeDtypeStruct(shape, dtype) for _, shape, dtype in outs),
        in_specs=[pl.BlockSpec(memory_space=SPACES[s]) for s in spaces],
        out_specs=tuple(pl.BlockSpec(memory_space=SPACES[s]) for s, _, _ in outs),
        scratch_shapes=[*scratch, *SEMS],
        compiler_params=pltpu.CompilerParams(
            collective_id=cid, has_side_effects=True, vmem_limit_bytes=mib << 20
        ),
        name=name,
    )(*args)


def top(ref):
    return ref.at[pl.ds(0, TOK // 2)]


def bottom(ref):
    return ref.at[pl.ds(TOK // 2, TOK // 2)]


class Gather:
    def __init__(self, links, a_ref, o_ref):
        self.links, self.o = links, o_ref
        own = o_ref.at[links.rank]
        self.kept = links.keep(a_ref, own)
        right, left = links.along_x(1), links.along_x(3)
        self.ahead = [links.push(top(a_ref), top(own), right)]
        self.back = [links.push(bottom(a_ref), bottom(own), left)]
        self.ahead.append(links.push(bottom(a_ref), bottom(own), right))
        self.back.append(links.push(top(a_ref), top(own), left))
        self.near = [links.push(a_ref, own, links.sibling)]

    def slot(self, k):
        return self.o.at[2 * lax.rem(self.links.x + 4 - k, 4) + self.links.c]

    def share(self, piece):
        self.near.append(self.links.push(piece, piece, self.links.sibling))

    def relay(self):
        links = self.links
        links.arrived(self.ahead[0])
        self.far = [links.push(top(self.slot(1)), top(self.slot(1)), links.along_x(1))]
        links.arrived(self.back[0])
        self.far.append(links.push(bottom(self.slot(3)), bottom(self.slot(3)), links.along_x(3)))
        self.share(top(self.slot(1)))
        self.share(bottom(self.slot(3)))

    def middle(self):
        links = self.links
        links.arrived(self.ahead[1])
        self.share(bottom(self.slot(1)))
        links.arrived(self.back[1])
        self.share(top(self.slot(3)))

    def last(self):
        links = self.links
        links.arrived(self.far[0])
        self.share(top(self.slot(2)))
        links.arrived(self.far[1])
        self.share(bottom(self.slot(2)))

    def complete(self):
        self.links.stored(self.kept)
        for copy in self.near:
            self.links.arrived(copy)


class Scatter:
    def __init__(self, links, p_ref, near, out, came):
        self.links, self.p, self.near, self.out, self.came = links, p_ref, near, out, came
        self.swaps = {}
        for k in (2, 1, 3, 0):
            to = lax.rem(links.x + k, 4)
            self.swaps[k] = links.push(p_ref.at[2 * to + 1 - links.c], near.at[k], links.sibling)

    def both(self, k):
        links = self.links
        links.arrived(self.swaps[k])
        to = lax.rem(links.x + k, 4)
        return self.p[2 * to + links.c].astype(F32) + self.near[k].astype(F32)

    def forward(self):
        links, out, came = self.links, self.out, self.came
        right, left = links.along_x(1), links.along_x(3)
        out[2] = self.both(2).astype(BF)
        ahead = links.push(top(out.at[2]), top(came.at[2]), right)
        back = links.push(bottom(out.at[2]), bottom(came.at[2]), left)
        half = TOK // 2
        one = self.both(1)
        out[1, half:] = one[half:].astype(BF)
        self.sends = [links.push(bottom(out.at[1]), bottom(came.at[1]), right)]
        three = self.both(3)
        out[3, :half] = three[:half].astype(BF)
        self.sends.append(links.push(top(out.at[3]), top(came.at[3]), left))
        links.arrived(ahead)
        out[1, :half] = (one[:half] + came[2, :half].astype(F32)).astype(BF)
        self.sends.append(links.push(top(out.at[1]), top(came.at[1]), right))
        links.arrived(back)
        out[3, half:] = (three[half:] + came[2, half:].astype(F32)).astype(BF)
        self.sends.append(links.push(bottom(out.at[3]), bottom(came.at[3]), left))

    def total(self):
        total = self.both(0)
        for copy in self.sends:
            self.links.arrived(copy)
        return total + self.came[1].astype(F32) + self.came[3].astype(F32)


SCATTER_ROOM = [pltpu.VMEM((4, TOK, D), BF)] * 3
PACKED = PART * HALF // 128
PIECES = (8, PACKED, 128)
GRADS_ROOM = [pltpu.VMEM((2, *PIECES), BF), pltpu.VMEM((16, PACKED, 128), BF)]


def pack(rows):
    tiles = [rows[:, 128 * t : 128 * (t + 1)] for t in range(4)]
    rest = jnp.concatenate([rows[17 * q : 17 * (q + 1), 512:] for q in range(4)], axis=1)
    return jnp.concatenate([*tiles, rest], axis=0)


def unpack(piece):
    tiles = [piece[PART * t : PART * (t + 1)] for t in range(4)]
    rest = [piece[4 * PART :, 32 * q : 32 * (q + 1)] for q in range(4)]
    return jnp.concatenate([*tiles, jnp.concatenate(rest, axis=0)], axis=1)


class GradScatter:
    def __init__(self, links, parts, came):
        self.links, self.parts, self.came = links, parts, came

    @staticmethod
    def between_cores(links, own, parts):
        kept = links.keep(own.at[links.c], parts.at[links.c])
        swap = links.push(own.at[1 - links.c], parts.at[links.c], links.sibling)
        return kept, swap

    def start(self):
        self.sends = [
            self.links.push(self.parts.at[zh, piece], self.came.at[n + 1], target)
            for n, (target, zh, piece) in enumerate(self.links.plane())
        ]

    def total(self):
        links = self.links
        total = self.parts[links.zh, 2 * links.y + links.zl].astype(F32)
        for n, send in enumerate(self.sends):
            links.arrived(send)
            total += self.came[n + 1].astype(F32)
        return total.astype(BF)


class Spread:
    def __init__(self, links, piece_ref, o_ref):
        self.links, self.o = links, o_ref
        slot = o_ref.at[2 * links.y + links.zl]
        self.other = links.push(piece_ref, slot, {"zl": 1 - links.zl})
        self.kept = links.keep(piece_ref, slot)
        self.copies = [links.push(piece_ref, slot, links.along_y(k)) for k in (2, 1, 3)]

    def turn(self):
        links = self.links
        links.arrived(self.other)
        slot = self.o.at[2 * links.y + 1 - links.zl]
        self.copies += [links.push(slot, slot, links.along_y(k)) for k in (2, 1, 3)]


def targets(links, *groups):
    found = []
    for group in groups:
        if group == "x":
            found += [links.along_x(k) for k in (1, 2, 3)]
        if group == "y":
            found += [links.along_y(k) for k in (1, 2, 3)]
        if group == "c":
            found.append(links.sibling)
        if group == "z":
            found.append(links.partner)
        if group == "line":
            found += [target for target, _ in links.line()]
        if group == "plane":
            found += [target for target, _, _ in links.plane()]
    return found


def normed(values, gain, shift):
    centre = jnp.mean(values, axis=1, keepdims=True)
    second_moment = jnp.mean(values * values, axis=1, keepdims=True)
    inverse = lax.rsqrt(second_moment - centre * centre + EPSILON)
    centred = (values - centre) * inverse
    return (centred * gain + shift).astype(BF), centred, inverse


def enter_kernel(a_ref, t_ref, wo_ref, w_ref, b0, b1, b2, b3, b4, b5, wo4_ref, colso_ref, tailo_ref, i_ref, n_ref, cent_ref, inv_ref, t32_ref, pair, tpair, tok, ttok, cols, tail, block, v0, v1, v2, v3, v4, v5, *sems):
    links = Links(*sems)
    x, y, zh, c = links.x, links.y, links.zh, links.c
    right, left = lax.rem(x + 1, 4), lax.rem(x + 3, 4)
    diagonal = [{"x": right, "zh": 1 - zh}, {"x": left, "zh": 1 - zh}]
    vectors = (v0, v1, v2, v3, v4, v5)
    loads = [links.keep(b, v) for b, v in zip((b0, b1, b2, b3, b4, b5), vectors)]
    load = links.keep(w_ref.at[jnp.minimum(y, 2)], block)
    links.greet(targets(links, "x", "c", "z") + diagonal)
    other = links.push(a_ref.at[1 - zh], pair.at[zh], links.partner)
    mine = links.keep(a_ref.at[zh], pair.at[zh])
    t_other = links.push(t_ref.at[1 - zh], tpair.at[zh], links.partner)
    t_mine = links.keep(t_ref.at[zh], tpair.at[zh])
    for copy in loads:
        links.stored(copy)
    cols[...] = jnp.concatenate([v[...].reshape(1, HALF) for v in (*vectors, v5, v5)], axis=0)
    swap = links.push(cols, colso_ref.at[c], links.sibling)
    own = links.keep(cols, colso_ref.at[c])
    for k in (2, 1, 3):
        links.push(wo_ref, wo4_ref.at[x], links.along_x(k))
    links.keep(wo_ref, wo4_ref.at[x])
    links.stored(load)
    tail[...] = block[88:]
    shifts = [
        pltpu.make_async_remote_copy(
            src_ref=tail,
            dst_ref=tailo_ref,
            send_sem=links.send.at[50 + i],
            recv_sem=links.recv.at[50],
            device_id=target,
            device_id_type=MESH,
        )
        for i, target in enumerate(({"x": right}, diagonal[0]))
    ]

    @pl.when(zh == 1)
    def _():
        for copy in shifts:
            copy.start()

    links.stored(mine)
    links.arrived(other)
    got = links.push(pair.at[1 - c], tok.at[c], links.sibling)
    kept = links.keep(pair.at[c], tok.at[c])
    links.stored(t_mine)
    links.arrived(t_other)
    t_got = links.push(tpair.at[1 - c], ttok.at[c], links.sibling)
    t_kept = links.keep(tpair.at[c], ttok.at[c])
    links.arrived(swap)
    links.stored(own)
    links.stored(kept)
    links.arrived(got)

    def whole(halves):
        return jnp.concatenate([halves[0].astype(F32), halves[1].astype(F32)], axis=0).T

    values = whole(tok)
    i_ref[...] = values
    gains = jnp.concatenate([colso_ref[0], colso_ref[1]], axis=1)
    n_ref[...], cent_ref[...], inv_ref[...] = normed(values, gains[1:2], gains[2:3])
    links.stored(t_kept)
    links.arrived(t_got)
    t32_ref[...] = whole(ttok).astype(BF)
    links.finish()
    shifts[0].wait_recv()

    @pl.when(zh == 1)
    def _():
        for copy in shifts:
            copy.wait_send()


def enter(block_in, out_grad, output_weight, w, columns):
    halves = pltpu.VMEM((2, HALF, TOK), BF)
    return call(
        enter_kernel,
        "enter",
        1,
        (block_in, out_grad, output_weight, w, *columns),
        "hhhhhhhhhh",
        [
            ("v", (4, 136, HALF), BF),
            ("v", (2, 8, HALF), F32),
            ("v", (48, HALF), BF),
            ("v", (TOK, D), F32),
            ("v", (TOK, D), BF),
            ("v", (TOK, D), F32),
            ("v", (TOK, 1), F32),
            ("v", (TOK, D), BF),
        ],
        [halves] * 4
        + [pltpu.VMEM((8, HALF), F32), pltpu.VMEM((48, HALF), BF), pltpu.VMEM((136, HALF), BF)]
        + [pltpu.VMEM((HALF,), F32)] * 6,
    )


def first_kernel(n_ref, w_ref, tail_ref, qv_in, up_in, o_ref, wq_ref, tails_ref, qvo_ref, b_ref, qv_ref, up_flat, up_ref, ups, *sems):
    links = Links(*sems)
    x, y, zh, c = links.x, links.y, links.zh, links.c
    right, left = lax.rem(x + 1, 4), lax.rem(x + 3, 4)
    diagonal = [{"x": right, "zh": 1 - zh}, {"x": left, "zh": 1 - zh}]
    loads = [links.keep(qv_in, qv_ref), links.keep(up_in, up_flat)]
    links.greet(targets(links, "x", "y", "c", "z") + diagonal)
    gather = Gather(links, n_ref, o_ref)
    for copy in loads:
        links.stored(copy)
    up_ref[...] = up_flat[...].reshape(1, HALF)
    w_other = links.push(w_ref, wq_ref.at[c, zh], links.partner)
    links.keep(w_ref, wq_ref.at[c, zh])
    links.push(w_ref, wq_ref.at[c, zh], links.sibling)
    links.push(qv_ref, qvo_ref.at[zh], links.partner)
    links.keep(qv_ref, qvo_ref.at[zh])
    up_other = links.push(up_ref, ups.at[zh], links.partner)
    up_mine = links.keep(up_ref, ups.at[zh])
    slot = tails_ref.at[c, y]
    links.keep(tail_ref, slot)
    links.push(tail_ref, slot, links.sibling)
    tails = [links.push(tail_ref, slot, links.along_y(k)) for k in (2, 1, 3)]
    shifts = [
        pltpu.make_async_remote_copy(
            src_ref=qv_ref,
            dst_ref=qvo_ref.at[2],
            send_sem=links.send.at[50 + i],
            recv_sem=links.recv.at[50],
            device_id=target,
            device_id_type=MESH,
        )
        for i, target in enumerate(({"x": right}, diagonal[0]))
    ]

    @pl.when(zh == 1)
    def _():
        for copy in shifts:
            copy.start()

    for k, copy in zip((2, 1, 3), tails):
        links.arrived(copy)
        slot = tails_ref.at[c, lax.rem(y + 4 - k, 4)]
        links.push(slot, slot, links.sibling)
    gather.relay()
    links.stored(up_mine)
    links.arrived(up_other)
    b_ref[...] = ups[c]
    gather.middle()
    links.arrived(w_other)
    slot = wq_ref.at[c, 1 - zh]
    links.push(slot, slot, links.sibling)
    gather.last()
    links.finish()
    shifts[0].wait_recv()

    @pl.when(zh == 1)
    def _():
        for copy in shifts:
            copy.wait_send()


def first(normed, w, tail, qv, up):
    return call(
        first_kernel,
        "first",
        2,
        (normed, w, tail, qv, up),
        "vhvhh",
        [
            ("v", (8, TOK, D), BF),
            ("v", (2, 2, 3, 136, HALF), BF),
            ("v", (2, 4, 48, HALF), BF),
            ("v", (3, 2, 136), F32),
            ("v", (1, HALF), F32),
        ],
        [pltpu.VMEM((2, 136), F32), pltpu.VMEM((HALF,), F32), pltpu.VMEM((1, HALF), F32), pltpu.VMEM((2, 1, HALF), F32)],
    )


class WeightBlock:
    def __init__(self, links, w_ref, pair, o_ref):
        self.links, self.pair, self.o = links, pair, o_ref
        self.other = links.push(w_ref.at[links.y], pair.at[links.zh, links.y], links.partner)
        self.kept = links.keep(w_ref, pair.at[links.zh])

    def turn(self):
        links = self.links
        links.arrived(self.other)
        slot = self.pair.at[1 - links.zh, links.y]
        self.round = [links.push(slot, slot, links.along_y(k)) for k in (2, 1, 3)]

    def between_cores(self):
        links = self.links
        links.stored(self.kept)
        for copy in self.round:
            links.arrived(copy)
        links.push(self.pair.at[1 - links.c], self.o.at[links.c], links.sibling)
        links.keep(self.pair.at[links.c], self.o.at[links.c])


QUARTERS = (4, 136, HALF)

BLOCK = 256


def dot(a, b, dims):
    return lax.dot_general(a, b, (dims, ((), ())), preferred_element_type=F32)


def attend_head(qkv_ref, h, m_ref, p_ref):
    keys = lax.broadcasted_iota(jnp.int32, (BLOCK, BLOCK), 0)
    queries = lax.broadcasted_iota(jnp.int32, (BLOCK, BLOCK), 1)
    head = pl.ds(h * HDIM, HDIM)
    for i in range(LEN // BLOCK):
        low, high = i * BLOCK, (i + 1) * BLOCK
        q = qkv_ref[0, head, low:high] * BF(HDIM**-0.5)
        parts = [dot(qkv_ref[1, head, low:high], q, ((0,), (0,)))]
        parts[0] = jnp.where(keys <= queries, parts[0], MASKED)
        if i:
            parts.insert(0, dot(qkv_ref[1, head, :low], q, ((0,), (0,))))
        highest = functools.reduce(jnp.maximum, [jnp.max(s, axis=0, keepdims=True) for s in parts])
        parts = [jnp.exp(s - highest) for s in parts]
        share = 1.0 / sum(jnp.sum(s, axis=0, keepdims=True) for s in parts)
        parts = [(s * share).astype(BF) for s in parts]
        p_ref[h, low:high, low:high] = parts[-1]
        mixed = dot(qkv_ref[2, head, low:high], parts[-1], ((1,), (0,)))
        if i:
            p_ref[h, :low, low:high] = parts[0]
            mixed += dot(qkv_ref[2, head, :low], parts[0], ((1,), (0,)))
        m_ref[head, low:high] = mixed.astype(BF)


def attend_kernel(t_ref, n_ref, wq_ref, tails_ref, qv_ref, up_ref, wo4_ref, qkv_ref, w_ref, m_ref, p_ref, f_ref, o_ref, upo_ref, woo_ref, room, pair, mid, *sems):
    links = Links(*sems)
    x, y, zh, c = links.x, links.y, links.zh, links.c
    links.greet(targets(links, "line", "y", "z"))
    wo_own = links.push(wo4_ref.at[y], mid, links.partner)
    gather = Gather(links, t_ref, o_ref)
    weight = WeightBlock(links, up_ref, pair, upo_ref)
    links.keep(wo4_ref, woo_ref.at[c, :, zh])
    links.push(wo4_ref, woo_ref.at[c, :, zh], links.sibling)
    n = n_ref[...].reshape(LEN, D)
    last = links.rank == 7
    start = pl.multiple_of(48 - 16 * x + 128 * c, 16)
    parts = [qv_ref[2][:, 88:], qv_ref[0], qv_ref[1], jnp.zeros((2, 64), F32)]
    bias = jnp.concatenate([jnp.concatenate(parts, axis=1), jnp.zeros((6, 384), F32)], axis=0)
    bias = pltpu.roll(bias, 384 - start, 1)[:, :256].T[:SLOT]
    real = jnp.logical_or(lax.broadcasted_iota(jnp.int32, (SLOT, 1), 0) < 128, last)
    bias = [jnp.where(real, bias[:, 0:1], 0.0), 0.0, jnp.where(real, bias[:, 1:2], 0.0)]
    for k in range(3):
        for h in range(2):
            columns = slice(h * HALF, (h + 1) * HALF)
            rows = [tails_ref[h, k], wq_ref[h, 0, k], wq_ref[h, 1, k], jnp.zeros((48, HALF), BF)]
            room[:, columns] = jnp.concatenate([r.astype(F32) for r in rows], axis=0)
        mine = room[pl.ds(start, SLOT)].astype(BF)
        low = slice(k * SLOT, k * SLOT + 128)
        high = slice(k * SLOT + 128, (k + 1) * SLOT)
        w_ref[low] = mine[:128]
        w_ref[high] = jnp.where(last, mine[128:], BF(0))
        rows = slice(k * SLOT, (k + 1) * SLOT)
        qkv_ref[k] = (dot(w_ref[rows], n, ((1,), (1,))) + bias[k]).astype(BF)
    gather.relay()
    links.arrived(wo_own)
    slot = woo_ref.at[c, y, 1 - zh]
    links.keep(mid, slot)
    round_y = [links.push(mid, slot, links.along_y(k)) for k in (2, 1, 3)]
    links.push(mid, slot, links.sibling)
    for h in range(SLOT // HDIM):
        attend_head(qkv_ref, h, m_ref, p_ref)
        if h == 0:
            weight.turn()
        if h == 1:
            gather.middle()
    own = links.rank
    columns = pl.ds(pl.multiple_of(own * TOK, TOK), TOK)
    links.keep(m_ref.at[:, columns], f_ref.at[own])
    for target, rank in links.line():
        columns = pl.ds(pl.multiple_of(rank * TOK, TOK), TOK)
        links.push(m_ref.at[:, columns], f_ref.at[own], target)
    for k, copy in zip((2, 1, 3), round_y):
        links.arrived(copy)
        slot = woo_ref.at[c, lax.rem(y + 4 - k, 4), 1 - zh]
        links.push(slot, slot, links.sibling)
    gather.last()
    weight.between_cores()
    links.finish()


def attend(tangent, rows, wq, tails, bias, up, wo4):
    return call(
        attend_kernel,
        "attend",
        3,
        (tangent, rows, wq, tails, bias, up, wo4),
        "vvvvvhv",
        [
            ("v", (3, SLOT, LEN), BF),
            ("v", (3 * SLOT, D), BF),
            ("v", (SLOT, LEN), BF),
            ("v", (SLOT // HDIM, LEN, LEN), BF),
            ("v", (8, SLOT, TOK), BF),
            ("v", (8, TOK, D), BF),
            ("v", (2, *QUARTERS), BF),
            ("v", (2, 4, 2, 136, HALF), BF),
        ],
        [pltpu.VMEM((368, D), F32), pltpu.VMEM((2, *QUARTERS), BF), pltpu.VMEM((136, HALF), BF)],
        20,
    )


def second_kernel(f_ref, wo_ref, i_ref, cols_ref, down_ref, o_ref, downo_ref, r_ref, cent_ref, inv_ref, m_ref, n, pair, *sems):
    links = Links(*sems)
    links.greet(targets(links, "x", "y", "c", "z"))
    weight = WeightBlock(links, down_ref, pair, downo_ref)
    for rank in range(7):
        m_ref[128 * rank : 128 * (rank + 1)] = f_ref[rank, :128]
    m_ref[896:] = f_ref[7]
    columns = jnp.concatenate([cols_ref[0], cols_ref[1]], axis=1)
    attended = [dot(m_ref[...], wo_ref[h], ((0,), (0,))) for h in range(2)]
    residual = i_ref[...] + (jnp.concatenate(attended, axis=1) + columns[0:1])
    r_ref[...] = residual + columns[5:6]
    n[...], cent_ref[...], inv_ref[...] = normed(residual, columns[3:4], columns[4:5])
    gather = Gather(links, n, o_ref)
    weight.turn()
    gather.relay()
    gather.middle()
    weight.between_cores()
    gather.last()
    links.finish()


def second(found, wo, inputs, columns, down):
    return call(
        second_kernel,
        "second",
        4,
        (found, wo, inputs, columns, down),
        "vvvvh",
        [
            ("v", (8, TOK, D), BF),
            ("v", (2, *QUARTERS), BF),
            ("v", (TOK, D), F32),
            ("v", (TOK, D), F32),
            ("v", (TOK, 1), F32),
        ],
        [pltpu.VMEM((D, TOK), BF), pltpu.VMEM((TOK, D), BF), pltpu.VMEM((2, *QUARTERS), BF)],
    )


STEP = 512


def hidden_kernel(n_ref, t_ref, up_ref, down_ref, b_ref, low_ref, dn_ref, gup_ref, gdown_ref, gb_ref, up, down, up_sum, down_sum):
    step = pl.program_id(0)

    @pl.when(step == 0)
    def _():
        for h in range(2):
            up[:, h * HALF : (h + 1) * HALF] = up_ref[h]
            down[:, h * HALF : (h + 1) * HALF] = down_ref[h]
        up_sum[...] = jnp.zeros_like(up_sum)
        down_sum[...] = jnp.zeros_like(down_sum)
        gb_ref[...] = jnp.zeros_like(gb_ref)

    n = n_ref[...].reshape(STEP, D)
    t = t_ref[...].reshape(STEP, D)
    pre = dot(n, up[...], ((1,), (1,))) + b_ref[...]
    cumulative = 0.5 * (1.0 + lax.erf(pre * 0.7071067811865476))
    density = jnp.exp(-0.5 * pre * pre) * 0.3989422804014327
    active = (pre * cumulative).astype(BF)
    slope = cumulative + pre * density
    low_ref[...] = dot(active, down[...], ((1,), (0,))).astype(BF).reshape(low_ref.shape)
    d_pre = (dot(t, down[...], ((1,), (1,))) * slope).astype(BF)
    dn_ref[...] = dot(d_pre, up[...], ((1,), (0,))).astype(BF).reshape(dn_ref.shape)
    down_sum[...] += dot(active, t, ((0,), (0,)))
    up_sum[...] += dot(d_pre, n, ((0,), (0,)))
    gb_ref[...] += jnp.sum(d_pre.astype(F32), axis=0, keepdims=True)

    @pl.when(step == pl.num_programs(0) - 1)
    def _():
        for h in range(2):
            for out, total in ((gup_ref, up_sum), (gdown_ref, down_sum)):
                for j in range(8):
                    out[h, j] = pack(total[j * PART : (j + 1) * PART, h * HALF : (h + 1) * HALF]).astype(BF)


def hidden_part(second_rows, tangent_rows, up, down, bias):
    rows = pl.BlockSpec((STEP // TOK, TOK, D), lambda i: (i, 0, 0))
    weight = pl.BlockSpec((2, HALF, HALF), lambda i: (0, 0, 0))
    grad = pl.BlockSpec((2, *PIECES), lambda i: (0, 0, 0, 0))
    one = pl.BlockSpec((1, HALF), lambda i: (0, 0))
    return pl.pallas_call(
        hidden_kernel,
        grid=(LEN // STEP,),
        in_specs=[rows, rows, weight, weight, one],
        out_specs=(rows, rows, grad, grad, one),
        out_shape=(
            jax.ShapeDtypeStruct((8, TOK, D), BF),
            jax.ShapeDtypeStruct((8, TOK, D), BF),
            jax.ShapeDtypeStruct((2, *PIECES), BF),
            jax.ShapeDtypeStruct((2, *PIECES), BF),
            jax.ShapeDtypeStruct((1, HALF), F32),
        ),
        scratch_shapes=[pltpu.VMEM((HALF, D), BF)] * 2 + [pltpu.VMEM((HALF, D), F32)] * 2,
        compiler_params=pltpu.CompilerParams(vmem_limit_bytes=32 << 20),
        name="hidden_part",
    )(second_rows, tangent_rows, up, down, bias)


def norm_back(upstream, centred, inverse, gain):
    scaled = upstream * gain
    result = inverse * (
        scaled
        - jnp.mean(scaled, axis=1, keepdims=True)
        - centred * jnp.mean(scaled * centred, axis=1, keepdims=True)
    )
    return result, jnp.sum(upstream * centred, axis=0, keepdims=True), jnp.sum(upstream, axis=0, keepdims=True)


def third_kernel(p_ref, g_ref, t_ref, cent_ref, inv_ref, cols_ref, wo_ref, d_ref, a_ref, dm_ref, v_ref, piece_ref, near, out, came, parts, found, *sems):
    links = Links(*sems)
    links.greet(targets(links, "x", "c", "plane"))
    grads = GradScatter(links, parts, found)
    kept, swap = grads.between_cores(links, g_ref, parts)
    scatter = Scatter(links, p_ref, near, out, came)
    links.stored(kept)
    links.arrived(swap)
    grads.start()
    scatter.forward()
    gains = jnp.concatenate([cols_ref[0], cols_ref[1]], axis=1)
    part, gain, shift = norm_back(scatter.total(), cent_ref[...], inv_ref[...], gains[3:4])
    tangent = t_ref[...].astype(F32)
    d_residual = tangent + part
    d_ref[...] = d_residual
    rounded = d_residual.astype(BF)
    a_ref[...] = rounded
    d_mixed = [dot(wo_ref[h], rounded[:, h * HALF : (h + 1) * HALF], ((1,), (1,))) for h in range(2)]
    dm_ref[...] = (d_mixed[0] + d_mixed[1]).astype(BF)
    v_ref[0] = jnp.sum(d_residual.astype(BF).astype(F32), axis=0, keepdims=True)
    v_ref[1] = gain
    v_ref[2] = shift
    v_ref[3] = jnp.sum(tangent, axis=0, keepdims=True)
    piece_ref[...] = grads.total()
    links.finish()


def third(d_normed, grad, tangent, centred, inverse, gain, wo):
    return call(
        third_kernel,
        "third",
        5,
        (d_normed, grad, tangent, centred, inverse, gain, wo),
        "vvvvvvv",
        [
            ("v", (TOK, D), F32),
            ("v", (TOK, D), BF),
            ("v", (D, TOK), BF),
            ("v", (4, 1, D), F32),
            ("v", (PACKED, 128), BF),
        ],
        SCATTER_ROOM + GRADS_ROOM,
        16,
    )


def attend_back_head(qkv_ref, h, u_ref, p_ref, d_ref, dk_sum, dv_sum):
    head = pl.ds(h * HDIM, HDIM)
    for i in range(LEN // BLOCK):
        low, high = i * BLOCK, (i + 1) * BLOCK
        q = qkv_ref[0, head, low:high] * BF(HDIM**-0.5)
        u = u_ref[head, low:high]
        p = p_ref[h, :high, low:high]
        wide = p.astype(F32)
        dp = dot(qkv_ref[2, head, :high], u, ((0,), (0,)))
        centre = jnp.sum(wide * dp, axis=0, keepdims=True)
        ds = (wide * (dp - centre)).astype(BF)
        d_ref[head, low:high] = (dot(qkv_ref[1, head, :high], ds, ((1,), (0,))) * HDIM**-0.5).astype(BF)
        dk = dot(q, ds, ((1,), (1,)))
        dv = dot(u, p, ((1,), (1,)))
        if i:
            dk_sum[:, :low] += dk[:, :low]
            dv_sum[:, :low] += dv[:, :low]
        dk_sum[:, low:high] = dk[:, low:]
        dv_sum[:, low:high] = dv[:, low:]
    d_ref[pl.ds(SLOT + h * HDIM, HDIM)] = dk_sum[...].astype(BF)
    d_ref[pl.ds(2 * SLOT + h * HDIM, HDIM)] = dv_sum[...].astype(BF)


def back_kernel(m_ref, a_ref, qkv_ref, p_ref, g_ref, mixed_ref, n_ref, w_ref, piece_ref, dn_ref, chip_ref, tail_ref, vb_ref, u, d, dk_sum, dv_sum, o, own_grads, parts, found, *sems):
    links = Links(*sems)
    c = links.c
    links.greet(targets(links, "line", "plane"))
    own = links.rank
    columns = pl.ds(pl.multiple_of(own * TOK, TOK), TOK)

    def rows(rank):
        return pl.ds(pl.multiple_of(rank * 2 * HDIM, 2 * HDIM), SLOT)

    mine = links.keep(m_ref.at[rows(own)], u.at[:, columns])
    others = [links.push(m_ref.at[rows(rank)], u.at[:, columns], target) for target, rank in links.line()]
    gather = Gather(links, a_ref, o)
    grads = GradScatter(links, parts, found)
    kept, swap = grads.between_cores(links, g_ref, parts)
    links.stored(kept)
    links.arrived(swap)
    grads.start()
    links.stored(mine)
    for copy in others:
        links.arrived(copy)
    n = n_ref[...].reshape(LEN, D)

    def weight_grad(left, right, k, rows):
        grad = dot(left, right, ((1,), (0,)))
        for h in range(2):
            own_grads[h, k, rows] = grad[:, h * HALF : (h + 1) * HALF].astype(BF)

    def between_cores(which):
        kept = links.keep(own_grads.at[(c, *which)], chip_ref.at[(c, *which)])
        return kept, links.push(own_grads.at[(1 - c, *which)], chip_ref.at[(c, *which)], links.sibling)

    def done(copies):
        links.stored(copies[0])
        links.arrived(copies[1])

    attend_back_head(qkv_ref, 0, u, p_ref, d, dk_sum, dv_sum)
    gather.relay()
    for k in range(3):
        weight_grad(d[k * SLOT : k * SLOT + HDIM], n, k, slice(0, HDIM))
    first_rows = between_cores((pl.ds(0, 3), pl.ds(0, HDIM)))
    attend_back_head(qkv_ref, 1, u, p_ref, d, dk_sum, dv_sum)
    done(first_rows)
    links.push(chip_ref.at[0, pl.ds(0, 3), pl.ds(0, HDIM)], tail_ref.at[pl.ds(0, 3)], links.along_x(3))
    gather.middle()
    attend_back_head(qkv_ref, 2, u, p_ref, d, dk_sum, dv_sum)
    gather.last()
    for k in range(3):
        weight_grad(d[k * SLOT + HDIM : (k + 1) * SLOT], n, k, slice(HDIM, SLOT))
    between_cores((pl.ds(0, 3), pl.ds(HDIM, SLOT - HDIM)))
    gather.complete()
    weight_grad(mixed_ref[...], o[...].reshape(LEN, D), 3, slice(0, SLOT))
    out_rows = between_cores((3,))
    for i in range(LEN // BLOCK):
        block = dot(d[:, i * BLOCK : (i + 1) * BLOCK], w_ref[...], ((0,), (0,))).astype(BF)
        dn_ref[2 * i : 2 * i + 2] = block.reshape(2, TOK, D)
        if i == 0:
            done(out_rows)
            links.push(chip_ref.at[0, 3, pl.ds(0, HDIM)], tail_ref.at[3], links.along_x(3))
    ones = jnp.ones((8, LEN), BF)
    vb_ref[...] = jnp.zeros_like(vb_ref)
    real = jnp.logical_or(lax.broadcasted_iota(jnp.int32, (1, SLOT), 1) < 128, own == 7)
    for i, k in enumerate((0, 2)):
        total = dot(ones, d[k * SLOT : (k + 1) * SLOT], ((1,), (1,)))[0:1]
        vb_ref[i, :, pl.ds(pl.multiple_of(own * 128, 128), SLOT)] = jnp.where(real, total, 0.0)
    piece_ref[...] = grads.total()
    links.finish()


def back(d_mixed, d_attended, qkv, probs, grad, mixed, rows, weight):
    return call(
        back_kernel,
        "back",
        6,
        (d_mixed, d_attended, qkv, probs, grad, mixed, rows, weight),
        "vvvvvvvv",
        [
            ("v", (PACKED, 128), BF),
            ("v", (8, TOK, D), BF),
            ("v", (2, 4, SLOT, HALF), BF),
            ("v", (4, HDIM, HALF), BF),
            ("v", (2, 1, D), F32),
        ],
        [pltpu.VMEM((SLOT, LEN), BF), pltpu.VMEM((3 * SLOT, LEN), BF)]
        + [pltpu.VMEM((HDIM, LEN), F32)] * 2
        + [pltpu.VMEM((8, TOK, D), BF), pltpu.VMEM((2, 4, SLOT, HALF), BF)]
        + GRADS_ROOM,
        24,
    )


def fourth_kernel(p_ref, chip, tail, r_ref, cent_ref, inv_ref, cols_ref, down_ref, i_ref, v_ref, piece_ref, gdown_ref, near, out, came, whole, exact, parts, found, *sems):
    links = Links(*sems)
    x = links.x
    links.greet(targets(links, "x", "c", "plane"))
    scatter = Scatter(links, p_ref, near, out, came)
    spread = Spread(links, down_ref, gdown_ref)
    whole[:, pl.ds(0, 128)] = chip[0, :, pl.ds(0, 128)]
    whole[:, pl.ds(128, 128)] = chip[1, :, pl.ds(0, 128)]
    whole[:, pl.ds(256, 64)] = jnp.where(x == 3, chip[1, :, pl.ds(128, 64)], tail[...])
    links.stored(links.keep(whole.at[:, pl.ds(pl.multiple_of(16 * x, 16), 272)], exact))
    for k in range(4):
        rows = exact[k].astype(F32)
        for j in range(4):
            parts[j // 2, 2 * k + j % 2] = pack(rows[j * PART : (j + 1) * PART]).astype(BF)
    grads = GradScatter(links, parts, found)
    grads.start()
    scatter.forward()
    spread.turn()
    gains = jnp.concatenate([cols_ref[0], cols_ref[1]], axis=1)
    part, gain, shift = norm_back(scatter.total(), cent_ref[...], inv_ref[...], gains[1:2])
    result = (r_ref[...] + part).T.astype(BF)
    i_ref[0] = result[:HALF]
    i_ref[1] = result[HALF:]
    v_ref[0] = gain
    v_ref[1] = shift
    piece_ref[...] = grads.total()
    links.finish()


def fourth(d_normed, chip, tail, residual, centred, inverse, columns, down_piece):
    return call(
        fourth_kernel,
        "fourth",
        7,
        (d_normed, chip, tail, residual, centred, inverse, columns, down_piece),
        "vvvvvvvv",
        [
            ("v", (2, HALF, TOK), BF),
            ("v", (2, 1, D), F32),
            ("v", (PACKED, 128), BF),
            ("v", PIECES, BF),
        ],
        SCATTER_ROOM + [pltpu.VMEM((4, 320, HALF), BF), pltpu.VMEM((4, 272, HALF), BF)] + GRADS_ROOM,
        16,
    )


WIDE = 1792


def leave_kernel(p_ref, r_ref, i_ref, g_ref, v2_ref, v1_ref, vb_ref, b_ref, gup_ref, oo_ref, io_ref, found, vo_ref, found_up, near, out, came, halves_o, pair_o, pair_i, v_all, v_line, v_own, v_plane, v_sum, *sems):
    links = Links(*sems)
    y, zh, zl, c = links.y, links.zh, links.zl, links.c
    links.greet(targets(links, "line", "plane"))
    scatter = Scatter(links, p_ref, near, out, came)
    v_all[0] = v2_ref[0]
    v_all[1:3] = v1_ref[...]
    v_all[3:6] = v2_ref[1:4]
    v_all[6:8] = vb_ref[...]
    line = [links.push(v_all.at[rank], v_line.at[n], target) for n, (target, rank) in enumerate(links.line())]

    def between_cores(src, pair):
        return links.keep(src.at[c], pair.at[c]), links.push(src.at[1 - c], pair.at[c], links.sibling)

    def to_partner(pair, dst, copies):
        links.stored(copies[0])
        links.arrived(copies[1])
        links.push(pair.at[1 - zh], dst.at[zh], links.partner)
        links.keep(pair.at[zh], dst.at[zh])

    spreads = [Spread(links, gup_ref, found_up), Spread(links, g_ref, found)]
    copies = between_cores(i_ref, pair_i)
    scatter.forward()
    to_partner(pair_i, io_ref, copies)
    for spread in spreads:
        spread.turn()
    total = v_all[links.rank]
    for n, copy in enumerate(line):
        links.arrived(copy)
        total += v_line[n]
    v_own[...] = jnp.zeros_like(v_own)
    v_own[:, :D] = total
    v_own[:, 1152 : 1152 + HALF] = b_ref[...]
    place = (2 * zh + zl) * 4 + y
    kept = links.keep(v_own, v_plane.at[place])
    plane = [links.push(v_own, v_plane.at[place], target) for target, _, _ in links.plane()]
    links.stored(kept)
    for copy in plane:
        links.arrived(copy)
    total = v_plane[0]
    for n in range(1, 16):
        total += v_plane[n]
    v_sum[...] = total
    links.keep(v_sum, vo_ref.at[links.rank])
    for target, _ in links.line():
        links.push(v_sum, vo_ref.at[links.rank], target)
    result = (scatter.total() + r_ref[...]).T.astype(BF)
    halves_o[0] = result[:HALF]
    halves_o[1] = result[HALF:]
    to_partner(pair_o, oo_ref, between_cores(halves_o, pair_o))
    links.finish()


def leave(lowered, residual, in_grad, piece, *vectors, up_piece):
    pair = pltpu.VMEM((2, HALF, TOK), BF)
    return call(
        leave_kernel,
        "leave",
        8,
        (lowered, residual, in_grad, piece, *vectors, up_piece),
        "vvvvvvvvv",
        [
            ("v", (2, HALF, TOK), BF),
            ("v", (2, HALF, TOK), BF),
            ("v", PIECES, BF),
            ("v", (8, 1, WIDE), F32),
            ("v", PIECES, BF),
        ],
        SCATTER_ROOM
        + [pair, pair, pair]
        + [pltpu.VMEM((8, 1, D), F32), pltpu.VMEM((7, 1, D), F32), pltpu.VMEM((1, WIDE), F32)]
        + [pltpu.VMEM((16, 1, WIDE), F32), pltpu.VMEM((1, WIDE), F32)],
        16,
    )


def finish_kernel(o_ref, i_ref, g_ref, up_ref, down_ref, block_ref, in_ref, qkv_ref, out_ref, fup_ref, fdown_ref):
    block_ref[...] = o_ref[...]
    in_ref[...] = i_ref[...].astype(F32)
    for j in range(8):
        rows = slice(PART * (j % 2), PART * (j % 2 + 1))
        piece = unpack(g_ref[j].astype(F32))
        if j < 6:
            qkv_ref[j // 2, rows] = piece
        else:
            out_ref[rows] = piece
        rows = slice(PART * j, PART * (j + 1))
        fup_ref[rows] = unpack(up_ref[j].astype(F32))
        fdown_ref[rows] = unpack(down_ref[j].astype(F32))


def finish(block_out, in_grad, grads, up_grad, down_grad):
    whole = pl.BlockSpec(memory_space=pltpu.VMEM)
    return pl.pallas_call(
        finish_kernel,
        out_shape=(
            jax.ShapeDtypeStruct((2, HALF, TOK), BF),
            jax.ShapeDtypeStruct((2, HALF, TOK), F32),
            jax.ShapeDtypeStruct((3, 136, HALF), F32),
            jax.ShapeDtypeStruct((136, HALF), F32),
            jax.ShapeDtypeStruct((HALF, HALF), F32),
            jax.ShapeDtypeStruct((HALF, HALF), F32),
        ),
        in_specs=[whole] * 5,
        out_specs=(whole,) * 6,
        compiler_params=pltpu.CompilerParams(vmem_limit_bytes=16 << 20),
        name="finish",
    )(block_out, in_grad, grads, up_grad, down_grad)


def per_device(
    block_in,
    query_key_value_weight,
    bias_qv,
    output_weight,
    bias_out,
    gain_one,
    shift_one,
    gain_two,
    shift_two,
    up_weight,
    bias_up,
    down_weight,
    bias_down,
    out_grad,
):
    x, zh, c = (lax.axis_index(a) for a in ("x", "zh", "c"))

    columns = (bias_out, gain_one, shift_one, gain_two, shift_two, bias_down)
    wo4, columns, tail, inputs, normed_one, centred_one, inverse_one, tangent = enter(
        jnp.transpose(block_in, (0, 2, 1)),
        jnp.transpose(out_grad, (0, 2, 1)),
        output_weight,
        query_key_value_weight,
        columns,
    )
    first_rows, wq, tails, qv, bias_up = first(normed_one, query_key_value_weight, tail, bias_qv, bias_up)

    qkv, weight_qkv, mixed, probs, found, tangent_rows, up, wo = attend(
        tangent, first_rows, wq, tails, qv, up_weight.reshape(QUARTERS), wo4
    )
    wo = wo.reshape(2, D, HALF)

    second_rows, down, residual, centred_two, inverse_two = second(
        found, wo, inputs, columns, down_weight.reshape(QUARTERS)
    )
    lowered, d_normed_two, up_grad, down_grad, grad_bias_up = hidden_part(
        second_rows,
        tangent_rows,
        up.reshape(2, HALF, HALF),
        down.reshape(2, HALF, HALF),
        bias_up,
    )
    d_residual, d_attended, d_mixed, sums_two, down_piece = third(
        d_normed_two, down_grad, tangent, centred_two, inverse_two, columns, wo
    )

    up_piece, d_normed_one, chip, tail, bias_sums = back(
        d_mixed, d_attended, qkv, probs, up_grad, mixed, first_rows, weight_qkv
    )
    in_grad, sums_one, piece, down_grad = fourth(
        d_normed_one, chip, tail, d_residual, centred_one, inverse_one, columns, down_piece
    )

    block_out, in_grad, grads, vectors, up_grad = leave(
        lowered, residual, in_grad, piece, sums_two, sums_one, bias_sums, grad_bias_up, up_piece=up_piece
    )
    block_out, in_grad, grad_qkv, grad_out, up_grad, down_grad = finish(block_out, in_grad, grads, up_grad, down_grad)
    row = 2 * x + zh
    vectors = vectors[:, 0]
    grad_bias_up = lax.dynamic_index_in_dim(vectors, row, 0, keepdims=False)[1152 : 1152 + HALF]
    six = lax.dynamic_slice_in_dim(vectors[:6], HALF * c, HALF, 1)
    grad_bias_out, grad_gain_one, grad_shift_one, grad_gain_two, grad_shift_two, grad_bias_down = six
    grad_bias_qv = lax.dynamic_slice_in_dim(vectors[6:], 136 * row, 136, 1)

    return (
        jnp.transpose(block_out, (0, 2, 1)),
        jnp.transpose(in_grad, (0, 2, 1)),
        grad_qkv,
        grad_bias_qv,
        grad_out,
        grad_bias_out,
        grad_gain_one,
        grad_shift_one,
        grad_gain_two,
        grad_shift_two,
        up_grad,
        grad_bias_up,
        down_grad,
        grad_bias_down,
    )


def solution(mesh):
    finer = Mesh(mesh.devices.reshape(2, 4, 4, 2, 2), ALL)
    return jax.shard_map(
        per_device,
        mesh=finer,
        in_specs=(
            P(DP, ROW, "c"),
            P(None, ROW, "c"),
            P(None, ROW),
            P(ROW, "c"),
            P("c"),
            P("c"),
            P("c"),
            P("c"),
            P("c"),
            P(ROW, "c"),
            P(ROW),
            P(ROW, "c"),
            P("c"),
            P(DP, ROW, "c"),
        ),
        out_specs=(
            P(DP, ROW, "c"),
            P(DP, ROW, "c"),
            P(None, ROW, "c"),
            P(None, ROW),
            P(ROW, "c"),
            P("c"),
            P("c"),
            P("c"),
            P("c"),
            P("c"),
            P(ROW, "c"),
            P(ROW),
            P(ROW, "c"),
            P("c"),
        ),
        check_vma=False,
    )
```

```python
import functools

import jax
import jax.numpy as jnp
from jax import lax
from jax.experimental import pallas as pl
from jax.experimental.pallas import tpu as pltpu
from jax.sharding import Mesh
from jax.sharding import PartitionSpec as P


HDIM = 64
D = 1088
HALF = D // 2
TOK = 128
LEN = 1024
SLOT = 192
EPSILON = 1e-05
MASKED = -1e30
DP = ("zl", "y")
ROW = ("x", "zh")
ALL = ("zl", "y", "x", "zh", "c")
MESH = pl.DeviceIdType.MESH
PART = 68
BF = jnp.bfloat16
F32 = jnp.float32


class Links:
    def __init__(self, send, recv, local):
        self.send, self.recv, self.local = send, recv, local
        self.pushed, self.kept = [], []
        self.x, self.c, self.y = lax.axis_index("x"), lax.axis_index("c"), lax.axis_index("y")
        self.zh, self.zl = lax.axis_index("zh"), lax.axis_index("zl")
        self.rank = 2 * self.x + self.c
        self.sibling = {"c": 1 - self.c}
        self.partner = {"zh": 1 - self.zh}

    def along_x(self, k):
        return {"x": lax.rem(self.x + k, 4)}

    def along_y(self, k):
        return {"y": lax.rem(self.y + k, 4)}

    def line(self):
        found = []
        for k, j in ((2, 0), (2, 1), (1, 0), (1, 1), (3, 0), (3, 1), (0, 1)):
            found.append((lax.rem(self.x + k, 4), lax.rem(self.c + j, 2)))
        return [({"x": x, "c": c}, 2 * x + c) for x, c in found]

    def plane(self, both=True):
        found = []
        for h in (1, 0) if both else (0,):
            for l in (1, 0):
                for k in (2, 1, 3, 0):
                    if h or l or k:
                        y, zl = lax.rem(self.y + k, 4), lax.rem(self.zl + l, 2)
                        zh = lax.rem(self.zh + h, 2)
                        found.append(({"y": y, "zl": zl, "zh": zh}, zh, 2 * y + zl))
        return found

    def greet(self, targets):
        barrier = pltpu.get_barrier_semaphore()
        for target in targets:
            pl.semaphore_signal(barrier, inc=1, device_id=target, device_id_type=MESH)
        pl.semaphore_wait(barrier, len(targets))

    def push(self, src, dst, target):
        n = len(self.pushed)
        copy = pltpu.make_async_remote_copy(
            src_ref=src,
            dst_ref=dst,
            send_sem=self.send.at[n],
            recv_sem=self.recv.at[n],
            device_id=target,
            device_id_type=MESH,
        )
        copy.start()
        self.pushed.append([copy, False])
        return n

    def arrived(self, n):
        if not self.pushed[n][1]:
            self.pushed[n][0].wait_recv()
            self.pushed[n][1] = True

    def keep(self, src, dst):
        n = len(self.kept)
        copy = pltpu.make_async_copy(src, dst, self.local.at[n])
        copy.start()
        self.kept.append([copy, False])
        return n

    def stored(self, n):
        if not self.kept[n][1]:
            self.kept[n][0].wait()
            self.kept[n][1] = True

    def finish(self):
        for n in range(len(self.kept)):
            self.stored(n)
        for n in range(len(self.pushed)):
            self.arrived(n)
        for copy, _ in self.pushed:
            copy.wait_send()


SEMS = [pltpu.SemaphoreType.DMA((64,)), pltpu.SemaphoreType.DMA((64,)), pltpu.SemaphoreType.DMA((32,))]
SPACES = {"v": pltpu.VMEM, "h": pltpu.HBM}


def call(kernel, name, cid, args, spaces, outs, scratch=(), mib=12):
    return pl.pallas_call(
        kernel,
        out_shape=tuple(jax.ShapeDtypeStruct(shape, dtype) for _, shape, dtype in outs),
        in_specs=[pl.BlockSpec(memory_space=SPACES[s]) for s in spaces],
        out_specs=tuple(pl.BlockSpec(memory_space=SPACES[s]) for s, _, _ in outs),
        scratch_shapes=[*scratch, *SEMS],
        compiler_params=pltpu.CompilerParams(
            collective_id=cid, has_side_effects=True, vmem_limit_bytes=mib << 20
        ),
        name=name,
    )(*args)


def top(ref):
    return ref.at[pl.ds(0, TOK // 2)]


def bottom(ref):
    return ref.at[pl.ds(TOK // 2, TOK // 2)]


class Gather:
    def __init__(self, links, a_ref, o_ref):
        self.links, self.o = links, o_ref
        own = o_ref.at[links.rank]
        self.kept = links.keep(a_ref, own)
        right, left = links.along_x(1), links.along_x(3)
        self.ahead = [links.push(top(a_ref), top(own), right)]
        self.back = [links.push(bottom(a_ref), bottom(own), left)]
        self.ahead.append(links.push(bottom(a_ref), bottom(own), right))
        self.back.append(links.push(top(a_ref), top(own), left))
        self.near = [links.push(a_ref, own, links.sibling)]

    def slot(self, k):
        return self.o.at[2 * lax.rem(self.links.x + 4 - k, 4) + self.links.c]

    def share(self, piece):
        self.near.append(self.links.push(piece, piece, self.links.sibling))

    def relay(self):
        links = self.links
        links.arrived(self.ahead[0])
        self.far = [links.push(top(self.slot(1)), top(self.slot(1)), links.along_x(1))]
        links.arrived(self.back[0])
        self.far.append(links.push(bottom(self.slot(3)), bottom(self.slot(3)), links.along_x(3)))
        self.share(top(self.slot(1)))
        self.share(bottom(self.slot(3)))

    def middle(self):
        links = self.links
        links.arrived(self.ahead[1])
        self.share(bottom(self.slot(1)))
        links.arrived(self.back[1])
        self.share(top(self.slot(3)))

    def last(self):
        links = self.links
        links.arrived(self.far[0])
        self.share(top(self.slot(2)))
        links.arrived(self.far[1])
        self.share(bottom(self.slot(2)))

    def complete(self):
        self.links.stored(self.kept)
        for copy in self.near:
            self.links.arrived(copy)


class Scatter:
    def __init__(self, links, p_ref, near, out, came):
        self.links, self.p, self.near, self.out, self.came = links, p_ref, near, out, came
        self.swaps = {}
        for k in (2, 1, 3, 0):
            to = lax.rem(links.x + k, 4)
            self.swaps[k] = links.push(p_ref.at[2 * to + 1 - links.c], near.at[k], links.sibling)

    def both(self, k):
        links = self.links
        links.arrived(self.swaps[k])
        to = lax.rem(links.x + k, 4)
        return self.p[2 * to + links.c].astype(F32) + self.near[k].astype(F32)

    def forward(self):
        links, out, came = self.links, self.out, self.came
        right, left = links.along_x(1), links.along_x(3)
        out[2] = self.both(2).astype(BF)
        ahead = links.push(top(out.at[2]), top(came.at[2]), right)
        back = links.push(bottom(out.at[2]), bottom(came.at[2]), left)
        half = TOK // 2
        one = self.both(1)
        out[1, half:] = one[half:].astype(BF)
        self.sends = [links.push(bottom(out.at[1]), bottom(came.at[1]), right)]
        three = self.both(3)
        out[3, :half] = three[:half].astype(BF)
        self.sends.append(links.push(top(out.at[3]), top(came.at[3]), left))
        links.arrived(ahead)
        out[1, :half] = (one[:half] + came[2, :half].astype(F32)).astype(BF)
        self.sends.append(links.push(top(out.at[1]), top(came.at[1]), right))
        links.arrived(back)
        out[3, half:] = (three[half:] + came[2, half:].astype(F32)).astype(BF)
        self.sends.append(links.push(bottom(out.at[3]), bottom(came.at[3]), left))

    def total(self):
        total = self.both(0)
        for copy in self.sends:
            self.links.arrived(copy)
        return total + self.came[1].astype(F32) + self.came[3].astype(F32)


SCATTER_ROOM = [pltpu.VMEM((4, TOK, D), BF)] * 3
PACKED = PART * HALF // 128
PIECES = (8, PACKED, 128)
GRADS_ROOM = [pltpu.VMEM((2, *PIECES), BF), pltpu.VMEM((16, PACKED, 128), BF)]


def pack(rows):
    tiles = [rows[:, 128 * t : 128 * (t + 1)] for t in range(4)]
    rest = jnp.concatenate([rows[17 * q : 17 * (q + 1), 512:] for q in range(4)], axis=1)
    return jnp.concatenate([*tiles, rest], axis=0)


def unpack(piece):
    tiles = [piece[PART * t : PART * (t + 1)] for t in range(4)]
    rest = [piece[4 * PART :, 32 * q : 32 * (q + 1)] for q in range(4)]
    return jnp.concatenate([*tiles, jnp.concatenate(rest, axis=0)], axis=1)


class GradScatter:
    def __init__(self, links, parts, came):
        self.links, self.parts, self.came = links, parts, came

    @staticmethod
    def between_cores(links, own, parts):
        kept = links.keep(own.at[links.c], parts.at[links.c])
        swap = links.push(own.at[1 - links.c], parts.at[links.c], links.sibling)
        return kept, swap

    def start(self):
        self.sends = [
            self.links.push(self.parts.at[zh, piece], self.came.at[n + 1], target)
            for n, (target, zh, piece) in enumerate(self.links.plane())
        ]

    def total(self):
        links = self.links
        total = self.parts[links.zh, 2 * links.y + links.zl].astype(F32)
        for n, send in enumerate(self.sends):
            links.arrived(send)
            total += self.came[n + 1].astype(F32)
        return total.astype(BF)


class Spread:
    def __init__(self, links, piece_ref, o_ref):
        self.links, self.o = links, o_ref
        slot = o_ref.at[2 * links.y + links.zl]
        self.other = links.push(piece_ref, slot, {"zl": 1 - links.zl})
        self.kept = links.keep(piece_ref, slot)
        self.copies = [links.push(piece_ref, slot, links.along_y(k)) for k in (2, 1, 3)]

    def turn(self):
        links = self.links
        links.arrived(self.other)
        slot = self.o.at[2 * links.y + 1 - links.zl]
        self.copies += [links.push(slot, slot, links.along_y(k)) for k in (2, 1, 3)]


def targets(links, *groups):
    found = []
    for group in groups:
        if group == "x":
            found += [links.along_x(k) for k in (1, 2, 3)]
        if group == "y":
            found += [links.along_y(k) for k in (1, 2, 3)]
        if group == "c":
            found.append(links.sibling)
        if group == "z":
            found.append(links.partner)
        if group == "line":
            found += [target for target, _ in links.line()]
        if group == "plane":
            found += [target for target, _, _ in links.plane()]
    return found


def normed(values, gain, shift):
    centre = jnp.mean(values, axis=1, keepdims=True)
    second_moment = jnp.mean(values * values, axis=1, keepdims=True)
    inverse = lax.rsqrt(second_moment - centre * centre + EPSILON)
    centred = (values - centre) * inverse
    return (centred * gain + shift).astype(BF), centred, inverse


def enter_kernel(a_ref, t_ref, wo_ref, w_ref, cols, wo4_ref, colso_ref, tailo_ref, i_ref, n_ref, cent_ref, inv_ref, t32_ref, pair, tpair, tok, ttok, tail, block, *sems):
    links = Links(*sems)
    x, y, zh, c = links.x, links.y, links.zh, links.c
    right, left = lax.rem(x + 1, 4), lax.rem(x + 3, 4)
    diagonal = [{"x": right, "zh": 1 - zh}, {"x": left, "zh": 1 - zh}]
    load = links.keep(w_ref.at[jnp.minimum(y, 2)], block)
    links.greet(targets(links, "x", "c", "z") + diagonal)
    other = links.push(a_ref.at[1 - zh], pair.at[zh], links.partner)
    mine = links.keep(a_ref.at[zh], pair.at[zh])
    t_other = links.push(t_ref.at[1 - zh], tpair.at[zh], links.partner)
    t_mine = links.keep(t_ref.at[zh], tpair.at[zh])
    swap = links.push(cols, colso_ref.at[c], links.sibling)
    own = links.keep(cols, colso_ref.at[c])
    for k in (2, 1, 3):
        links.push(wo_ref, wo4_ref.at[x], links.along_x(k))
    links.keep(wo_ref, wo4_ref.at[x])
    links.stored(load)
    tail[...] = block[88:]
    shifts = [
        pltpu.make_async_remote_copy(
            src_ref=tail,
            dst_ref=tailo_ref,
            send_sem=links.send.at[50 + i],
            recv_sem=links.recv.at[50],
            device_id=target,
            device_id_type=MESH,
        )
        for i, target in enumerate(({"x": right}, diagonal[0]))
    ]

    @pl.when(zh == 1)
    def _():
        for copy in shifts:
            copy.start()

    links.stored(mine)
    links.arrived(other)
    got = links.push(pair.at[1 - c], tok.at[c], links.sibling)
    kept = links.keep(pair.at[c], tok.at[c])
    links.stored(t_mine)
    links.arrived(t_other)
    t_got = links.push(tpair.at[1 - c], ttok.at[c], links.sibling)
    t_kept = links.keep(tpair.at[c], ttok.at[c])
    links.arrived(swap)
    links.stored(own)
    links.stored(kept)
    links.arrived(got)

    def whole(halves):
        return jnp.concatenate([halves[0].astype(F32), halves[1].astype(F32)], axis=0).T

    values = whole(tok)
    i_ref[...] = values
    gains = jnp.concatenate([colso_ref[0], colso_ref[1]], axis=1)
    n_ref[...], cent_ref[...], inv_ref[...] = normed(values, gains[1:2], gains[2:3])
    links.stored(t_kept)
    links.arrived(t_got)
    t32_ref[...] = whole(ttok).astype(BF)
    links.finish()
    shifts[0].wait_recv()

    @pl.when(zh == 1)
    def _():
        for copy in shifts:
            copy.wait_send()


def enter(block_in, out_grad, output_weight, w, columns):
    halves = pltpu.VMEM((2, HALF, TOK), BF)
    return call(
        enter_kernel,
        "enter",
        1,
        (block_in, out_grad, output_weight, w, columns),
        "hhhhv",
        [
            ("v", (4, 136, HALF), BF),
            ("v", (2, 8, HALF), F32),
            ("v", (48, HALF), BF),
            ("v", (TOK, D), F32),
            ("v", (TOK, D), BF),
            ("v", (TOK, D), F32),
            ("v", (TOK, 1), F32),
            ("v", (TOK, D), BF),
        ],
        [halves] * 4
        + [pltpu.VMEM((48, HALF), BF), pltpu.VMEM((136, HALF), BF)],
    )


def first_kernel(n_ref, w_ref, tail_ref, qv_in, cols_ref, o_ref, wq_ref, tails_ref, qvo_ref, b_ref, qv_ref, up_ref, ups, *sems):
    links = Links(*sems)
    x, y, zh, c = links.x, links.y, links.zh, links.c
    right, left = lax.rem(x + 1, 4), lax.rem(x + 3, 4)
    diagonal = [{"x": right, "zh": 1 - zh}, {"x": left, "zh": 1 - zh}]
    load = links.keep(qv_in, qv_ref)
    links.greet(targets(links, "x", "y", "c", "z") + diagonal)
    gather = Gather(links, n_ref, o_ref)
    links.stored(load)
    up_ref[...] = cols_ref[c, 6:7]
    w_other = links.push(w_ref, wq_ref.at[c, zh], links.partner)
    links.keep(w_ref, wq_ref.at[c, zh])
    links.push(w_ref, wq_ref.at[c, zh], links.sibling)
    links.push(qv_ref, qvo_ref.at[zh], links.partner)
    links.keep(qv_ref, qvo_ref.at[zh])
    up_other = links.push(up_ref, ups.at[zh], links.partner)
    up_mine = links.keep(up_ref, ups.at[zh])
    slot = tails_ref.at[c, y]
    links.keep(tail_ref, slot)
    links.push(tail_ref, slot, links.sibling)
    tails = [links.push(tail_ref, slot, links.along_y(k)) for k in (2, 1, 3)]
    shifts = [
        pltpu.make_async_remote_copy(
            src_ref=qv_ref,
            dst_ref=qvo_ref.at[2],
            send_sem=links.send.at[50 + i],
            recv_sem=links.recv.at[50],
            device_id=target,
            device_id_type=MESH,
        )
        for i, target in enumerate(({"x": right}, diagonal[0]))
    ]

    @pl.when(zh == 1)
    def _():
        for copy in shifts:
            copy.start()

    for k, copy in zip((2, 1, 3), tails):
        links.arrived(copy)
        slot = tails_ref.at[c, lax.rem(y + 4 - k, 4)]
        links.push(slot, slot, links.sibling)
    gather.relay()
    links.stored(up_mine)
    links.arrived(up_other)
    b_ref[...] = ups[c]
    gather.middle()
    links.arrived(w_other)
    slot = wq_ref.at[c, 1 - zh]
    links.push(slot, slot, links.sibling)
    gather.last()
    links.finish()
    shifts[0].wait_recv()

    @pl.when(zh == 1)
    def _():
        for copy in shifts:
            copy.wait_send()


def first(normed, w, tail, qv, up):
    return call(
        first_kernel,
        "first",
        2,
        (normed, w, tail, qv, up),
        "vhvhv",
        [
            ("v", (8, TOK, D), BF),
            ("v", (2, 2, 3, 136, HALF), BF),
            ("v", (2, 4, 48, HALF), BF),
            ("v", (3, 2, 136), F32),
            ("v", (1, HALF), F32),
        ],
        [pltpu.VMEM((2, 136), F32), pltpu.VMEM((1, HALF), F32), pltpu.VMEM((2, 1, HALF), F32)],
    )


class WeightBlock:
    def __init__(self, links, w_ref, pair, o_ref):
        self.links, self.pair, self.o = links, pair, o_ref
        self.other = links.push(w_ref.at[links.y], pair.at[links.zh, links.y], links.partner)
        self.kept = links.keep(w_ref, pair.at[links.zh])

    def turn(self):
        links = self.links
        links.arrived(self.other)
        slot = self.pair.at[1 - links.zh, links.y]
        self.round = [links.push(slot, slot, links.along_y(k)) for k in (2, 1, 3)]

    def between_cores(self):
        links = self.links
        links.stored(self.kept)
        for copy in self.round:
            links.arrived(copy)
        links.push(self.pair.at[1 - links.c], self.o.at[links.c], links.sibling)
        links.keep(self.pair.at[links.c], self.o.at[links.c])


QUARTERS = (4, 136, HALF)

BLOCK = 256


def dot(a, b, dims):
    return lax.dot_general(a, b, (dims, ((), ())), preferred_element_type=F32)


def attend_head(qkv_ref, h, m_ref, p_ref):
    keys = lax.broadcasted_iota(jnp.int32, (BLOCK, BLOCK), 0)
    queries = lax.broadcasted_iota(jnp.int32, (BLOCK, BLOCK), 1)
    head = pl.ds(h * HDIM, HDIM)
    for i in range(LEN // BLOCK):
        low, high = i * BLOCK, (i + 1) * BLOCK
        q = qkv_ref[0, head, low:high] * BF(HDIM**-0.5)
        parts = [dot(qkv_ref[1, head, low:high], q, ((0,), (0,)))]
        parts[0] = jnp.where(keys <= queries, parts[0], MASKED)
        if i:
            parts.insert(0, dot(qkv_ref[1, head, :low], q, ((0,), (0,))))
        highest = functools.reduce(jnp.maximum, [jnp.max(s, axis=0, keepdims=True) for s in parts])
        parts = [jnp.exp(s - highest) for s in parts]
        share = 1.0 / sum(jnp.sum(s, axis=0, keepdims=True) for s in parts)
        parts = [(s * share).astype(BF) for s in parts]
        p_ref[h, low:high, low:high] = parts[-1]
        mixed = dot(qkv_ref[2, head, low:high], parts[-1], ((1,), (0,)))
        if i:
            p_ref[h, :low, low:high] = parts[0]
            mixed += dot(qkv_ref[2, head, :low], parts[0], ((1,), (0,)))
        m_ref[head, low:high] = mixed.astype(BF)


def attend_kernel(t_ref, n_ref, wq_ref, tails_ref, qv_ref, up_ref, wo4_ref, qkv_ref, w_ref, m_ref, p_ref, f_ref, o_ref, upo_ref, woo_ref, room, pair, mid, *sems):
    links = Links(*sems)
    x, y, zh, c = links.x, links.y, links.zh, links.c
    links.greet(targets(links, "line", "y", "z"))
    wo_own = links.push(wo4_ref.at[y], mid, links.partner)
    gather = Gather(links, t_ref, o_ref)
    weight = WeightBlock(links, up_ref, pair, upo_ref)
    links.keep(wo4_ref, woo_ref.at[c, :, zh])
    links.push(wo4_ref, woo_ref.at[c, :, zh], links.sibling)
    n = n_ref[...].reshape(LEN, D)
    last = links.rank == 7
    start = pl.multiple_of(48 - 16 * x + 128 * c, 16)
    parts = [qv_ref[2][:, 88:], qv_ref[0], qv_ref[1], jnp.zeros((2, 64), F32)]
    bias = jnp.concatenate([jnp.concatenate(parts, axis=1), jnp.zeros((6, 384), F32)], axis=0)
    bias = pltpu.roll(bias, 384 - start, 1)[:, :256].T[:SLOT]
    real = jnp.logical_or(lax.broadcasted_iota(jnp.int32, (SLOT, 1), 0) < 128, last)
    bias = [jnp.where(real, bias[:, 0:1], 0.0), 0.0, jnp.where(real, bias[:, 1:2], 0.0)]
    for k in range(3):
        for h in range(2):
            columns = slice(h * HALF, (h + 1) * HALF)
            rows = [tails_ref[h, k], wq_ref[h, 0, k], wq_ref[h, 1, k], jnp.zeros((48, HALF), BF)]
            room[:, columns] = jnp.concatenate([r.astype(F32) for r in rows], axis=0)
        mine = room[pl.ds(start, SLOT)].astype(BF)
        low = slice(k * SLOT, k * SLOT + 128)
        high = slice(k * SLOT + 128, (k + 1) * SLOT)
        w_ref[low] = mine[:128]
        w_ref[high] = jnp.where(last, mine[128:], BF(0))
        rows = slice(k * SLOT, (k + 1) * SLOT)
        qkv_ref[k] = (dot(w_ref[rows], n, ((1,), (1,))) + bias[k]).astype(BF)
    gather.relay()
    links.arrived(wo_own)
    slot = woo_ref.at[c, y, 1 - zh]
    links.keep(mid, slot)
    round_y = [links.push(mid, slot, links.along_y(k)) for k in (2, 1, 3)]
    links.push(mid, slot, links.sibling)
    for h in range(SLOT // HDIM):
        attend_head(qkv_ref, h, m_ref, p_ref)
        if h == 0:
            weight.turn()
        if h == 1:
            gather.middle()
    own = links.rank
    columns = pl.ds(pl.multiple_of(own * TOK, TOK), TOK)
    links.keep(m_ref.at[:, columns], f_ref.at[own])
    for target, rank in links.line():
        columns = pl.ds(pl.multiple_of(rank * TOK, TOK), TOK)
        links.push(m_ref.at[:, columns], f_ref.at[own], target)
    for k, copy in zip((2, 1, 3), round_y):
        links.arrived(copy)
        slot = woo_ref.at[c, lax.rem(y + 4 - k, 4), 1 - zh]
        links.push(slot, slot, links.sibling)
    gather.last()
    weight.between_cores()
    links.finish()


def attend(tangent, rows, wq, tails, bias, up, wo4):
    return call(
        attend_kernel,
        "attend",
        3,
        (tangent, rows, wq, tails, bias, up, wo4),
        "vvvvvhv",
        [
            ("v", (3, SLOT, LEN), BF),
            ("v", (3 * SLOT, D), BF),
            ("v", (SLOT, LEN), BF),
            ("v", (SLOT // HDIM, LEN, LEN), BF),
            ("v", (8, SLOT, TOK), BF),
            ("v", (8, TOK, D), BF),
            ("v", (2, *QUARTERS), BF),
            ("v", (2, 4, 2, 136, HALF), BF),
        ],
        [pltpu.VMEM((368, D), F32), pltpu.VMEM((2, *QUARTERS), BF), pltpu.VMEM((136, HALF), BF)],
        20,
    )


def second_kernel(f_ref, wo_ref, i_ref, cols_ref, down_ref, o_ref, downo_ref, r_ref, cent_ref, inv_ref, m_ref, n, pair, *sems):
    links = Links(*sems)
    links.greet(targets(links, "x", "y", "c", "z"))
    weight = WeightBlock(links, down_ref, pair, downo_ref)
    for rank in range(7):
        m_ref[128 * rank : 128 * (rank + 1)] = f_ref[rank, :128]
    m_ref[896:] = f_ref[7]
    columns = jnp.concatenate([cols_ref[0], cols_ref[1]], axis=1)
    attended = [dot(m_ref[...], wo_ref[h], ((0,), (0,))) for h in range(2)]
    residual = i_ref[...] + (jnp.concatenate(attended, axis=1) + columns[0:1])
    r_ref[...] = residual + columns[5:6]
    n[...], cent_ref[...], inv_ref[...] = normed(residual, columns[3:4], columns[4:5])
    gather = Gather(links, n, o_ref)
    weight.turn()
    gather.relay()
    gather.middle()
    weight.between_cores()
    gather.last()
    links.finish()


def second(found, wo, inputs, columns, down):
    return call(
        second_kernel,
        "second",
        4,
        (found, wo, inputs, columns, down),
        "vvvvh",
        [
            ("v", (8, TOK, D), BF),
            ("v", (2, *QUARTERS), BF),
            ("v", (TOK, D), F32),
            ("v", (TOK, D), F32),
            ("v", (TOK, 1), F32),
        ],
        [pltpu.VMEM((D, TOK), BF), pltpu.VMEM((TOK, D), BF), pltpu.VMEM((2, *QUARTERS), BF)],
    )


STEP = 512


def hidden_kernel(n_ref, t_ref, up_ref, down_ref, b_ref, low_ref, dn_ref, gup_ref, gdown_ref, gb_ref, up, down, up_sum, down_sum):
    step = pl.program_id(0)

    @pl.when(step == 0)
    def _():
        for h in range(2):
            up[:, h * HALF : (h + 1) * HALF] = up_ref[h]
            down[:, h * HALF : (h + 1) * HALF] = down_ref[h]
        up_sum[...] = jnp.zeros_like(up_sum)
        down_sum[...] = jnp.zeros_like(down_sum)
        gb_ref[...] = jnp.zeros_like(gb_ref)

    n = n_ref[...].reshape(STEP, D)
    t = t_ref[...].reshape(STEP, D)
    pre = dot(n, up[...], ((1,), (1,))) + b_ref[...]
    cumulative = 0.5 * (1.0 + lax.erf(pre * 0.7071067811865476))
    density = jnp.exp(-0.5 * pre * pre) * 0.3989422804014327
    active = (pre * cumulative).astype(BF)
    slope = cumulative + pre * density
    low_ref[...] = dot(active, down[...], ((1,), (0,))).astype(BF).reshape(low_ref.shape)
    d_pre = (dot(t, down[...], ((1,), (1,))) * slope).astype(BF)
    dn_ref[...] = dot(d_pre, up[...], ((1,), (0,))).astype(BF).reshape(dn_ref.shape)
    down_sum[...] += dot(active, t, ((0,), (0,)))
    up_sum[...] += dot(d_pre, n, ((0,), (0,)))
    gb_ref[...] += jnp.sum(d_pre.astype(F32), axis=0, keepdims=True)

    @pl.when(step == pl.num_programs(0) - 1)
    def _():
        for h in range(2):
            for out, total in ((gup_ref, up_sum), (gdown_ref, down_sum)):
                for j in range(8):
                    out[h, j] = pack(total[j * PART : (j + 1) * PART, h * HALF : (h + 1) * HALF]).astype(BF)


def hidden_part(second_rows, tangent_rows, up, down, bias):
    rows = pl.BlockSpec((STEP // TOK, TOK, D), lambda i: (i, 0, 0))
    weight = pl.BlockSpec((2, HALF, HALF), lambda i: (0, 0, 0))
    grad = pl.BlockSpec((2, *PIECES), lambda i: (0, 0, 0, 0))
    one = pl.BlockSpec((1, HALF), lambda i: (0, 0))
    return pl.pallas_call(
        hidden_kernel,
        grid=(LEN // STEP,),
        in_specs=[rows, rows, weight, weight, one],
        out_specs=(rows, rows, grad, grad, one),
        out_shape=(
            jax.ShapeDtypeStruct((8, TOK, D), BF),
            jax.ShapeDtypeStruct((8, TOK, D), BF),
            jax.ShapeDtypeStruct((2, *PIECES), BF),
            jax.ShapeDtypeStruct((2, *PIECES), BF),
            jax.ShapeDtypeStruct((1, HALF), F32),
        ),
        scratch_shapes=[pltpu.VMEM((HALF, D), BF)] * 2 + [pltpu.VMEM((HALF, D), F32)] * 2,
        compiler_params=pltpu.CompilerParams(vmem_limit_bytes=32 << 20),
        name="hidden_part",
    )(second_rows, tangent_rows, up, down, bias)


def norm_back(upstream, centred, inverse, gain):
    scaled = upstream * gain
    result = inverse * (
        scaled
        - jnp.mean(scaled, axis=1, keepdims=True)
        - centred * jnp.mean(scaled * centred, axis=1, keepdims=True)
    )
    return result, jnp.sum(upstream * centred, axis=0, keepdims=True), jnp.sum(upstream, axis=0, keepdims=True)


def third_kernel(p_ref, g_ref, t_ref, cent_ref, inv_ref, cols_ref, wo_ref, d_ref, a_ref, dm_ref, v_ref, piece_ref, near, out, came, parts, found, *sems):
    links = Links(*sems)
    links.greet(targets(links, "x", "c", "plane"))
    grads = GradScatter(links, parts, found)
    kept, swap = grads.between_cores(links, g_ref, parts)
    scatter = Scatter(links, p_ref, near, out, came)
    links.stored(kept)
    links.arrived(swap)
    grads.start()
    scatter.forward()
    gains = jnp.concatenate([cols_ref[0], cols_ref[1]], axis=1)
    part, gain, shift = norm_back(scatter.total(), cent_ref[...], inv_ref[...], gains[3:4])
    tangent = t_ref[...].astype(F32)
    d_residual = tangent + part
    d_ref[...] = d_residual
    rounded = d_residual.astype(BF)
    a_ref[...] = rounded
    d_mixed = [dot(wo_ref[h], rounded[:, h * HALF : (h + 1) * HALF], ((1,), (1,))) for h in range(2)]
    dm_ref[...] = (d_mixed[0] + d_mixed[1]).astype(BF)
    v_ref[0] = jnp.sum(d_residual.astype(BF).astype(F32), axis=0, keepdims=True)
    v_ref[1] = gain
    v_ref[2] = shift
    v_ref[3] = jnp.sum(tangent, axis=0, keepdims=True)
    piece_ref[...] = grads.total()
    links.finish()


def third(d_normed, grad, tangent, centred, inverse, gain, wo):
    return call(
        third_kernel,
        "third",
        5,
        (d_normed, grad, tangent, centred, inverse, gain, wo),
        "vvvvvvv",
        [
            ("v", (TOK, D), F32),
            ("v", (TOK, D), BF),
            ("v", (D, TOK), BF),
            ("v", (4, 1, D), F32),
            ("v", (PACKED, 128), BF),
        ],
        SCATTER_ROOM + GRADS_ROOM,
        16,
    )


def attend_back_head(qkv_ref, h, u_ref, p_ref, d_ref, dk_sum, dv_sum):
    head = pl.ds(h * HDIM, HDIM)
    for i in range(LEN // BLOCK):
        low, high = i * BLOCK, (i + 1) * BLOCK
        q = qkv_ref[0, head, low:high] * BF(HDIM**-0.5)
        u = u_ref[head, low:high]
        p = p_ref[h, :high, low:high]
        wide = p.astype(F32)
        dp = dot(qkv_ref[2, head, :high], u, ((0,), (0,)))
        centre = jnp.sum(wide * dp, axis=0, keepdims=True)
        ds = (wide * (dp - centre)).astype(BF)
        d_ref[head, low:high] = (dot(qkv_ref[1, head, :high], ds, ((1,), (0,))) * HDIM**-0.5).astype(BF)
        dk = dot(q, ds, ((1,), (1,)))
        dv = dot(u, p, ((1,), (1,)))
        if i:
            dk_sum[:, :low] += dk[:, :low]
            dv_sum[:, :low] += dv[:, :low]
        dk_sum[:, low:high] = dk[:, low:]
        dv_sum[:, low:high] = dv[:, low:]
    d_ref[pl.ds(SLOT + h * HDIM, HDIM)] = dk_sum[...].astype(BF)
    d_ref[pl.ds(2 * SLOT + h * HDIM, HDIM)] = dv_sum[...].astype(BF)


def back_kernel(m_ref, a_ref, qkv_ref, p_ref, g_ref, mixed_ref, n_ref, w_ref, piece_ref, dn_ref, chip_ref, tail_ref, vb_ref, u, d, dk_sum, dv_sum, o, own_grads, parts, found, *sems):
    links = Links(*sems)
    c = links.c
    links.greet(targets(links, "line", "plane"))
    own = links.rank
    columns = pl.ds(pl.multiple_of(own * TOK, TOK), TOK)

    def rows(rank):
        return pl.ds(pl.multiple_of(rank * 2 * HDIM, 2 * HDIM), SLOT)

    mine = links.keep(m_ref.at[rows(own)], u.at[:, columns])
    others = [links.push(m_ref.at[rows(rank)], u.at[:, columns], target) for target, rank in links.line()]
    gather = Gather(links, a_ref, o)
    grads = GradScatter(links, parts, found)
    kept, swap = grads.between_cores(links, g_ref, parts)
    links.stored(kept)
    links.arrived(swap)
    grads.start()
    links.stored(mine)
    for copy in others:
        links.arrived(copy)
    n = n_ref[...].reshape(LEN, D)

    def weight_grad(left, right, k, rows):
        grad = dot(left, right, ((1,), (0,)))
        for h in range(2):
            own_grads[h, k, rows] = grad[:, h * HALF : (h + 1) * HALF].astype(BF)

    def between_cores(which):
        kept = links.keep(own_grads.at[(c, *which)], chip_ref.at[(c, *which)])
        return kept, links.push(own_grads.at[(1 - c, *which)], chip_ref.at[(c, *which)], links.sibling)

    def done(copies):
        links.stored(copies[0])
        links.arrived(copies[1])

    attend_back_head(qkv_ref, 0, u, p_ref, d, dk_sum, dv_sum)
    gather.relay()
    for k in range(3):
        weight_grad(d[k * SLOT : k * SLOT + HDIM], n, k, slice(0, HDIM))
    first_rows = between_cores((pl.ds(0, 3), pl.ds(0, HDIM)))
    attend_back_head(qkv_ref, 1, u, p_ref, d, dk_sum, dv_sum)
    done(first_rows)
    links.push(chip_ref.at[0, pl.ds(0, 3), pl.ds(0, HDIM)], tail_ref.at[pl.ds(0, 3)], links.along_x(3))
    gather.middle()
    attend_back_head(qkv_ref, 2, u, p_ref, d, dk_sum, dv_sum)
    gather.last()
    for k in range(3):
        weight_grad(d[k * SLOT + HDIM : (k + 1) * SLOT], n, k, slice(HDIM, SLOT))
    between_cores((pl.ds(0, 3), pl.ds(HDIM, SLOT - HDIM)))
    gather.complete()
    weight_grad(mixed_ref[...], o[...].reshape(LEN, D), 3, slice(0, SLOT))
    out_rows = between_cores((3,))
    for i in range(LEN // BLOCK):
        block = dot(d[:, i * BLOCK : (i + 1) * BLOCK], w_ref[...], ((0,), (0,))).astype(BF)
        dn_ref[2 * i : 2 * i + 2] = block.reshape(2, TOK, D)
        if i == 0:
            done(out_rows)
            links.push(chip_ref.at[0, 3, pl.ds(0, HDIM)], tail_ref.at[3], links.along_x(3))
    ones = jnp.ones((8, LEN), BF)
    vb_ref[...] = jnp.zeros_like(vb_ref)
    real = jnp.logical_or(lax.broadcasted_iota(jnp.int32, (1, SLOT), 1) < 128, own == 7)
    for i, k in enumerate((0, 2)):
        total = dot(ones, d[k * SLOT : (k + 1) * SLOT], ((1,), (1,)))[0:1]
        vb_ref[i, :, pl.ds(pl.multiple_of(own * 128, 128), SLOT)] = jnp.where(real, total, 0.0)
    piece_ref[...] = grads.total()
    links.finish()


def back(d_mixed, d_attended, qkv, probs, grad, mixed, rows, weight):
    return call(
        back_kernel,
        "back",
        6,
        (d_mixed, d_attended, qkv, probs, grad, mixed, rows, weight),
        "vvvvvvvv",
        [
            ("v", (PACKED, 128), BF),
            ("v", (8, TOK, D), BF),
            ("v", (2, 4, SLOT, HALF), BF),
            ("v", (4, HDIM, HALF), BF),
            ("v", (2, 1, D), F32),
        ],
        [pltpu.VMEM((SLOT, LEN), BF), pltpu.VMEM((3 * SLOT, LEN), BF)]
        + [pltpu.VMEM((HDIM, LEN), F32)] * 2
        + [pltpu.VMEM((8, TOK, D), BF), pltpu.VMEM((2, 4, SLOT, HALF), BF)]
        + GRADS_ROOM,
        24,
    )


def fourth_kernel(p_ref, chip, tail, r_ref, cent_ref, inv_ref, cols_ref, down_ref, i_ref, v_ref, piece_ref, gdown_ref, near, out, came, whole, exact, parts, found, *sems):
    links = Links(*sems)
    x = links.x
    links.greet(targets(links, "x", "c", "plane"))
    scatter = Scatter(links, p_ref, near, out, came)
    spread = Spread(links, down_ref, gdown_ref)
    whole[:, pl.ds(0, 128)] = chip[0, :, pl.ds(0, 128)]
    whole[:, pl.ds(128, 128)] = chip[1, :, pl.ds(0, 128)]
    whole[:, pl.ds(256, 64)] = jnp.where(x == 3, chip[1, :, pl.ds(128, 64)], tail[...])
    links.stored(links.keep(whole.at[:, pl.ds(pl.multiple_of(16 * x, 16), 272)], exact))
    for k in range(4):
        rows = exact[k].astype(F32)
        for j in range(4):
            parts[j // 2, 2 * k + j % 2] = pack(rows[j * PART : (j + 1) * PART]).astype(BF)
    grads = GradScatter(links, parts, found)
    grads.start()
    scatter.forward()
    spread.turn()
    gains = jnp.concatenate([cols_ref[0], cols_ref[1]], axis=1)
    part, gain, shift = norm_back(scatter.total(), cent_ref[...], inv_ref[...], gains[1:2])
    result = (r_ref[...] + part).T.astype(BF)
    i_ref[0] = result[:HALF]
    i_ref[1] = result[HALF:]
    v_ref[0] = gain
    v_ref[1] = shift
    piece_ref[...] = grads.total()
    links.finish()


def fourth(d_normed, chip, tail, residual, centred, inverse, columns, down_piece):
    return call(
        fourth_kernel,
        "fourth",
        7,
        (d_normed, chip, tail, residual, centred, inverse, columns, down_piece),
        "vvvvvvvv",
        [
            ("v", (2, HALF, TOK), BF),
            ("v", (2, 1, D), F32),
            ("v", (PACKED, 128), BF),
            ("v", PIECES, BF),
        ],
        SCATTER_ROOM + [pltpu.VMEM((4, 320, HALF), BF), pltpu.VMEM((4, 272, HALF), BF)] + GRADS_ROOM,
        16,
    )


WIDE = 1792


def leave_kernel(p_ref, r_ref, i_ref, g_ref, v2_ref, v1_ref, vb_ref, b_ref, gup_ref, oo_ref, io_ref, found, vo_ref, found_up, near, out, came, halves_o, pair_o, pair_i, v_all, v_line, v_own, v_plane, v_sum, *sems):
    links = Links(*sems)
    y, zh, zl, c = links.y, links.zh, links.zl, links.c
    links.greet(targets(links, "line", "plane"))
    scatter = Scatter(links, p_ref, near, out, came)
    v_all[0] = v2_ref[0]
    v_all[1:3] = v1_ref[...]
    v_all[3:6] = v2_ref[1:4]
    v_all[6:8] = vb_ref[...]
    line = [links.push(v_all.at[rank], v_line.at[n], target) for n, (target, rank) in enumerate(links.line())]

    def between_cores(src, pair):
        return links.keep(src.at[c], pair.at[c]), links.push(src.at[1 - c], pair.at[c], links.sibling)

    def to_partner(pair, dst, copies):
        links.stored(copies[0])
        links.arrived(copies[1])
        links.push(pair.at[1 - zh], dst.at[zh], links.partner)
        links.keep(pair.at[zh], dst.at[zh])

    spreads = [Spread(links, gup_ref, found_up), Spread(links, g_ref, found)]
    copies = between_cores(i_ref, pair_i)
    scatter.forward()
    to_partner(pair_i, io_ref, copies)
    for spread in spreads:
        spread.turn()
    total = v_all[links.rank]
    for n, copy in enumerate(line):
        links.arrived(copy)
        total += v_line[n]
    v_own[...] = jnp.zeros_like(v_own)
    v_own[:, :D] = total
    v_own[:, 1152 : 1152 + HALF] = b_ref[...]
    place = (2 * zh + zl) * 4 + y
    kept = links.keep(v_own, v_plane.at[place])
    plane = [links.push(v_own, v_plane.at[place], target) for target, _, _ in links.plane()]
    links.stored(kept)
    for copy in plane:
        links.arrived(copy)
    total = v_plane[0]
    for n in range(1, 16):
        total += v_plane[n]
    v_sum[...] = total
    links.keep(v_sum, vo_ref.at[links.rank])
    for target, _ in links.line():
        links.push(v_sum, vo_ref.at[links.rank], target)
    result = (scatter.total() + r_ref[...]).T.astype(BF)
    halves_o[0] = result[:HALF]
    halves_o[1] = result[HALF:]
    to_partner(pair_o, oo_ref, between_cores(halves_o, pair_o))
    links.finish()


def leave(lowered, residual, in_grad, piece, *vectors, up_piece):
    pair = pltpu.VMEM((2, HALF, TOK), BF)
    return call(
        leave_kernel,
        "leave",
        8,
        (lowered, residual, in_grad, piece, *vectors, up_piece),
        "vvvvvvvvv",
        [
            ("v", (2, HALF, TOK), BF),
            ("v", (2, HALF, TOK), BF),
            ("v", PIECES, BF),
            ("v", (8, 1, WIDE), F32),
            ("v", PIECES, BF),
        ],
        SCATTER_ROOM
        + [pair, pair, pair]
        + [pltpu.VMEM((8, 1, D), F32), pltpu.VMEM((7, 1, D), F32), pltpu.VMEM((1, WIDE), F32)]
        + [pltpu.VMEM((16, 1, WIDE), F32), pltpu.VMEM((1, WIDE), F32)],
        16,
    )


def finish_kernel(o_ref, i_ref, g_ref, up_ref, down_ref, block_ref, in_ref, qkv_ref, out_ref, fup_ref, fdown_ref):
    block_ref[...] = o_ref[...]
    in_ref[...] = i_ref[...].astype(F32)
    for j in range(8):
        rows = slice(PART * (j % 2), PART * (j % 2 + 1))
        piece = unpack(g_ref[j].astype(F32))
        if j < 6:
            qkv_ref[j // 2, rows] = piece
        else:
            out_ref[rows] = piece
        rows = slice(PART * j, PART * (j + 1))
        fup_ref[rows] = unpack(up_ref[j].astype(F32))
        fdown_ref[rows] = unpack(down_ref[j].astype(F32))


def finish(block_out, in_grad, grads, up_grad, down_grad):
    whole = pl.BlockSpec(memory_space=pltpu.VMEM)
    return pl.pallas_call(
        finish_kernel,
        out_shape=(
            jax.ShapeDtypeStruct((2, HALF, TOK), BF),
            jax.ShapeDtypeStruct((2, HALF, TOK), F32),
            jax.ShapeDtypeStruct((3, 136, HALF), F32),
            jax.ShapeDtypeStruct((136, HALF), F32),
            jax.ShapeDtypeStruct((HALF, HALF), F32),
            jax.ShapeDtypeStruct((HALF, HALF), F32),
        ),
        in_specs=[whole] * 5,
        out_specs=(whole,) * 6,
        compiler_params=pltpu.CompilerParams(vmem_limit_bytes=16 << 20),
        name="finish",
    )(block_out, in_grad, grads, up_grad, down_grad)


def per_device(
    block_in,
    query_key_value_weight,
    bias_qv,
    output_weight,
    bias_out,
    gain_one,
    shift_one,
    gain_two,
    shift_two,
    up_weight,
    bias_up,
    down_weight,
    bias_down,
    out_grad,
):
    x, zh, c = (lax.axis_index(a) for a in ("x", "zh", "c"))

    place = lax.broadcasted_iota(jnp.int32, (8, HALF), 0)
    columns = jnp.zeros((8, HALF), F32)
    for i, vector in enumerate((bias_out, gain_one, shift_one, gain_two, shift_two, bias_down, bias_up)):
        columns = jnp.where(place == i, vector[None], columns)
    wo4, columns, tail, inputs, normed_one, centred_one, inverse_one, tangent = enter(
        jnp.transpose(block_in, (0, 2, 1)),
        jnp.transpose(out_grad, (0, 2, 1)),
        output_weight,
        query_key_value_weight,
        columns,
    )
    first_rows, wq, tails, qv, bias_up = first(normed_one, query_key_value_weight, tail, bias_qv, columns)

    qkv, weight_qkv, mixed, probs, found, tangent_rows, up, wo = attend(
        tangent, first_rows, wq, tails, qv, up_weight.reshape(QUARTERS), wo4
    )
    wo = wo.reshape(2, D, HALF)

    second_rows, down, residual, centred_two, inverse_two = second(
        found, wo, inputs, columns, down_weight.reshape(QUARTERS)
    )
    lowered, d_normed_two, up_grad, down_grad, grad_bias_up = hidden_part(
        second_rows,
        tangent_rows,
        up.reshape(2, HALF, HALF),
        down.reshape(2, HALF, HALF),
        bias_up,
    )
    d_residual, d_attended, d_mixed, sums_two, down_piece = third(
        d_normed_two, down_grad, tangent, centred_two, inverse_two, columns, wo
    )

    up_piece, d_normed_one, chip, tail, bias_sums = back(
        d_mixed, d_attended, qkv, probs, up_grad, mixed, first_rows, weight_qkv
    )
    in_grad, sums_one, piece, down_grad = fourth(
        d_normed_one, chip, tail, d_residual, centred_one, inverse_one, columns, down_piece
    )

    block_out, in_grad, grads, vectors, up_grad = leave(
        lowered, residual, in_grad, piece, sums_two, sums_one, bias_sums, grad_bias_up, up_piece=up_piece
    )
    block_out, in_grad, grad_qkv, grad_out, up_grad, down_grad = finish(block_out, in_grad, grads, up_grad, down_grad)
    row = 2 * x + zh
    vectors = vectors[:, 0]
    grad_bias_up = lax.dynamic_index_in_dim(vectors, row, 0, keepdims=False)[1152 : 1152 + HALF]
    six = lax.dynamic_slice_in_dim(vectors[:6], HALF * c, HALF, 1)
    grad_bias_out, grad_gain_one, grad_shift_one, grad_gain_two, grad_shift_two, grad_bias_down = six
    grad_bias_qv = lax.dynamic_slice_in_dim(vectors[6:], 136 * row, 136, 1)

    return (
        jnp.transpose(block_out, (0, 2, 1)),
        jnp.transpose(in_grad, (0, 2, 1)),
        grad_qkv,
        grad_bias_qv,
        grad_out,
        grad_bias_out,
        grad_gain_one,
        grad_shift_one,
        grad_gain_two,
        grad_shift_two,
        up_grad,
        grad_bias_up,
        down_grad,
        grad_bias_down,
    )


def solution(mesh):
    finer = Mesh(mesh.devices.reshape(2, 4, 4, 2, 2), ALL)
    return jax.shard_map(
        per_device,
        mesh=finer,
        in_specs=(
            P(DP, ROW, "c"),
            P(None, ROW, "c"),
            P(None, ROW),
            P(ROW, "c"),
            P("c"),
            P("c"),
            P("c"),
            P("c"),
            P("c"),
            P(ROW, "c"),
            P(ROW),
            P(ROW, "c"),
            P("c"),
            P(DP, ROW, "c"),
        ),
        out_specs=(
            P(DP, ROW, "c"),
            P(DP, ROW, "c"),
            P(None, ROW, "c"),
            P(None, ROW),
            P(ROW, "c"),
            P("c"),
            P("c"),
            P("c"),
            P("c"),
            P("c"),
            P(ROW, "c"),
            P(ROW),
            P(ROW, "c"),
            P("c"),
        ),
        check_vma=False,
    )
```

```python
import functools

import jax
import jax.numpy as jnp
from jax import lax
from jax.experimental import pallas as pl
from jax.experimental.pallas import tpu as pltpu
from jax.sharding import Mesh
from jax.sharding import PartitionSpec as P


HDIM = 64
D = 1088
HALF = D // 2
TOK = 128
LEN = 1024
SLOT = 192
EPSILON = 1e-05
MASKED = -1e30
DP = ("zl", "y")
ROW = ("x", "zh")
ALL = ("zl", "y", "x", "zh", "c")
MESH = pl.DeviceIdType.MESH
PART = 68
BF = jnp.bfloat16
F32 = jnp.float32


class Links:
    def __init__(self, send, recv, local):
        self.send, self.recv, self.local = send, recv, local
        self.pushed, self.kept = [], []
        self.x, self.c, self.y = lax.axis_index("x"), lax.axis_index("c"), lax.axis_index("y")
        self.zh, self.zl = lax.axis_index("zh"), lax.axis_index("zl")
        self.rank = 2 * self.x + self.c
        self.sibling = {"c": 1 - self.c}
        self.partner = {"zh": 1 - self.zh}

    def along_x(self, k):
        return {"x": lax.rem(self.x + k, 4)}

    def along_y(self, k):
        return {"y": lax.rem(self.y + k, 4)}

    def line(self):
        found = []
        for k, j in ((2, 0), (2, 1), (1, 0), (1, 1), (3, 0), (3, 1), (0, 1)):
            found.append((lax.rem(self.x + k, 4), lax.rem(self.c + j, 2)))
        return [({"x": x, "c": c}, 2 * x + c) for x, c in found]

    def plane(self, both=True):
        found = []
        for h in (1, 0) if both else (0,):
            for l in (1, 0):
                for k in (2, 1, 3, 0):
                    if h or l or k:
                        y, zl = lax.rem(self.y + k, 4), lax.rem(self.zl + l, 2)
                        zh = lax.rem(self.zh + h, 2)
                        found.append(({"y": y, "zl": zl, "zh": zh}, zh, 2 * y + zl))
        return found

    def greet(self, targets):
        barrier = pltpu.get_barrier_semaphore()
        for target in targets:
            pl.semaphore_signal(barrier, inc=1, device_id=target, device_id_type=MESH)
        pl.semaphore_wait(barrier, len(targets))

    def push(self, src, dst, target):
        n = len(self.pushed)
        copy = pltpu.make_async_remote_copy(
            src_ref=src,
            dst_ref=dst,
            send_sem=self.send.at[n],
            recv_sem=self.recv.at[n],
            device_id=target,
            device_id_type=MESH,
        )
        copy.start()
        self.pushed.append([copy, False])
        return n

    def arrived(self, n):
        if not self.pushed[n][1]:
            self.pushed[n][0].wait_recv()
            self.pushed[n][1] = True

    def keep(self, src, dst):
        n = len(self.kept)
        copy = pltpu.make_async_copy(src, dst, self.local.at[n])
        copy.start()
        self.kept.append([copy, False])
        return n

    def stored(self, n):
        if not self.kept[n][1]:
            self.kept[n][0].wait()
            self.kept[n][1] = True

    def finish(self):
        for n in range(len(self.kept)):
            self.stored(n)
        for n in range(len(self.pushed)):
            self.arrived(n)
        for copy, _ in self.pushed:
            copy.wait_send()


SEMS = [pltpu.SemaphoreType.DMA((64,)), pltpu.SemaphoreType.DMA((64,)), pltpu.SemaphoreType.DMA((32,))]
SPACES = {"v": pltpu.VMEM, "h": pltpu.HBM}


def call(kernel, name, cid, args, spaces, outs, scratch=(), mib=12):
    return pl.pallas_call(
        kernel,
        out_shape=tuple(jax.ShapeDtypeStruct(shape, dtype) for _, shape, dtype in outs),
        in_specs=[pl.BlockSpec(memory_space=SPACES[s]) for s in spaces],
        out_specs=tuple(pl.BlockSpec(memory_space=SPACES[s]) for s, _, _ in outs),
        scratch_shapes=[*scratch, *SEMS],
        compiler_params=pltpu.CompilerParams(
            collective_id=cid, has_side_effects=True, vmem_limit_bytes=mib << 20
        ),
        name=name,
    )(*args)


def top(ref):
    return ref.at[pl.ds(0, TOK // 2)]


def bottom(ref):
    return ref.at[pl.ds(TOK // 2, TOK // 2)]


class Gather:
    def __init__(self, links, a_ref, o_ref):
        self.links, self.o = links, o_ref
        own = o_ref.at[links.rank]
        self.kept = links.keep(a_ref, own)
        right, left = links.along_x(1), links.along_x(3)
        self.ahead = [links.push(top(a_ref), top(own), right)]
        self.back = [links.push(bottom(a_ref), bottom(own), left)]
        self.ahead.append(links.push(bottom(a_ref), bottom(own), right))
        self.back.append(links.push(top(a_ref), top(own), left))
        self.near = [links.push(a_ref, own, links.sibling)]

    def slot(self, k):
        return self.o.at[2 * lax.rem(self.links.x + 4 - k, 4) + self.links.c]

    def share(self, piece):
        self.near.append(self.links.push(piece, piece, self.links.sibling))

    def relay(self):
        links = self.links
        links.arrived(self.ahead[0])
        self.far = [links.push(top(self.slot(1)), top(self.slot(1)), links.along_x(1))]
        links.arrived(self.back[0])
        self.far.append(links.push(bottom(self.slot(3)), bottom(self.slot(3)), links.along_x(3)))
        self.share(top(self.slot(1)))
        self.share(bottom(self.slot(3)))

    def middle(self):
        links = self.links
        links.arrived(self.ahead[1])
        self.share(bottom(self.slot(1)))
        links.arrived(self.back[1])
        self.share(top(self.slot(3)))

    def last(self):
        links = self.links
        links.arrived(self.far[0])
        self.share(top(self.slot(2)))
        links.arrived(self.far[1])
        self.share(bottom(self.slot(2)))

    def complete(self):
        self.links.stored(self.kept)
        for copy in self.near:
            self.links.arrived(copy)


class Scatter:
    def __init__(self, links, p_ref, near, out, came):
        self.links, self.p, self.near, self.out, self.came = links, p_ref, near, out, came
        self.swaps = {}
        for k in (2, 1, 3, 0):
            to = lax.rem(links.x + k, 4)
            self.swaps[k] = links.push(p_ref.at[2 * to + 1 - links.c], near.at[k], links.sibling)

    def both(self, k):
        links = self.links
        links.arrived(self.swaps[k])
        to = lax.rem(links.x + k, 4)
        return self.p[2 * to + links.c].astype(F32) + self.near[k].astype(F32)

    def forward(self):
        links, out, came = self.links, self.out, self.came
        right, left = links.along_x(1), links.along_x(3)
        out[2] = self.both(2).astype(BF)
        ahead = links.push(top(out.at[2]), top(came.at[2]), right)
        back = links.push(bottom(out.at[2]), bottom(came.at[2]), left)
        half = TOK // 2
        one = self.both(1)
        out[1, half:] = one[half:].astype(BF)
        self.sends = [links.push(bottom(out.at[1]), bottom(came.at[1]), right)]
        three = self.both(3)
        out[3, :half] = three[:half].astype(BF)
        self.sends.append(links.push(top(out.at[3]), top(came.at[3]), left))
        links.arrived(ahead)
        out[1, :half] = (one[:half] + came[2, :half].astype(F32)).astype(BF)
        self.sends.append(links.push(top(out.at[1]), top(came.at[1]), right))
        links.arrived(back)
        out[3, half:] = (three[half:] + came[2, half:].astype(F32)).astype(BF)
        self.sends.append(links.push(bottom(out.at[3]), bottom(came.at[3]), left))

    def total(self):
        total = self.both(0)
        for copy in self.sends:
            self.links.arrived(copy)
        return total + self.came[1].astype(F32) + self.came[3].astype(F32)


SCATTER_ROOM = [pltpu.VMEM((4, TOK, D), BF)] * 3
PACKED = PART * HALF // 128
PIECES = (8, PACKED, 128)
GRADS_ROOM = [pltpu.VMEM((2, *PIECES), BF), pltpu.VMEM((16, PACKED, 128), BF)]


def pack(rows):
    tiles = [rows[:, 128 * t : 128 * (t + 1)] for t in range(4)]
    rest = jnp.concatenate([rows[17 * q : 17 * (q + 1), 512:] for q in range(4)], axis=1)
    return jnp.concatenate([*tiles, rest], axis=0)


def unpack(piece):
    tiles = [piece[PART * t : PART * (t + 1)] for t in range(4)]
    rest = [piece[4 * PART :, 32 * q : 32 * (q + 1)] for q in range(4)]
    return jnp.concatenate([*tiles, jnp.concatenate(rest, axis=0)], axis=1)


class GradScatter:
    def __init__(self, links, parts, came):
        self.links, self.parts, self.came = links, parts, came

    @staticmethod
    def between_cores(links, own, parts):
        kept = links.keep(own.at[links.c], parts.at[links.c])
        swap = links.push(own.at[1 - links.c], parts.at[links.c], links.sibling)
        return kept, swap

    def start(self):
        self.sends = [
            self.links.push(self.parts.at[zh, piece], self.came.at[n + 1], target)
            for n, (target, zh, piece) in enumerate(self.links.plane())
        ]

    def total(self):
        links = self.links
        total = self.parts[links.zh, 2 * links.y + links.zl].astype(F32)
        for n, send in enumerate(self.sends):
            links.arrived(send)
            total += self.came[n + 1].astype(F32)
        return total.astype(BF)


class Spread:
    def __init__(self, links, piece_ref, o_ref):
        self.links, self.o = links, o_ref
        slot = o_ref.at[2 * links.y + links.zl]
        self.other = links.push(piece_ref, slot, {"zl": 1 - links.zl})
        self.kept = links.keep(piece_ref, slot)
        self.copies = [links.push(piece_ref, slot, links.along_y(k)) for k in (2, 1, 3)]

    def turn(self):
        links = self.links
        links.arrived(self.other)
        slot = self.o.at[2 * links.y + 1 - links.zl]
        self.copies += [links.push(slot, slot, links.along_y(k)) for k in (2, 1, 3)]


def targets(links, *groups):
    found = []
    for group in groups:
        if group == "x":
            found += [links.along_x(k) for k in (1, 2, 3)]
        if group == "y":
            found += [links.along_y(k) for k in (1, 2, 3)]
        if group == "c":
            found.append(links.sibling)
        if group == "z":
            found.append(links.partner)
        if group == "line":
            found += [target for target, _ in links.line()]
        if group == "plane":
            found += [target for target, _, _ in links.plane()]
    return found


def normed(values, gain, shift):
    centre = jnp.mean(values, axis=1, keepdims=True)
    second_moment = jnp.mean(values * values, axis=1, keepdims=True)
    inverse = lax.rsqrt(second_moment - centre * centre + EPSILON)
    centred = (values - centre) * inverse
    return (centred * gain + shift).astype(BF), centred, inverse


def enter_kernel(a_ref, t_ref, wo_ref, w_ref, cols, wo4_ref, colso_ref, tailo_ref, i_ref, n_ref, cent_ref, inv_ref, t32_ref, pair, tpair, tok, ttok, tail, block, *sems):
    links = Links(*sems)
    x, y, zh, c = links.x, links.y, links.zh, links.c
    right, left = lax.rem(x + 1, 4), lax.rem(x + 3, 4)
    diagonal = [{"x": right, "zh": 1 - zh}, {"x": left, "zh": 1 - zh}]
    load = links.keep(w_ref.at[jnp.minimum(y, 2)], block)
    links.greet(targets(links, "x", "c", "z") + diagonal)
    other = links.push(a_ref.at[1 - zh], pair.at[zh], links.partner)
    mine = links.keep(a_ref.at[zh], pair.at[zh])
    t_other = links.push(t_ref.at[1 - zh], tpair.at[zh], links.partner)
    t_mine = links.keep(t_ref.at[zh], tpair.at[zh])
    swap = links.push(cols, colso_ref.at[c], links.sibling)
    own = links.keep(cols, colso_ref.at[c])
    for k in (2, 1, 3):
        links.push(wo_ref, wo4_ref.at[x], links.along_x(k))
    links.keep(wo_ref, wo4_ref.at[x])
    links.stored(load)
    tail[...] = block[88:]
    shifts = [
        pltpu.make_async_remote_copy(
            src_ref=tail,
            dst_ref=tailo_ref,
            send_sem=links.send.at[50 + i],
            recv_sem=links.recv.at[50],
            device_id=target,
            device_id_type=MESH,
        )
        for i, target in enumerate(({"x": right}, diagonal[0]))
    ]

    @pl.when(zh == 1)
    def _():
        for copy in shifts:
            copy.start()

    links.stored(mine)
    links.arrived(other)
    got = links.push(pair.at[1 - c], tok.at[c], links.sibling)
    kept = links.keep(pair.at[c], tok.at[c])
    links.stored(t_mine)
    links.arrived(t_other)
    t_got = links.push(tpair.at[1 - c], ttok.at[c], links.sibling)
    t_kept = links.keep(tpair.at[c], ttok.at[c])
    links.arrived(swap)
    links.stored(own)
    links.stored(kept)
    links.arrived(got)

    def whole(halves):
        return jnp.concatenate([halves[0].astype(F32), halves[1].astype(F32)], axis=0).T

    values = whole(tok)
    i_ref[...] = values
    gains = jnp.concatenate([colso_ref[0], colso_ref[1]], axis=1)
    n_ref[...], cent_ref[...], inv_ref[...] = normed(values, gains[1:2], gains[2:3])
    links.stored(t_kept)
    links.arrived(t_got)
    t32_ref[...] = whole(ttok).astype(BF)
    links.finish()
    shifts[0].wait_recv()

    @pl.when(zh == 1)
    def _():
        for copy in shifts:
            copy.wait_send()


def enter(block_in, out_grad, output_weight, w, columns):
    halves = pltpu.VMEM((2, HALF, TOK), BF)
    return call(
        enter_kernel,
        "enter",
        1,
        (block_in, out_grad, output_weight, w, columns),
        "hhhhv",
        [
            ("v", (4, 136, HALF), BF),
            ("v", (2, 8, HALF), F32),
            ("v", (48, HALF), BF),
            ("v", (TOK, D), F32),
            ("v", (TOK, D), BF),
            ("v", (TOK, D), F32),
            ("v", (TOK, 1), F32),
            ("v", (TOK, D), BF),
        ],
        [halves] * 4
        + [pltpu.VMEM((48, HALF), BF), pltpu.VMEM((136, HALF), BF)],
    )


def first_kernel(n_ref, w_ref, tail_ref, qv_in, cols_ref, o_ref, wq_ref, tails_ref, qvo_ref, b_ref, qv_ref, up_ref, ups, *sems):
    links = Links(*sems)
    x, y, zh, c = links.x, links.y, links.zh, links.c
    right, left = lax.rem(x + 1, 4), lax.rem(x + 3, 4)
    diagonal = [{"x": right, "zh": 1 - zh}, {"x": left, "zh": 1 - zh}]
    load = links.keep(qv_in, qv_ref)
    links.greet(targets(links, "x", "y", "c", "z") + diagonal)
    gather = Gather(links, n_ref, o_ref)
    links.stored(load)
    up_ref[...] = cols_ref[c, 6:7]
    w_other = links.push(w_ref, wq_ref.at[c, zh], links.partner)
    links.keep(w_ref, wq_ref.at[c, zh])
    links.push(w_ref, wq_ref.at[c, zh], links.sibling)
    links.push(qv_ref, qvo_ref.at[zh], links.partner)
    links.keep(qv_ref, qvo_ref.at[zh])
    up_other = links.push(up_ref, ups.at[zh], links.partner)
    up_mine = links.keep(up_ref, ups.at[zh])
    slot = tails_ref.at[c, y]
    links.keep(tail_ref, slot)
    links.push(tail_ref, slot, links.sibling)
    tails = [links.push(tail_ref, slot, links.along_y(k)) for k in (2, 1, 3)]
    shifts = [
        pltpu.make_async_remote_copy(
            src_ref=qv_ref,
            dst_ref=qvo_ref.at[2],
            send_sem=links.send.at[50 + i],
            recv_sem=links.recv.at[50],
            device_id=target,
            device_id_type=MESH,
        )
        for i, target in enumerate(({"x": right}, diagonal[0]))
    ]

    @pl.when(zh == 1)
    def _():
        for copy in shifts:
            copy.start()

    for k, copy in zip((2, 1, 3), tails):
        links.arrived(copy)
        slot = tails_ref.at[c, lax.rem(y + 4 - k, 4)]
        links.push(slot, slot, links.sibling)
    gather.relay()
    links.stored(up_mine)
    links.arrived(up_other)
    b_ref[...] = ups[c]
    gather.middle()
    links.arrived(w_other)
    slot = wq_ref.at[c, 1 - zh]
    links.push(slot, slot, links.sibling)
    gather.last()
    links.finish()
    shifts[0].wait_recv()

    @pl.when(zh == 1)
    def _():
        for copy in shifts:
            copy.wait_send()


def first(normed, w, tail, qv, up):
    return call(
        first_kernel,
        "first",
        2,
        (normed, w, tail, qv, up),
        "vhvhv",
        [
            ("v", (8, TOK, D), BF),
            ("v", (2, 2, 3, 136, HALF), BF),
            ("v", (2, 4, 48, HALF), BF),
            ("v", (3, 2, 136), F32),
            ("v", (1, HALF), F32),
        ],
        [pltpu.VMEM((2, 136), F32), pltpu.VMEM((1, HALF), F32), pltpu.VMEM((2, 1, HALF), F32)],
    )


class WeightBlock:
    def __init__(self, links, w_ref, pair, o_ref):
        self.links, self.pair, self.o = links, pair, o_ref
        self.other = links.push(w_ref.at[links.y], pair.at[links.zh, links.y], links.partner)
        self.kept = links.keep(w_ref, pair.at[links.zh])

    def turn(self):
        links = self.links
        links.arrived(self.other)
        slot = self.pair.at[1 - links.zh, links.y]
        self.round = [links.push(slot, slot, links.along_y(k)) for k in (2, 1, 3)]

    def between_cores(self):
        links = self.links
        links.stored(self.kept)
        for copy in self.round:
            links.arrived(copy)
        links.push(self.pair.at[1 - links.c], self.o.at[links.c], links.sibling)
        links.keep(self.pair.at[links.c], self.o.at[links.c])


QUARTERS = (4, 136, HALF)

BLOCK = 256


def dot(a, b, dims):
    return lax.dot_general(a, b, (dims, ((), ())), preferred_element_type=F32)


def attend_head(qkv_ref, h, m_ref, p_ref):
    keys = lax.broadcasted_iota(jnp.int32, (BLOCK, BLOCK), 0)
    queries = lax.broadcasted_iota(jnp.int32, (BLOCK, BLOCK), 1)
    head = pl.ds(h * HDIM, HDIM)
    for i in range(LEN // BLOCK):
        low, high = i * BLOCK, (i + 1) * BLOCK
        q = qkv_ref[0, head, low:high] * BF(HDIM**-0.5)
        parts = [dot(qkv_ref[1, head, low:high], q, ((0,), (0,)))]
        parts[0] = jnp.where(keys <= queries, parts[0], MASKED)
        if i:
            parts.insert(0, dot(qkv_ref[1, head, :low], q, ((0,), (0,))))
        highest = functools.reduce(jnp.maximum, [jnp.max(s, axis=0, keepdims=True) for s in parts])
        parts = [jnp.exp(s - highest) for s in parts]
        share = 1.0 / sum(jnp.sum(s, axis=0, keepdims=True) for s in parts)
        parts = [(s * share).astype(BF) for s in parts]
        p_ref[h, low:high, low:high] = parts[-1]
        mixed = dot(qkv_ref[2, head, low:high], parts[-1], ((1,), (0,)))
        if i:
            p_ref[h, :low, low:high] = parts[0]
            mixed += dot(qkv_ref[2, head, :low], parts[0], ((1,), (0,)))
        m_ref[head, low:high] = mixed.astype(BF)


def attend_kernel(t_ref, n_ref, wq_ref, tails_ref, qv_ref, up_ref, wo4_ref, qkv_ref, w_ref, m_ref, p_ref, f_ref, o_ref, upo_ref, woo_ref, room, pair, mid, *sems):
    links = Links(*sems)
    x, y, zh, c = links.x, links.y, links.zh, links.c
    links.greet(targets(links, "line", "y", "z"))
    wo_own = links.push(wo4_ref.at[y], mid, links.partner)
    gather = Gather(links, t_ref, o_ref)
    weight = WeightBlock(links, up_ref, pair, upo_ref)
    links.keep(wo4_ref, woo_ref.at[c, :, zh])
    links.push(wo4_ref, woo_ref.at[c, :, zh], links.sibling)
    n = n_ref[...].reshape(LEN, D)
    last = links.rank == 7
    start = pl.multiple_of(48 - 16 * x + 128 * c, 16)
    parts = [qv_ref[2][:, 88:], qv_ref[0], qv_ref[1], jnp.zeros((2, 64), F32)]
    bias = jnp.concatenate([jnp.concatenate(parts, axis=1), jnp.zeros((6, 384), F32)], axis=0)
    bias = pltpu.roll(bias, 384 - start, 1)[:, :256].T[:SLOT]
    real = jnp.logical_or(lax.broadcasted_iota(jnp.int32, (SLOT, 1), 0) < 128, last)
    bias = [jnp.where(real, bias[:, 0:1], 0.0), 0.0, jnp.where(real, bias[:, 1:2], 0.0)]
    for k in range(3):
        for h in range(2):
            columns = slice(h * HALF, (h + 1) * HALF)
            rows = [tails_ref[h, k], wq_ref[h, 0, k], wq_ref[h, 1, k], jnp.zeros((48, HALF), BF)]
            room[:, columns] = jnp.concatenate([r.astype(F32) for r in rows], axis=0)
        mine = room[pl.ds(start, SLOT)].astype(BF)
        low = slice(k * SLOT, k * SLOT + 128)
        high = slice(k * SLOT + 128, (k + 1) * SLOT)
        w_ref[low] = mine[:128]
        w_ref[high] = jnp.where(last, mine[128:], BF(0))
        rows = slice(k * SLOT, (k + 1) * SLOT)
        qkv_ref[k] = (dot(w_ref[rows], n, ((1,), (1,))) + bias[k]).astype(BF)
        if k == 0:
            links.arrived(wo_own)
            slot = woo_ref.at[c, y, 1 - zh]
            links.keep(mid, slot)
            round_y = [links.push(mid, slot, links.along_y(j)) for j in (2, 1, 3)]
            links.push(mid, slot, links.sibling)
        if k == 1:
            gather.relay()
    weight.turn()
    for h in range(SLOT // HDIM):
        attend_head(qkv_ref, h, m_ref, p_ref)
        if h == 1:
            gather.middle()
    own = links.rank
    columns = pl.ds(pl.multiple_of(own * TOK, TOK), TOK)
    links.keep(m_ref.at[:, columns], f_ref.at[own])
    for target, rank in links.line():
        columns = pl.ds(pl.multiple_of(rank * TOK, TOK), TOK)
        links.push(m_ref.at[:, columns], f_ref.at[own], target)
    for k, copy in zip((2, 1, 3), round_y):
        links.arrived(copy)
        slot = woo_ref.at[c, lax.rem(y + 4 - k, 4), 1 - zh]
        links.push(slot, slot, links.sibling)
    gather.last()
    weight.between_cores()
    links.finish()


def attend(tangent, rows, wq, tails, bias, up, wo4):
    return call(
        attend_kernel,
        "attend",
        3,
        (tangent, rows, wq, tails, bias, up, wo4),
        "vvvvvhv",
        [
            ("v", (3, SLOT, LEN), BF),
            ("v", (3 * SLOT, D), BF),
            ("v", (SLOT, LEN), BF),
            ("v", (SLOT // HDIM, LEN, LEN), BF),
            ("v", (8, SLOT, TOK), BF),
            ("v", (8, TOK, D), BF),
            ("v", (2, *QUARTERS), BF),
            ("v", (2, 4, 2, 136, HALF), BF),
        ],
        [pltpu.VMEM((368, D), F32), pltpu.VMEM((2, *QUARTERS), BF), pltpu.VMEM((136, HALF), BF)],
        20,
    )


def second_kernel(f_ref, wo_ref, i_ref, cols_ref, down_ref, o_ref, downo_ref, r_ref, cent_ref, inv_ref, m_ref, n, pair, *sems):
    links = Links(*sems)
    links.greet(targets(links, "x", "y", "c", "z"))
    weight = WeightBlock(links, down_ref, pair, downo_ref)
    for rank in range(7):
        m_ref[128 * rank : 128 * (rank + 1)] = f_ref[rank, :128]
    m_ref[896:] = f_ref[7]
    columns = jnp.concatenate([cols_ref[0], cols_ref[1]], axis=1)
    attended = [dot(m_ref[...], wo_ref[h], ((0,), (0,))) for h in range(2)]
    residual = i_ref[...] + (jnp.concatenate(attended, axis=1) + columns[0:1])
    r_ref[...] = residual + columns[5:6]
    n[...], cent_ref[...], inv_ref[...] = normed(residual, columns[3:4], columns[4:5])
    gather = Gather(links, n, o_ref)
    weight.turn()
    gather.relay()
    gather.middle()
    weight.between_cores()
    gather.last()
    links.finish()


def second(found, wo, inputs, columns, down):
    return call(
        second_kernel,
        "second",
        4,
        (found, wo, inputs, columns, down),
        "vvvvh",
        [
            ("v", (8, TOK, D), BF),
            ("v", (2, *QUARTERS), BF),
            ("v", (TOK, D), F32),
            ("v", (TOK, D), F32),
            ("v", (TOK, 1), F32),
        ],
        [pltpu.VMEM((D, TOK), BF), pltpu.VMEM((TOK, D), BF), pltpu.VMEM((2, *QUARTERS), BF)],
    )


STEP = 512


def hidden_kernel(n_ref, t_ref, up_ref, down_ref, b_ref, low_ref, dn_ref, gup_ref, gdown_ref, gb_ref, up, down, up_sum, down_sum):
    step = pl.program_id(0)

    @pl.when(step == 0)
    def _():
        for h in range(2):
            up[:, h * HALF : (h + 1) * HALF] = up_ref[h]
            down[:, h * HALF : (h + 1) * HALF] = down_ref[h]
        up_sum[...] = jnp.zeros_like(up_sum)
        down_sum[...] = jnp.zeros_like(down_sum)
        gb_ref[...] = jnp.zeros_like(gb_ref)

    n = n_ref[...].reshape(STEP, D)
    t = t_ref[...].reshape(STEP, D)
    pre = dot(n, up[...], ((1,), (1,))) + b_ref[...]
    cumulative = 0.5 * (1.0 + lax.erf(pre * 0.7071067811865476))
    density = jnp.exp(-0.5 * pre * pre) * 0.3989422804014327
    active = (pre * cumulative).astype(BF)
    slope = cumulative + pre * density
    low_ref[...] = dot(active, down[...], ((1,), (0,))).astype(BF).reshape(low_ref.shape)
    d_pre = (dot(t, down[...], ((1,), (1,))) * slope).astype(BF)
    dn_ref[...] = dot(d_pre, up[...], ((1,), (0,))).astype(BF).reshape(dn_ref.shape)
    down_sum[...] += dot(active, t, ((0,), (0,)))
    up_sum[...] += dot(d_pre, n, ((0,), (0,)))
    gb_ref[...] += jnp.sum(d_pre.astype(F32), axis=0, keepdims=True)

    @pl.when(step == pl.num_programs(0) - 1)
    def _():
        for h in range(2):
            for out, total in ((gup_ref, up_sum), (gdown_ref, down_sum)):
                for j in range(8):
                    out[h, j] = pack(total[j * PART : (j + 1) * PART, h * HALF : (h + 1) * HALF]).astype(BF)


def hidden_part(second_rows, tangent_rows, up, down, bias):
    rows = pl.BlockSpec((STEP // TOK, TOK, D), lambda i: (i, 0, 0))
    weight = pl.BlockSpec((2, HALF, HALF), lambda i: (0, 0, 0))
    grad = pl.BlockSpec((2, *PIECES), lambda i: (0, 0, 0, 0))
    one = pl.BlockSpec((1, HALF), lambda i: (0, 0))
    return pl.pallas_call(
        hidden_kernel,
        grid=(LEN // STEP,),
        in_specs=[rows, rows, weight, weight, one],
        out_specs=(rows, rows, grad, grad, one),
        out_shape=(
            jax.ShapeDtypeStruct((8, TOK, D), BF),
            jax.ShapeDtypeStruct((8, TOK, D), BF),
            jax.ShapeDtypeStruct((2, *PIECES), BF),
            jax.ShapeDtypeStruct((2, *PIECES), BF),
            jax.ShapeDtypeStruct((1, HALF), F32),
        ),
        scratch_shapes=[pltpu.VMEM((HALF, D), BF)] * 2 + [pltpu.VMEM((HALF, D), F32)] * 2,
        compiler_params=pltpu.CompilerParams(vmem_limit_bytes=32 << 20),
        name="hidden_part",
    )(second_rows, tangent_rows, up, down, bias)


def norm_back(upstream, centred, inverse, gain):
    scaled = upstream * gain
    result = inverse * (
        scaled
        - jnp.mean(scaled, axis=1, keepdims=True)
        - centred * jnp.mean(scaled * centred, axis=1, keepdims=True)
    )
    return result, jnp.sum(upstream * centred, axis=0, keepdims=True), jnp.sum(upstream, axis=0, keepdims=True)


def third_kernel(p_ref, g_ref, t_ref, cent_ref, inv_ref, cols_ref, wo_ref, d_ref, a_ref, dm_ref, v_ref, piece_ref, near, out, came, parts, found, *sems):
    links = Links(*sems)
    links.greet(targets(links, "x", "c", "plane"))
    grads = GradScatter(links, parts, found)
    kept, swap = grads.between_cores(links, g_ref, parts)
    scatter = Scatter(links, p_ref, near, out, came)
    links.stored(kept)
    links.arrived(swap)
    grads.start()
    scatter.forward()
    gains = jnp.concatenate([cols_ref[0], cols_ref[1]], axis=1)
    part, gain, shift = norm_back(scatter.total(), cent_ref[...], inv_ref[...], gains[3:4])
    tangent = t_ref[...].astype(F32)
    d_residual = tangent + part
    d_ref[...] = d_residual
    rounded = d_residual.astype(BF)
    a_ref[...] = rounded
    d_mixed = [dot(wo_ref[h], rounded[:, h * HALF : (h + 1) * HALF], ((1,), (1,))) for h in range(2)]
    dm_ref[...] = (d_mixed[0] + d_mixed[1]).astype(BF)
    v_ref[0] = jnp.sum(d_residual.astype(BF).astype(F32), axis=0, keepdims=True)
    v_ref[1] = gain
    v_ref[2] = shift
    v_ref[3] = jnp.sum(tangent, axis=0, keepdims=True)
    piece_ref[...] = grads.total()
    links.finish()


def third(d_normed, grad, tangent, centred, inverse, gain, wo):
    return call(
        third_kernel,
        "third",
        5,
        (d_normed, grad, tangent, centred, inverse, gain, wo),
        "vvvvvvv",
        [
            ("v", (TOK, D), F32),
            ("v", (TOK, D), BF),
            ("v", (D, TOK), BF),
            ("v", (4, 1, D), F32),
            ("v", (PACKED, 128), BF),
        ],
        SCATTER_ROOM + GRADS_ROOM,
        16,
    )


def attend_back_head(qkv_ref, h, u_ref, p_ref, d_ref, dk_sum, dv_sum):
    head = pl.ds(h * HDIM, HDIM)
    for i in range(LEN // BLOCK):
        low, high = i * BLOCK, (i + 1) * BLOCK
        q = qkv_ref[0, head, low:high] * BF(HDIM**-0.5)
        u = u_ref[head, low:high]
        p = p_ref[h, :high, low:high]
        wide = p.astype(F32)
        dp = dot(qkv_ref[2, head, :high], u, ((0,), (0,)))
        centre = jnp.sum(wide * dp, axis=0, keepdims=True)
        ds = (wide * (dp - centre)).astype(BF)
        d_ref[head, low:high] = (dot(qkv_ref[1, head, :high], ds, ((1,), (0,))) * HDIM**-0.5).astype(BF)
        dk = dot(q, ds, ((1,), (1,)))
        dv = dot(u, p, ((1,), (1,)))
        if i:
            dk_sum[:, :low] += dk[:, :low]
            dv_sum[:, :low] += dv[:, :low]
        dk_sum[:, low:high] = dk[:, low:]
        dv_sum[:, low:high] = dv[:, low:]
    d_ref[pl.ds(SLOT + h * HDIM, HDIM)] = dk_sum[...].astype(BF)
    d_ref[pl.ds(2 * SLOT + h * HDIM, HDIM)] = dv_sum[...].astype(BF)


def back_kernel(m_ref, a_ref, qkv_ref, p_ref, g_ref, mixed_ref, n_ref, w_ref, piece_ref, dn_ref, chip_ref, tail_ref, vb_ref, u, d, dk_sum, dv_sum, o, own_grads, parts, found, *sems):
    links = Links(*sems)
    c = links.c
    links.greet(targets(links, "line", "plane"))
    own = links.rank
    columns = pl.ds(pl.multiple_of(own * TOK, TOK), TOK)

    def rows(rank):
        return pl.ds(pl.multiple_of(rank * 2 * HDIM, 2 * HDIM), SLOT)

    mine = links.keep(m_ref.at[rows(own)], u.at[:, columns])
    others = [links.push(m_ref.at[rows(rank)], u.at[:, columns], target) for target, rank in links.line()]
    gather = Gather(links, a_ref, o)
    grads = GradScatter(links, parts, found)
    kept, swap = grads.between_cores(links, g_ref, parts)
    links.stored(kept)
    links.arrived(swap)
    grads.start()
    links.stored(mine)
    for copy in others:
        links.arrived(copy)
    n = n_ref[...].reshape(LEN, D)

    def weight_grad(left, right, k, rows):
        grad = dot(left, right, ((1,), (0,)))
        for h in range(2):
            own_grads[h, k, rows] = grad[:, h * HALF : (h + 1) * HALF].astype(BF)

    def between_cores(which):
        kept = links.keep(own_grads.at[(c, *which)], chip_ref.at[(c, *which)])
        return kept, links.push(own_grads.at[(1 - c, *which)], chip_ref.at[(c, *which)], links.sibling)

    def done(copies):
        links.stored(copies[0])
        links.arrived(copies[1])

    attend_back_head(qkv_ref, 0, u, p_ref, d, dk_sum, dv_sum)
    gather.relay()
    for k in range(3):
        weight_grad(d[k * SLOT : k * SLOT + HDIM], n, k, slice(0, HDIM))
    first_rows = between_cores((pl.ds(0, 3), pl.ds(0, HDIM)))
    attend_back_head(qkv_ref, 1, u, p_ref, d, dk_sum, dv_sum)
    done(first_rows)
    links.push(chip_ref.at[0, pl.ds(0, 3), pl.ds(0, HDIM)], tail_ref.at[pl.ds(0, 3)], links.along_x(3))
    gather.middle()
    attend_back_head(qkv_ref, 2, u, p_ref, d, dk_sum, dv_sum)
    gather.last()
    for k in range(3):
        weight_grad(d[k * SLOT + HDIM : (k + 1) * SLOT], n, k, slice(HDIM, SLOT))
    between_cores((pl.ds(0, 3), pl.ds(HDIM, SLOT - HDIM)))
    gather.complete()
    weight_grad(mixed_ref[...], o[...].reshape(LEN, D), 3, slice(0, SLOT))
    out_rows = between_cores((3,))
    for i in range(LEN // BLOCK):
        block = dot(d[:, i * BLOCK : (i + 1) * BLOCK], w_ref[...], ((0,), (0,))).astype(BF)
        dn_ref[2 * i : 2 * i + 2] = block.reshape(2, TOK, D)
        if i == 0:
            done(out_rows)
            links.push(chip_ref.at[0, 3, pl.ds(0, HDIM)], tail_ref.at[3], links.along_x(3))
    ones = jnp.ones((8, LEN), BF)
    vb_ref[...] = jnp.zeros_like(vb_ref)
    real = jnp.logical_or(lax.broadcasted_iota(jnp.int32, (1, SLOT), 1) < 128, own == 7)
    for i, k in enumerate((0, 2)):
        total = dot(ones, d[k * SLOT : (k + 1) * SLOT], ((1,), (1,)))[0:1]
        vb_ref[i, :, pl.ds(pl.multiple_of(own * 128, 128), SLOT)] = jnp.where(real, total, 0.0)
    piece_ref[...] = grads.total()
    links.finish()


def back(d_mixed, d_attended, qkv, probs, grad, mixed, rows, weight):
    return call(
        back_kernel,
        "back",
        6,
        (d_mixed, d_attended, qkv, probs, grad, mixed, rows, weight),
        "vvvvvvvv",
        [
            ("v", (PACKED, 128), BF),
            ("v", (8, TOK, D), BF),
            ("v", (2, 4, SLOT, HALF), BF),
            ("v", (4, HDIM, HALF), BF),
            ("v", (2, 1, D), F32),
        ],
        [pltpu.VMEM((SLOT, LEN), BF), pltpu.VMEM((3 * SLOT, LEN), BF)]
        + [pltpu.VMEM((HDIM, LEN), F32)] * 2
        + [pltpu.VMEM((8, TOK, D), BF), pltpu.VMEM((2, 4, SLOT, HALF), BF)]
        + GRADS_ROOM,
        24,
    )


def fourth_kernel(p_ref, chip, tail, r_ref, cent_ref, inv_ref, cols_ref, down_ref, i_ref, v_ref, piece_ref, gdown_ref, near, out, came, whole, exact, parts, found, *sems):
    links = Links(*sems)
    x = links.x
    links.greet(targets(links, "x", "c", "plane"))
    scatter = Scatter(links, p_ref, near, out, came)
    spread = Spread(links, down_ref, gdown_ref)
    whole[:, pl.ds(0, 128)] = chip[0, :, pl.ds(0, 128)]
    whole[:, pl.ds(128, 128)] = chip[1, :, pl.ds(0, 128)]
    whole[:, pl.ds(256, 64)] = jnp.where(x == 3, chip[1, :, pl.ds(128, 64)], tail[...])
    links.stored(links.keep(whole.at[:, pl.ds(pl.multiple_of(16 * x, 16), 272)], exact))
    for k in range(4):
        rows = exact[k].astype(F32)
        for j in range(4):
            parts[j // 2, 2 * k + j % 2] = pack(rows[j * PART : (j + 1) * PART]).astype(BF)
    grads = GradScatter(links, parts, found)
    grads.start()
    scatter.forward()
    spread.turn()
    gains = jnp.concatenate([cols_ref[0], cols_ref[1]], axis=1)
    part, gain, shift = norm_back(scatter.total(), cent_ref[...], inv_ref[...], gains[1:2])
    result = (r_ref[...] + part).T.astype(BF)
    i_ref[0] = result[:HALF]
    i_ref[1] = result[HALF:]
    v_ref[0] = gain
    v_ref[1] = shift
    piece_ref[...] = grads.total()
    links.finish()


def fourth(d_normed, chip, tail, residual, centred, inverse, columns, down_piece):
    return call(
        fourth_kernel,
        "fourth",
        7,
        (d_normed, chip, tail, residual, centred, inverse, columns, down_piece),
        "vvvvvvvv",
        [
            ("v", (2, HALF, TOK), BF),
            ("v", (2, 1, D), F32),
            ("v", (PACKED, 128), BF),
            ("v", PIECES, BF),
        ],
        SCATTER_ROOM + [pltpu.VMEM((4, 320, HALF), BF), pltpu.VMEM((4, 272, HALF), BF)] + GRADS_ROOM,
        16,
    )


WIDE = 1792


def leave_kernel(p_ref, r_ref, i_ref, g_ref, v2_ref, v1_ref, vb_ref, b_ref, gup_ref, oo_ref, io_ref, found, vo_ref, found_up, near, out, came, halves_o, pair_o, pair_i, v_all, v_line, v_own, v_plane, v_sum, *sems):
    links = Links(*sems)
    y, zh, zl, c = links.y, links.zh, links.zl, links.c
    links.greet(targets(links, "line", "plane"))
    scatter = Scatter(links, p_ref, near, out, came)
    v_all[0] = v2_ref[0]
    v_all[1:3] = v1_ref[...]
    v_all[3:6] = v2_ref[1:4]
    v_all[6:8] = vb_ref[...]
    line = [links.push(v_all.at[rank], v_line.at[n], target) for n, (target, rank) in enumerate(links.line())]

    def between_cores(src, pair):
        return links.keep(src.at[c], pair.at[c]), links.push(src.at[1 - c], pair.at[c], links.sibling)

    def to_partner(pair, dst, copies):
        links.stored(copies[0])
        links.arrived(copies[1])
        links.push(pair.at[1 - zh], dst.at[zh], links.partner)
        links.keep(pair.at[zh], dst.at[zh])

    spreads = [Spread(links, gup_ref, found_up), Spread(links, g_ref, found)]
    copies = between_cores(i_ref, pair_i)
    scatter.forward()
    to_partner(pair_i, io_ref, copies)
    for spread in spreads:
        spread.turn()
    total = v_all[links.rank]
    for n, copy in enumerate(line):
        links.arrived(copy)
        total += v_line[n]
    v_own[...] = jnp.zeros_like(v_own)
    v_own[:, :D] = total
    v_own[:, 1152 : 1152 + HALF] = b_ref[...]
    place = (2 * zh + zl) * 4 + y
    kept = links.keep(v_own, v_plane.at[place])
    plane = [links.push(v_own, v_plane.at[place], target) for target, _, _ in links.plane()]
    links.stored(kept)
    for copy in plane:
        links.arrived(copy)
    total = v_plane[0]
    for n in range(1, 16):
        total += v_plane[n]
    v_sum[...] = total
    links.keep(v_sum, vo_ref.at[links.rank])
    for target, _ in links.line():
        links.push(v_sum, vo_ref.at[links.rank], target)
    result = (scatter.total() + r_ref[...]).T.astype(BF)
    halves_o[0] = result[:HALF]
    halves_o[1] = result[HALF:]
    to_partner(pair_o, oo_ref, between_cores(halves_o, pair_o))
    links.finish()


def leave(lowered, residual, in_grad, piece, *vectors, up_piece):
    pair = pltpu.VMEM((2, HALF, TOK), BF)
    return call(
        leave_kernel,
        "leave",
        8,
        (lowered, residual, in_grad, piece, *vectors, up_piece),
        "vvvvvvvvv",
        [
            ("v", (2, HALF, TOK), BF),
            ("v", (2, HALF, TOK), BF),
            ("v", PIECES, BF),
            ("v", (8, 1, WIDE), F32),
            ("v", PIECES, BF),
        ],
        SCATTER_ROOM
        + [pair, pair, pair]
        + [pltpu.VMEM((8, 1, D), F32), pltpu.VMEM((7, 1, D), F32), pltpu.VMEM((1, WIDE), F32)]
        + [pltpu.VMEM((16, 1, WIDE), F32), pltpu.VMEM((1, WIDE), F32)],
        16,
    )


def finish_kernel(o_ref, i_ref, g_ref, up_ref, down_ref, block_ref, in_ref, qkv_ref, out_ref, fup_ref, fdown_ref):
    block_ref[...] = o_ref[...]
    in_ref[...] = i_ref[...].astype(F32)
    for j in range(8):
        rows = slice(PART * (j % 2), PART * (j % 2 + 1))
        piece = unpack(g_ref[j].astype(F32))
        if j < 6:
            qkv_ref[j // 2, rows] = piece
        else:
            out_ref[rows] = piece
        rows = slice(PART * j, PART * (j + 1))
        fup_ref[rows] = unpack(up_ref[j].astype(F32))
        fdown_ref[rows] = unpack(down_ref[j].astype(F32))


def finish(block_out, in_grad, grads, up_grad, down_grad):
    whole = pl.BlockSpec(memory_space=pltpu.VMEM)
    return pl.pallas_call(
        finish_kernel,
        out_shape=(
            jax.ShapeDtypeStruct((2, HALF, TOK), BF),
            jax.ShapeDtypeStruct((2, HALF, TOK), F32),
            jax.ShapeDtypeStruct((3, 136, HALF), F32),
            jax.ShapeDtypeStruct((136, HALF), F32),
            jax.ShapeDtypeStruct((HALF, HALF), F32),
            jax.ShapeDtypeStruct((HALF, HALF), F32),
        ),
        in_specs=[whole] * 5,
        out_specs=(whole,) * 6,
        compiler_params=pltpu.CompilerParams(vmem_limit_bytes=16 << 20),
        name="finish",
    )(block_out, in_grad, grads, up_grad, down_grad)


def per_device(
    block_in,
    query_key_value_weight,
    bias_qv,
    output_weight,
    bias_out,
    gain_one,
    shift_one,
    gain_two,
    shift_two,
    up_weight,
    bias_up,
    down_weight,
    bias_down,
    out_grad,
):
    x, zh, c = (lax.axis_index(a) for a in ("x", "zh", "c"))

    place = lax.broadcasted_iota(jnp.int32, (8, HALF), 0)
    columns = jnp.zeros((8, HALF), F32)
    for i, vector in enumerate((bias_out, gain_one, shift_one, gain_two, shift_two, bias_down, bias_up)):
        columns = jnp.where(place == i, vector[None], columns)
    wo4, columns, tail, inputs, normed_one, centred_one, inverse_one, tangent = enter(
        jnp.transpose(block_in, (0, 2, 1)),
        jnp.transpose(out_grad, (0, 2, 1)),
        output_weight,
        query_key_value_weight,
        columns,
    )
    first_rows, wq, tails, qv, bias_up = first(normed_one, query_key_value_weight, tail, bias_qv, columns)

    qkv, weight_qkv, mixed, probs, found, tangent_rows, up, wo = attend(
        tangent, first_rows, wq, tails, qv, up_weight.reshape(QUARTERS), wo4
    )
    wo = wo.reshape(2, D, HALF)

    second_rows, down, residual, centred_two, inverse_two = second(
        found, wo, inputs, columns, down_weight.reshape(QUARTERS)
    )
    lowered, d_normed_two, up_grad, down_grad, grad_bias_up = hidden_part(
        second_rows,
        tangent_rows,
        up.reshape(2, HALF, HALF),
        down.reshape(2, HALF, HALF),
        bias_up,
    )
    d_residual, d_attended, d_mixed, sums_two, down_piece = third(
        d_normed_two, down_grad, tangent, centred_two, inverse_two, columns, wo
    )

    up_piece, d_normed_one, chip, tail, bias_sums = back(
        d_mixed, d_attended, qkv, probs, up_grad, mixed, first_rows, weight_qkv
    )
    in_grad, sums_one, piece, down_grad = fourth(
        d_normed_one, chip, tail, d_residual, centred_one, inverse_one, columns, down_piece
    )

    block_out, in_grad, grads, vectors, up_grad = leave(
        lowered, residual, in_grad, piece, sums_two, sums_one, bias_sums, grad_bias_up, up_piece=up_piece
    )
    block_out, in_grad, grad_qkv, grad_out, up_grad, down_grad = finish(block_out, in_grad, grads, up_grad, down_grad)
    row = 2 * x + zh
    vectors = vectors[:, 0]
    grad_bias_up = lax.dynamic_index_in_dim(vectors, row, 0, keepdims=False)[1152 : 1152 + HALF]
    six = lax.dynamic_slice_in_dim(vectors[:6], HALF * c, HALF, 1)
    grad_bias_out, grad_gain_one, grad_shift_one, grad_gain_two, grad_shift_two, grad_bias_down = six
    grad_bias_qv = lax.dynamic_slice_in_dim(vectors[6:], 136 * row, 136, 1)

    return (
        jnp.transpose(block_out, (0, 2, 1)),
        jnp.transpose(in_grad, (0, 2, 1)),
        grad_qkv,
        grad_bias_qv,
        grad_out,
        grad_bias_out,
        grad_gain_one,
        grad_shift_one,
        grad_gain_two,
        grad_shift_two,
        up_grad,
        grad_bias_up,
        down_grad,
        grad_bias_down,
    )


def solution(mesh):
    finer = Mesh(mesh.devices.reshape(2, 4, 4, 2, 2), ALL)
    return jax.shard_map(
        per_device,
        mesh=finer,
        in_specs=(
            P(DP, ROW, "c"),
            P(None, ROW, "c"),
            P(None, ROW),
            P(ROW, "c"),
            P("c"),
            P("c"),
            P("c"),
            P("c"),
            P("c"),
            P(ROW, "c"),
            P(ROW),
            P(ROW, "c"),
            P("c"),
            P(DP, ROW, "c"),
        ),
        out_specs=(
            P(DP, ROW, "c"),
            P(DP, ROW, "c"),
            P(None, ROW, "c"),
            P(None, ROW),
            P(ROW, "c"),
            P("c"),
            P("c"),
            P("c"),
            P("c"),
            P("c"),
            P(ROW, "c"),
            P(ROW),
            P(ROW, "c"),
            P("c"),
        ),
        check_vma=False,
    )
```
